32 devices in a mesh: parts: 2 (over x), row: 2 (over core), col: 8 (over z, y).
Axes of the slice: x: 2, y: 2, z: 4, core: 2. Of those that a mesh axis runs over, the one named last changes fastest.
Arguments:
- pair_state: bfloat16 [224, 112, 128], P(('parts', 'row'), 'col'), parts along dimension 0, may hold values from -6 to 6
- valid_length: int32 [2], P('parts'), parts along dimension 0, may hold values from 56 to 112
- input_gain: float32 [128], replicated, may hold values from 0.1 to 1.9
- left_gate: bfloat16 [128, 128], replicated, may hold values from -0.5 to 0.5
- left_value: bfloat16 [128, 128], replicated, may hold values from -0.5 to 0.5
- right_gate: bfloat16 [128, 128], replicated, may hold values from -0.5 to 0.5
- right_value: bfloat16 [128, 128], replicated, may hold values from -0.5 to 0.5
- out_gate: bfloat16 [128, 128], replicated, may hold values from -0.5 to 0.5
- output_gain: float32 [128], replicated, may hold values from 0.1 to 1.9
- out_weight: bfloat16 [128, 128], replicated, may hold values from -0.5 to 0.5
Outputs:
- update: bfloat16 [224, 112, 128], P(('parts', 'row'), 'col'), parts along dimension 0
The draws below stay inside these ranges and needn't reach their ends.
There are 2 independent parts, one for each index of `parts`. The reference program is written for one: setup_inputs(seed, part) draws one part's arguments, and reference() takes and returns one part's arrays. A program takes and returns all parts, laid end to end along the dimension named above; an argument that names none is the same for every part. Nothing has to cross between parts.
All inputs are finite; a program needn't handle non-finite values.
Results may differ from the reference program's by a relative error of at most 0.014.
Values may be sent and summed in bfloat16 or wider, within the bound.
No kernel may reach another device: no remote copies, remote signals or barrier semaphores. Data moves between devices by JAX's collectives and lax.ppermute only.
A program may use at most 128 MiB of HBM per device.

```python
import jax
import jax.numpy as jnp
from jax import lax

C = 128
CH = 128
J_DEV = 14
N = 112
N_COL = 8


def level_of(own_key, extent, shards, low, high):
    def one(axis_at, parts):
        draws = jax.random.uniform(jax.random.fold_in(jax.random.fold_in(own_key, 6), axis_at), (parts,), jnp.float32, low / len(shards), high / len(shards))
        return jnp.repeat(jnp.exp(draws), extent[axis_at] // parts).reshape((-1,) + (1,) * (len(extent) - axis_at - 1))

    factor_of = one(*shards[0])
    for cut in shards[1:]:
        factor_of = factor_of * one(*cut)
    return factor_of


def centred(rng, shape, width, limit, shards=(), kind=jnp.bfloat16):
    array = width * jax.random.normal(rng, shape, jnp.float32)
    if shards:
        array = array * level_of(rng, shape, shards, -0.22, 0.18)
    return jnp.clip(array, -limit, limit).astype(kind)


def setup_inputs(seed: int = 0, part: int = 0) -> dict:
    seeds = jax.random.split(jax.random.key(seed), 11)
    own_keys = jax.random.split(jax.random.fold_in(seeds[10], part), 11)
    return {
        "pair_state": centred(own_keys[0], (N, N, C), 1.0, 6.0, ((0, 2), (1, 8))),
        "valid_length": jax.random.randint(own_keys[1], (1,), N // 2, N + 1).astype(jnp.int32),
        "input_gain": jnp.clip(1.0 + 0.18 * jax.random.normal(seeds[2], (C,), jnp.float32), 0.1, 1.9),
        "left_gate": centred(seeds[3], (C, CH), C ** -0.5, 0.5),
        "left_value": centred(seeds[4], (C, CH), C ** -0.5, 0.5),
        "right_gate": centred(seeds[5], (C, CH), C ** -0.5, 0.5),
        "right_value": centred(seeds[6], (C, CH), C ** -0.5, 0.5),
        "out_gate": centred(seeds[7], (C, C), C ** -0.5, 0.5),
        "output_gain": jnp.clip(1.0 + 0.18 * jax.random.normal(seeds[8], (CH,), jnp.float32), 0.1, 1.9),
        "out_weight": centred(seeds[9], (CH, C), CH ** -0.5, 0.5),
    }


def norm_last(values, gain):
    average = lax.optimization_barrier(jnp.mean(values, -1, keepdims=True))
    centered = values - average
    variance = lax.optimization_barrier(jnp.mean(centered * centered, -1, keepdims=True))
    return centered * lax.rsqrt(variance + 1e-05) * gain

def reference(pair_state, valid_length, input_gain, left_gate, left_value, right_gate, right_value, out_gate, output_gain, out_weight):
    flat = pair_state.astype(jnp.float32).reshape(N * N, C)
    normed = norm_last(flat, input_gain).astype(jnp.bfloat16)
    position = jnp.arange(N, dtype=jnp.int32)
    valid = (position < valid_length[0]).astype(jnp.float32)
    pair_mask = (valid[:, None] * valid[None, :]).reshape(N * N, 1)

    def project(weight):
        return jnp.dot(normed, weight, preferred_element_type=jnp.float32)
    left = (jax.nn.sigmoid(project(left_gate)) * project(left_value) * pair_mask).astype(jnp.bfloat16)
    right = (jax.nn.sigmoid(project(right_gate)) * project(right_value) * pair_mask).astype(jnp.bfloat16)
    gating = jax.nn.sigmoid(project(out_gate))
    left_full = left.reshape(N, N, CH)
    right_full = right.reshape(N, N, CH)

    def add_block(total, block):
        start = (block * J_DEV).astype(jnp.int32)
        left_part = lax.dynamic_slice_in_dim(left_full, start, J_DEV, 1).astype(jnp.float32)
        right_part = lax.dynamic_slice_in_dim(right_full, start, J_DEV, 1).astype(jnp.float32)
        term = jnp.einsum('ikc,jkc->ijc', left_part, right_part, precision=lax.Precision.HIGHEST)
        return (total + term.astype(jnp.bfloat16).astype(jnp.float32), None)
    combined, _ = lax.scan(add_block, jnp.zeros((N, N, CH), jnp.float32), jnp.arange(N_COL, dtype=jnp.int32))
    settled = norm_last(combined.reshape(N * N, CH), output_gain).astype(jnp.bfloat16)
    update = gating * jnp.dot(settled, out_weight, preferred_element_type=jnp.float32)
    return update.astype(jnp.bfloat16).reshape(N, N, C)
```

```python
import functools

import jax
import jax.numpy as jnp
from jax import lax
from jax.experimental import pallas as pl
from jax.experimental.pallas import tpu as pltpu
from jax.sharding import PartitionSpec as P

F32 = jnp.float32
BF16 = jnp.bfloat16
LANES = 128
SUBLANES = 16
EPS = 1e-05


def round_up(value, multiple):
    return -(-value // multiple) * multiple


class Sizes:
    def __init__(self, mesh, height, width, channels, hidden):
        self.rows = mesh.shape["row"]
        self.cols = mesh.shape["col"]
        self.peers = self.rows * self.cols
        self.height, self.width = height, width
        self.channels, self.hidden = channels, hidden
        self.each = hidden // self.peers
        fits = self.rows * height <= LANES
        self.pack = self.rows if fits and width % self.rows == 0 and self.each % self.rows == 0 else 1
        self.steps = width // self.pack
        self.groups = self.each // self.pack
        self.lanes = round_up(self.pack * height, LANES)
        self.slots = round_up(width, SUBLANES)
        self.direct = self.each % 8 == 0 and self.lanes == LANES


def normalise(values):
    average = jnp.mean(values, -1, keepdims=True)
    centered = values - average
    variance = jnp.mean(centered * centered, -1, keepdims=True)
    return centered * lax.rsqrt(variance + EPS)


def sigmoid(values):
    return 0.5 * jnp.tanh(0.5 * values) + 0.5


def swap_blocks(first, second, height):
    lanes = first.shape[-1]
    low = lax.broadcasted_iota(jnp.int32, first.shape, 1) < height
    return (
        jnp.where(low, first, pltpu.roll(second, height, 1)),
        jnp.where(low, pltpu.roll(first, lanes - height, 1), second),
    )


def produce(s, pair, length, gain, left_gate, left_value, right_gate, right_value, message):
    first = lax.axis_index("row") * s.height
    second = lax.axis_index("col") * s.width
    limit = length[0]
    weights = jnp.concatenate(
        [w[...].T for w in (left_gate, left_value, right_gate, right_value)], 0
    )
    scale = gain[...]
    lane = lax.broadcasted_iota(jnp.int32, (1, s.lanes), 1)
    block = lane // s.height
    token = first + lane - block * s.height
    for step in range(s.steps):
        normed = [
            normalise(pair[at * s.steps + step].astype(F32)) * scale for at in range(s.pack)
        ]
        if s.lanes > s.pack * s.height:
            normed.append(jnp.zeros((s.lanes - s.pack * s.height, s.channels), F32))
        normed = jnp.concatenate(normed, 0).astype(BF16)
        out = lax.dot_general(weights, normed, (((1,), (1,)), ((), ())), preferred_element_type=F32)
        inner = second + block * s.steps + step
        mask = ((token < limit) & (inner < limit)).astype(F32)
        h = s.hidden
        left = sigmoid(out[:h]) * out[h : 2 * h] * mask
        right = sigmoid(out[2 * h : 3 * h]) * out[3 * h :] * mask
        if s.direct:
            split = (s.peers, s.each, s.lanes)
            both = jnp.concatenate([left.reshape(split), right.reshape(split)], 1)
            message[:, step] = both.astype(BF16)
        else:
            message[step] = jnp.concatenate([left, right], 0).astype(BF16)


def gate(s, pair, gain, out_gate, out_weight, output_gain, gating, weight, scale, wide):
    for at in range(s.width):
        normed = (normalise(pair[at].astype(F32)) * gain[...]).astype(BF16)
        gating[at] = sigmoid(jnp.dot(normed, out_gate[...], preferred_element_type=F32))
    count = s.hidden // s.pack
    wide[...] = out_weight[...].astype(F32)
    for at in range(s.pack):
        part = wide[pl.ds(at, count, stride=s.pack), :]
        weight[:, at * s.channels : (at + 1) * s.channels] = part.astype(BF16)
    wide[...] = jnp.broadcast_to(output_gain[...], (s.hidden, s.hidden)).T
    parts = [wide[pl.ds(at, count, stride=s.pack), :][:, :1] for at in range(s.pack)]
    block = lax.broadcasted_iota(jnp.int32, (count, s.lanes), 1) // s.height
    total = jnp.broadcast_to(parts[0], (count, s.lanes))
    for at in range(1, s.pack):
        total = jnp.where(block == at, parts[at], total)
    scale[...] = total


def multiply(s, received, message, wide, square):
    span = s.steps * 2 * s.each
    if s.direct:
        for peer in range(s.peers):
            wide[peer * span : (peer + 1) * span] = (
                received[peer].reshape(span, s.lanes).astype(F32)
            )
    depth = s.cols * s.steps

    def operand(side, channel):
        at = side * s.each + channel
        if s.direct:
            blocks = [
                wide[pl.ds(row * s.cols * span + at, depth, stride=2 * s.each), :]
                for row in range(s.rows)
            ]
        else:
            blocks = [received[at, row].astype(F32) for row in range(s.rows)]
        if s.pack == 1:
            return jnp.concatenate(blocks, 1).astype(BF16)
        pad = round_up(depth, 64) - depth
        blocks = swap_blocks(*blocks, s.height)
        if pad:
            empty = jnp.zeros((pad, s.lanes), F32)
            blocks = [part for block in blocks for part in (block, empty)]
        return jnp.concatenate(blocks, 0).astype(BF16)

    for group in range(s.groups):
        sums = []
        for at in range(s.pack):
            channel = group * s.pack + at
            left, right = operand(0, channel), operand(1, channel)
            sums.append(jnp.dot(right.T, left, preferred_element_type=F32))
        if s.pack == 1:
            sums = [sums[0][:, row * s.lanes : (row + 1) * s.lanes] for row in range(s.rows)]
        else:
            sums = swap_blocks(*sums, s.height)
        for row in range(s.rows):
            square[row] = sums[row]
        for row in range(s.rows):
            for col in range(s.cols):
                start = col * s.width
                if s.pack == 1:
                    start = start // s.height * s.lanes + start % s.height
                message[row * s.cols + col, group] = square[row, start : start + s.slots].astype(BF16)


def finish(s, received, gating, weight, scale, update, wide):
    count = s.hidden // s.pack
    values = received[...].reshape(count, s.slots, s.lanes).astype(F32)

    def fold(total):
        if s.pack == 1:
            return total
        low = lax.broadcasted_iota(jnp.int32, total.shape, 1) < s.height
        up = pltpu.roll(total, s.height, 1)
        down = pltpu.roll(total, s.lanes - s.height, 1)
        return total + jnp.where(low, down, up)

    average = fold(jnp.sum(values, 0)) * (1.0 / s.hidden)
    centered = values - average[None]
    variance = fold(jnp.sum(centered * centered, 0)) * (1.0 / s.hidden)
    settled = centered * lax.rsqrt(variance + EPS)[None]
    settled = settled.reshape(count * s.slots, s.lanes)
    for tile in range(s.lanes // LANES):
        wide[tile] = settled[:, tile * LANES : (tile + 1) * LANES]
    for at in range(s.width):
        rows = [
            wide[tile, pl.ds(at, count, stride=s.slots), :] for tile in range(s.lanes // LANES)
        ]
        rows = (jnp.concatenate(rows, 1) * scale[...]).astype(BF16)
        out = jnp.dot(rows.T, weight[...], preferred_element_type=F32)
        total = out[: s.height, : s.channels]
        for block in range(1, s.pack):
            total += out[
                block * s.height : (block + 1) * s.height,
                block * s.channels : (block + 1) * s.channels,
            ]
        update[at] = (gating[at] * total).astype(BF16)


def call(body, s, out_shape, scratch, flops, *operands):
    def space(operand):
        return pl.BlockSpec(memory_space=pltpu.SMEM if operand.dtype == jnp.int32 else pltpu.VMEM)

    sent = sum(o.size * o.dtype.itemsize for o in operands)
    return pl.pallas_call(
        functools.partial(body, s),
        out_shape=out_shape,
        in_specs=[space(o) for o in operands],
        out_specs=jax.tree.map(lambda _: pl.BlockSpec(memory_space=pltpu.VMEM), out_shape),
        scratch_shapes=scratch,
        compiler_params=pltpu.CompilerParams(vmem_limit_bytes=56 * 1024 * 1024),
        cost_estimate=pl.CostEstimate(flops=flops, bytes_accessed=sent, transcendentals=0),
        name=body.__name__,
    )(*operands)


def exchange(blocks):
    return lax.all_to_all(blocks, ("row", "col"), split_axis=0, concat_axis=0, tiled=True)


def local(
    mesh,
    pair_state,
    valid_length,
    input_gain,
    left_gate,
    left_value,
    right_gate,
    right_value,
    out_gate,
    output_gain,
    out_weight,
):
    height, width, channels = pair_state.shape
    hidden = left_gate.shape[1]
    s = Sizes(mesh, height, width, channels, hidden)
    shape = jax.ShapeDtypeStruct
    pair = jnp.transpose(pair_state, (1, 0, 2))
    gain = input_gain.reshape(1, channels)
    cells = height * width

    sent = (s.peers, s.steps, 2 * s.each, s.lanes)
    message = call(
        produce,
        s,
        shape(sent if s.direct else (s.steps, 2 * hidden, s.lanes), BF16),
        [],
        8 * cells * channels * hidden,
        pair,
        valid_length,
        gain,
        left_gate,
        left_value,
        right_gate,
        right_value,
    )
    if not s.direct:
        message = message.reshape(s.steps, 2, s.peers, s.each, s.lanes)
        message = message.transpose(2, 0, 1, 3, 4).reshape(sent)
    received = exchange(message)
    gating, weight, scale = call(
        gate,
        s,
        (
            shape((width, height, channels), F32),
            shape((hidden // s.pack, s.pack * channels), BF16),
            shape((hidden // s.pack, s.lanes), F32),
        ),
        [pltpu.VMEM((hidden, channels), F32)],
        2 * cells * channels * channels,
        pair,
        gain,
        out_gate,
        out_weight,
        output_gain.reshape(1, hidden),
    )
    scratch = (s.peers * s.steps * 2 * s.each, s.lanes)
    if not s.direct:
        received = received.reshape(s.rows, s.cols * s.steps, 2 * s.each, s.lanes)
        received = received.transpose(2, 0, 1, 3)
        scratch = (8, s.lanes)
    side = s.lanes if s.pack > 1 else s.rows * s.lanes
    sums = call(
        multiply,
        s,
        shape((s.peers, s.groups, s.slots, s.lanes), BF16),
        [pltpu.VMEM(scratch, F32), pltpu.VMEM((s.rows, side, s.lanes), F32)],
        2 * s.each * (s.rows * height) ** 2 * s.cols * width,
        received,
    )
    update = call(
        finish,
        s,
        shape((width, height, channels), BF16),
        [pltpu.VMEM((s.lanes // LANES, hidden // s.pack * s.slots, LANES), F32)],
        2 * cells * channels * hidden,
        exchange(sums),
        gating,
        weight,
        scale,
    )
    return jnp.transpose(update, (1, 0, 2))


def solution(mesh):
    return jax.shard_map(
        functools.partial(local, mesh),
        mesh=mesh,
        in_specs=(P(("parts", "row"), "col", None), P("parts")) + (P(),) * 8,
        out_specs=P(("parts", "row"), "col", None),
        check_vma=False,
    )
```

```python
import functools

import jax
import jax.numpy as jnp
from jax import lax
from jax.experimental import pallas as pl
from jax.experimental.pallas import tpu as pltpu
from jax.sharding import PartitionSpec as P

F32 = jnp.float32
BF16 = jnp.bfloat16
LANES = 128
SUBLANES = 16
EPS = 1e-05


def round_up(value, multiple):
    return -(-value // multiple) * multiple


class Sizes:
    def __init__(self, mesh, height, width, channels, hidden):
        self.rows = mesh.shape["row"]
        self.cols = mesh.shape["col"]
        self.peers = self.rows * self.cols
        self.height, self.width = height, width
        self.channels, self.hidden = channels, hidden
        self.each = hidden // self.peers
        fits = self.rows * height <= LANES
        self.pack = self.rows if fits and width % self.rows == 0 and self.each % self.rows == 0 else 1
        self.steps = width // self.pack
        self.groups = self.each // self.pack
        self.lanes = round_up(self.pack * height, LANES)
        self.slots = round_up(width, SUBLANES)
        self.direct = self.each % 8 == 0 and self.lanes == LANES


def normalise(values):
    average = jnp.mean(values, -1, keepdims=True)
    centered = values - average
    variance = jnp.mean(centered * centered, -1, keepdims=True)
    return centered * lax.rsqrt(variance + EPS)


def sigmoid(values):
    return 0.5 * jnp.tanh(0.5 * values) + 0.5


def swap_blocks(first, second, height):
    lanes = first.shape[-1]
    low = lax.broadcasted_iota(jnp.int32, first.shape, 1) < height
    return (
        jnp.where(low, first, pltpu.roll(second, height, 1)),
        jnp.where(low, pltpu.roll(first, lanes - height, 1), second),
    )


def produce(s, pair, length, gain, left_gate, left_value, right_gate, right_value, *rest):
    *outs, message = rest
    first = lax.axis_index("row") * s.height
    second = lax.axis_index("col") * s.width
    limit = length[0]
    weights = jnp.concatenate(
        [w[...].T for w in (left_gate, left_value, right_gate, right_value)], 0
    )
    scale = gain[...]
    lane = lax.broadcasted_iota(jnp.int32, (1, s.lanes), 1)
    block = lane // s.height
    token = first + lane - block * s.height
    for step in range(s.steps):
        normed = [
            normalise(pair[at * s.steps + step].astype(F32)) * scale for at in range(s.pack)
        ]
        if s.lanes > s.pack * s.height:
            normed.append(jnp.zeros((s.lanes - s.pack * s.height, s.channels), F32))
        normed = jnp.concatenate(normed, 0).astype(BF16)
        out = lax.dot_general(weights, normed, (((1,), (1,)), ((), ())), preferred_element_type=F32)
        inner = second + block * s.steps + step
        mask = ((token < limit) & (inner < limit)).astype(F32)
        h = s.hidden
        left = sigmoid(out[:h]) * out[h : 2 * h] * mask
        right = sigmoid(out[2 * h : 3 * h]) * out[3 * h :] * mask
        if s.direct:
            split = (s.peers, s.each, s.lanes)
            both = jnp.concatenate([left.reshape(split), right.reshape(split)], 1)
            message[:, step] = both.astype(BF16)
        else:
            outs[0][step] = jnp.concatenate([left, right], 0).astype(BF16)
    if s.direct:
        own = lax.axis_index("row") * s.cols + lax.axis_index("col")
        for mask, out in enumerate(outs):
            out[...] = message[own ^ mask]


def gate(s, pair, gain, out_gate, out_weight, output_gain, gating, weight, scale, wide):
    for at in range(s.width):
        normed = (normalise(pair[at].astype(F32)) * gain[...]).astype(BF16)
        gating[at] = sigmoid(jnp.dot(normed, out_gate[...], preferred_element_type=F32))
    count = s.hidden // s.pack
    wide[...] = out_weight[...].astype(F32)
    for at in range(s.pack):
        part = wide[pl.ds(at, count, stride=s.pack), :]
        weight[:, at * s.channels : (at + 1) * s.channels] = part.astype(BF16)
    wide[...] = jnp.broadcast_to(output_gain[...], (s.hidden, s.hidden)).T
    parts = [wide[pl.ds(at, count, stride=s.pack), :][:, :1] for at in range(s.pack)]
    block = lax.broadcasted_iota(jnp.int32, (count, s.lanes), 1) // s.height
    total = jnp.broadcast_to(parts[0], (count, s.lanes))
    for at in range(1, s.pack):
        total = jnp.where(block == at, parts[at], total)
    scale[...] = total


def multiply(s, *refs):
    span = s.steps * 2 * s.each
    own = lax.axis_index("row") * s.cols + lax.axis_index("col")
    if s.direct:
        received, outs, (message, wide, square) = refs[: s.peers], refs[s.peers : -3], refs[-3:]
        for mask in range(s.peers):
            at = pl.multiple_of((own ^ mask) * span, span)
            wide[pl.ds(at, span)] = received[mask][...].reshape(span, s.lanes).astype(F32)
    else:
        received, *outs, message, wide, square = refs
    depth = s.cols * s.steps

    def operand(side, channel):
        at = side * s.each + channel
        if s.direct:
            blocks = [
                wide[pl.ds(row * s.cols * span + at, depth, stride=2 * s.each), :]
                for row in range(s.rows)
            ]
        else:
            blocks = [received[at, row].astype(F32) for row in range(s.rows)]
        if s.pack == 1:
            return jnp.concatenate(blocks, 1).astype(BF16)
        pad = round_up(depth, 64) - depth
        blocks = swap_blocks(*blocks, s.height)
        if pad:
            empty = jnp.zeros((pad, s.lanes), F32)
            blocks = [part for block in blocks for part in (block, empty)]
        return jnp.concatenate(blocks, 0).astype(BF16)

    for group in range(s.groups):
        sums = []
        for at in range(s.pack):
            channel = group * s.pack + at
            left, right = operand(0, channel), operand(1, channel)
            sums.append(jnp.dot(right.T, left, preferred_element_type=F32))
        if s.pack == 1:
            sums = [sums[0][:, row * s.lanes : (row + 1) * s.lanes] for row in range(s.rows)]
        else:
            sums = swap_blocks(*sums, s.height)
        for row in range(s.rows):
            square[row] = sums[row]
        for row in range(s.rows):
            for col in range(s.cols):
                start = col * s.width
                if s.pack == 1:
                    start = start // s.height * s.lanes + start % s.height
                message[row * s.cols + col, group] = square[row, start : start + s.slots].astype(BF16)
    for mask, out in enumerate(outs):
        out[...] = message[own ^ mask]


def finish(s, *refs):
    received, (gating, weight, scale, update, gathered, wide) = refs[: s.peers], refs[s.peers :]
    own = lax.axis_index("row") * s.cols + lax.axis_index("col")
    for mask in range(s.peers):
        gathered[own ^ mask] = received[mask][...]
    count = s.hidden // s.pack
    values = gathered[...].reshape(count, s.slots, s.lanes).astype(F32)

    def fold(total):
        if s.pack == 1:
            return total
        low = lax.broadcasted_iota(jnp.int32, total.shape, 1) < s.height
        up = pltpu.roll(total, s.height, 1)
        down = pltpu.roll(total, s.lanes - s.height, 1)
        return total + jnp.where(low, down, up)

    average = fold(jnp.sum(values, 0)) * (1.0 / s.hidden)
    centered = values - average[None]
    variance = fold(jnp.sum(centered * centered, 0)) * (1.0 / s.hidden)
    settled = centered * lax.rsqrt(variance + EPS)[None]
    settled = settled.reshape(count * s.slots, s.lanes)
    for tile in range(s.lanes // LANES):
        wide[tile] = settled[:, tile * LANES : (tile + 1) * LANES]
    for at in range(s.width):
        rows = [
            wide[tile, pl.ds(at, count, stride=s.slots), :] for tile in range(s.lanes // LANES)
        ]
        rows = (jnp.concatenate(rows, 1) * scale[...]).astype(BF16)
        out = jnp.dot(rows.T, weight[...], preferred_element_type=F32)
        total = out[: s.height, : s.channels]
        for block in range(1, s.pack):
            total += out[
                block * s.height : (block + 1) * s.height,
                block * s.channels : (block + 1) * s.channels,
            ]
        update[at] = (gating[at] * total).astype(BF16)


def call(body, s, out_shape, scratch, flops, *operands):
    def space(operand):
        return pl.BlockSpec(memory_space=pltpu.SMEM if operand.dtype == jnp.int32 else pltpu.VMEM)

    sent = sum(o.size * o.dtype.itemsize for o in operands)
    return pl.pallas_call(
        functools.partial(body, s),
        out_shape=out_shape,
        in_specs=[space(o) for o in operands],
        out_specs=jax.tree.map(lambda _: pl.BlockSpec(memory_space=pltpu.VMEM), out_shape),
        scratch_shapes=scratch,
        compiler_params=pltpu.CompilerParams(vmem_limit_bytes=24 * 1024 * 1024),
        cost_estimate=pl.CostEstimate(flops=flops, bytes_accessed=sent, transcendentals=0),
        name=body.__name__,
    )(*operands)


def exchange(blocks):
    peers = len(blocks)
    return [blocks[0]] + [
        lax.ppermute(blocks[mask], ("row", "col"), [(at, at ^ mask) for at in range(peers)])
        for mask in range(1, peers)
    ]


def local(
    mesh,
    pair_state,
    valid_length,
    input_gain,
    left_gate,
    left_value,
    right_gate,
    right_value,
    out_gate,
    output_gain,
    out_weight,
):
    height, width, channels = pair_state.shape
    hidden = left_gate.shape[1]
    s = Sizes(mesh, height, width, channels, hidden)
    shape = jax.ShapeDtypeStruct
    pair = jnp.transpose(pair_state, (1, 0, 2))
    gain = input_gain.reshape(1, channels)
    cells = height * width

    sent = (s.steps, 2 * s.each, s.lanes)
    message = call(
        produce,
        s,
        [shape(sent, BF16)] * s.peers if s.direct else [shape((s.steps, 2 * hidden, s.lanes), BF16)],
        [pltpu.VMEM((s.peers if s.direct else 1, *sent), BF16)],
        8 * cells * channels * hidden,
        pair,
        valid_length,
        gain,
        left_gate,
        left_value,
        right_gate,
        right_value,
    )
    if not s.direct:
        message = message[0].reshape(s.steps, 2, s.peers, s.each, s.lanes)
        message = message.transpose(2, 0, 1, 3, 4).reshape(s.peers, *sent)
        own = lax.axis_index("row") * s.cols + lax.axis_index("col")
        order = own ^ jnp.arange(s.peers, dtype=jnp.int32)
        message = list(message[order])
    received = exchange(message)
    gating, weight, scale = call(
        gate,
        s,
        (
            shape((width, height, channels), F32),
            shape((hidden // s.pack, s.pack * channels), BF16),
            shape((hidden // s.pack, s.lanes), F32),
        ),
        [pltpu.VMEM((hidden, channels), F32)],
        2 * cells * channels * channels,
        pair,
        gain,
        out_gate,
        out_weight,
        output_gain.reshape(1, hidden),
    )
    scratch = (s.peers * s.steps * 2 * s.each, s.lanes)
    if not s.direct:
        received = jnp.stack(received)[order]
        received = received.reshape(s.rows, s.cols * s.steps, 2 * s.each, s.lanes)
        received = [received.transpose(2, 0, 1, 3)]
        scratch = (8, s.lanes)
    back = (s.groups, s.slots, s.lanes)
    side = s.lanes if s.pack > 1 else s.rows * s.lanes
    sums = call(
        multiply,
        s,
        [shape(back, BF16)] * s.peers,
        [
            pltpu.VMEM((s.peers, *back), BF16),
            pltpu.VMEM(scratch, F32),
            pltpu.VMEM((s.rows, side, s.lanes), F32),
        ],
        2 * s.each * (s.rows * height) ** 2 * s.cols * width,
        *received,
    )
    update = call(
        finish,
        s,
        shape((width, height, channels), BF16),
        [
            pltpu.VMEM((s.peers, *back), BF16),
            pltpu.VMEM((s.lanes // LANES, hidden // s.pack * s.slots, LANES), F32),
        ],
        2 * cells * channels * hidden,
        *exchange(sums),
        gating,
        weight,
        scale,
    )
    return jnp.transpose(update, (1, 0, 2))


def solution(mesh):
    return jax.shard_map(
        functools.partial(local, mesh),
        mesh=mesh,
        in_specs=(P(("parts", "row"), "col", None), P("parts")) + (P(),) * 8,
        out_specs=P(("parts", "row"), "col", None),
        check_vma=False,
    )
```

```python
import functools

import jax
import jax.numpy as jnp
from jax import lax
from jax.experimental import pallas as pl
from jax.experimental.pallas import tpu as pltpu
from jax.sharding import PartitionSpec as P

F32 = jnp.float32
BF16 = jnp.bfloat16
LANES = 128
EPS = 1e-05


def round_up(value, multiple):
    return -(-value // multiple) * multiple


class Sizes:
    def __init__(self, mesh, height, width, channels, hidden):
        self.rows = mesh.shape["row"]
        self.cols = mesh.shape["col"]
        self.peers = self.rows * self.cols
        self.height, self.width = height, width
        self.channels, self.hidden = channels, hidden
        self.each = hidden // self.peers
        fits = self.rows * height <= LANES
        self.pack = self.rows if fits and width % self.rows == 0 and self.each % self.rows == 0 else 1
        self.steps = width // self.pack
        self.groups = self.each // self.pack
        self.lanes = round_up(self.pack * height, LANES)
        self.direct = self.each % 8 == 0 and self.lanes == LANES


def normalise(values):
    average = jnp.mean(values, -1, keepdims=True)
    centered = values - average
    variance = jnp.mean(centered * centered, -1, keepdims=True)
    return centered * lax.rsqrt(variance + EPS)


def sigmoid(values):
    return 0.5 * jnp.tanh(0.5 * values) + 0.5


def swap_blocks(first, second, height):
    lanes = first.shape[-1]
    low = lax.broadcasted_iota(jnp.int32, first.shape, 1) < height
    return (
        jnp.where(low, first, pltpu.roll(second, height, 1)),
        jnp.where(low, pltpu.roll(first, lanes - height, 1), second),
    )


def produce(s, length, *refs):
    sources, message, held, arrived = refs[:6], refs[6], refs[7:13], refs[13]
    copies = [
        pltpu.make_async_copy(source, target, arrived.at[at])
        for at, (source, target) in enumerate(zip(sources, held))
    ]
    for copy in copies:
        copy.start()
    pair, gain, left_gate, left_value, right_gate, right_value = held
    for copy in copies:
        copy.wait()
    first = lax.axis_index("row") * s.height
    second = lax.axis_index("col") * s.width
    limit = length[0]
    weights = jnp.concatenate(
        [w[...].T for w in (left_gate, left_value, right_gate, right_value)], 0
    )
    scale = gain[...]
    lane = lax.broadcasted_iota(jnp.int32, (1, s.lanes), 1)
    block = lane // s.height
    token = first + lane - block * s.height
    for step in range(s.steps):
        normed = [
            normalise(pair[at * s.steps + step].astype(F32)) * scale for at in range(s.pack)
        ]
        if s.lanes > s.pack * s.height:
            normed.append(jnp.zeros((s.lanes - s.pack * s.height, s.channels), F32))
        normed = jnp.concatenate(normed, 0).astype(BF16)
        out = lax.dot_general(weights, normed, (((1,), (1,)), ((), ())), preferred_element_type=F32)
        inner = second + block * s.steps + step
        mask = ((token < limit) & (inner < limit)).astype(F32)
        h = s.hidden
        left = sigmoid(out[:h]) * out[h : 2 * h] * mask
        right = sigmoid(out[2 * h : 3 * h]) * out[3 * h :] * mask
        if s.direct:
            split = (s.peers, s.each, s.lanes)
            both = jnp.concatenate([left.reshape(split), right.reshape(split)], 1)
            message[:, step] = both.astype(BF16)
        else:
            message[step] = jnp.concatenate([left, right], 0).astype(BF16)


def gate(s, pair, gain, out_gate, out_weight, output_gain, gating, weight, scale, wide):
    for at in range(s.width):
        normed = (normalise(pair[at].astype(F32)) * gain[...]).astype(BF16)
        gating[at] = sigmoid(jnp.dot(normed, out_gate[...], preferred_element_type=F32))
    count = s.hidden // s.pack
    wide[...] = out_weight[...].astype(F32)
    for at in range(s.pack):
        part = wide[pl.ds(at, count, stride=s.pack), :]
        weight[:, at * s.channels : (at + 1) * s.channels] = part.astype(BF16)
    wide[...] = jnp.broadcast_to(output_gain[...], (s.hidden, s.hidden)).T
    parts = [wide[pl.ds(at, count, stride=s.pack), :][:, :1] for at in range(s.pack)]
    block = lax.broadcasted_iota(jnp.int32, (count, s.lanes), 1) // s.height
    total = jnp.broadcast_to(parts[0], (count, s.lanes))
    for at in range(1, s.pack):
        total = jnp.where(block == at, parts[at], total)
    scale[...] = total


def multiply(s, received, message, wide, square, stage):
    span = s.steps * 2 * s.each
    if s.direct:
        for peer in range(s.peers):
            wide[peer * span : (peer + 1) * span] = (
                received[peer].reshape(span, s.lanes).astype(F32)
            )
    depth = s.cols * s.steps

    def operand(side, channel):
        at = side * s.each + channel
        if s.direct:
            blocks = [
                wide[pl.ds(row * s.cols * span + at, depth, stride=2 * s.each), :]
                for row in range(s.rows)
            ]
        else:
            blocks = [received[at, row].astype(F32) for row in range(s.rows)]
        if s.pack == 1:
            return jnp.concatenate(blocks, 1).astype(BF16)
        pad = round_up(depth, 64) - depth
        blocks = swap_blocks(*blocks, s.height)
        if pad:
            empty = jnp.zeros((pad, s.lanes), F32)
            blocks = [part for block in blocks for part in (block, empty)]
        return jnp.concatenate(blocks, 0).astype(BF16)

    for group in range(s.groups):
        sums = []
        for at in range(s.pack):
            channel = group * s.pack + at
            left, right = operand(0, channel), operand(1, channel)
            sums.append(jnp.dot(right.T, left, preferred_element_type=F32))
        if s.pack == 1:
            sums = [sums[0][:, row * s.lanes : (row + 1) * s.lanes] for row in range(s.rows)]
        else:
            sums = swap_blocks(*sums, s.height)
        for row in range(s.rows):
            square[group, row] = sums[row]
    for row in range(s.rows):
        for col in range(s.cols):
            peer = row * s.cols + col
            start = col * s.width
            if s.pack == 1:
                start = start // s.height * s.lanes + start % s.height
            for group in range(s.groups):
                stage[peer, group * s.width : (group + 1) * s.width] = (
                    square[group, row, start : start + s.width]
                )
            message[peer] = stage[peer].astype(BF16)


def finish(s, received, gating, weight, scale, update, wide):
    count = s.hidden // s.pack
    tiles = s.lanes // LANES
    for peer in range(s.peers):
        rows = received[peer].astype(F32)
        for tile in range(tiles):
            wide[tile, peer * rows.shape[0] : (peer + 1) * rows.shape[0]] = (
                rows[:, tile * LANES : (tile + 1) * LANES]
            )

    def average(values):
        total = jnp.sum(values, 0, keepdims=True)
        if s.pack > 1:
            low = lax.broadcasted_iota(jnp.int32, total.shape, 1) < s.height
            up = pltpu.roll(total, s.height, 1)
            down = pltpu.roll(total, s.lanes - s.height, 1)
            total = total + jnp.where(low, down, up)
        return total * (1.0 / s.hidden)

    for at in range(s.width):
        rows = [wide[tile, pl.ds(at, count, stride=s.width), :] for tile in range(tiles)]
        rows = jnp.concatenate(rows, 1)
        rows = rows - average(rows)
        rows = rows * lax.rsqrt(average(rows * rows) + EPS) * scale[...]
        out = jnp.dot(rows.astype(BF16).T, weight[...], preferred_element_type=F32)
        total = out[: s.height, : s.channels]
        for block in range(1, s.pack):
            total += out[
                block * s.height : (block + 1) * s.height,
                block * s.channels : (block + 1) * s.channels,
            ]
        update[at] = (gating[at] * total).astype(BF16)


def call(body, s, out_shape, scratch, flops, *operands, memory=pltpu.VMEM):
    def space(operand):
        return pl.BlockSpec(memory_space=pltpu.SMEM if operand.dtype == jnp.int32 else memory)

    sent = sum(o.size * o.dtype.itemsize for o in operands)
    return pl.pallas_call(
        functools.partial(body, s),
        out_shape=out_shape,
        in_specs=[space(o) for o in operands],
        out_specs=jax.tree.map(lambda _: pl.BlockSpec(memory_space=pltpu.VMEM), out_shape),
        scratch_shapes=scratch,
        compiler_params=pltpu.CompilerParams(vmem_limit_bytes=24 * 1024 * 1024),
        cost_estimate=pl.CostEstimate(flops=flops, bytes_accessed=sent, transcendentals=0),
        name=body.__name__,
    )(*operands)


def exchange(blocks):
    return lax.all_to_all(blocks, ("row", "col"), split_axis=0, concat_axis=0, tiled=True)


def local(
    mesh,
    pair_state,
    valid_length,
    input_gain,
    left_gate,
    left_value,
    right_gate,
    right_value,
    out_gate,
    output_gain,
    out_weight,
):
    height, width, channels = pair_state.shape
    hidden = left_gate.shape[1]
    s = Sizes(mesh, height, width, channels, hidden)
    shape = jax.ShapeDtypeStruct
    pair = jnp.transpose(pair_state, (1, 0, 2))
    gain = input_gain.reshape(1, channels)
    cells = height * width

    sent = (s.peers, s.steps, 2 * s.each, s.lanes)
    operands = (pair, gain, left_gate, left_value, right_gate, right_value)
    message = call(
        produce,
        s,
        shape(sent if s.direct else (s.steps, 2 * hidden, s.lanes), BF16),
        [pltpu.VMEM(o.shape, o.dtype) for o in operands]
        + [pltpu.SemaphoreType.DMA((len(operands),))],
        8 * cells * channels * hidden,
        valid_length,
        *operands,
        memory=pltpu.HBM,
    )
    if not s.direct:
        message = message.reshape(s.steps, 2, s.peers, s.each, s.lanes)
        message = message.transpose(2, 0, 1, 3, 4).reshape(sent)
    received = exchange(message)
    gating, weight, scale = call(
        gate,
        s,
        (
            shape((width, height, channels), F32),
            shape((hidden // s.pack, s.pack * channels), BF16),
            shape((hidden // s.pack, s.lanes), F32),
        ),
        [pltpu.VMEM((hidden, channels), F32)],
        2 * cells * channels * channels,
        pair,
        gain,
        out_gate,
        out_weight,
        output_gain.reshape(1, hidden),
    )
    scratch = (s.peers * s.steps * 2 * s.each, s.lanes)
    if not s.direct:
        received = received.reshape(s.rows, s.cols * s.steps, 2 * s.each, s.lanes)
        received = received.transpose(2, 0, 1, 3)
        scratch = (8, s.lanes)
    side = s.lanes if s.pack > 1 else s.rows * s.lanes
    sums = call(
        multiply,
        s,
        shape((s.peers, s.groups * s.width, s.lanes), BF16),
        [
            pltpu.VMEM(scratch, F32),
            pltpu.VMEM((s.groups, s.rows, side, s.lanes), F32),
            pltpu.VMEM((s.peers, s.groups * s.width, s.lanes), F32),
        ],
        2 * s.each * (s.rows * height) ** 2 * s.cols * width,
        received,
    )
    update = call(
        finish,
        s,
        shape((width, height, channels), BF16),
        [pltpu.VMEM((s.lanes // LANES, hidden // s.pack * width, LANES), F32)],
        2 * cells * channels * hidden,
        exchange(sums),
        gating,
        weight,
        scale,
    )
    return jnp.transpose(update, (1, 0, 2))


def solution(mesh):
    return jax.shard_map(
        functools.partial(local, mesh),
        mesh=mesh,
        in_specs=(P(("parts", "row"), "col", None), P("parts")) + (P(),) * 8,
        out_specs=P(("parts", "row"), "col", None),
        check_vma=False,
    )
```

```python
import functools

import jax
import jax.numpy as jnp
from jax import lax
from jax.experimental import pallas as pl
from jax.experimental.pallas import tpu as pltpu
from jax.sharding import PartitionSpec as P

F32 = jnp.float32
BF16 = jnp.bfloat16
LANES = 128
EPS = 1e-05


def round_up(value, multiple):
    return -(-value // multiple) * multiple


class Sizes:
    def __init__(self, mesh, height, width, channels, hidden):
        self.rows = mesh.shape["row"]
        self.cols = mesh.shape["col"]
        self.peers = self.rows * self.cols
        self.height, self.width = height, width
        self.channels, self.hidden = channels, hidden
        self.each = hidden // self.peers
        self.tokens = self.rows * height
        self.wide = round_up(self.tokens, LANES)
        fits = self.tokens <= LANES and self.each % self.rows == 0
        self.pack = self.rows if fits else 1
        self.groups = self.each // self.pack
        self.lanes = round_up(self.pack * height, LANES)
        self.direct = self.each % 8 == 0 and self.wide == LANES


def normalise(values):
    average = jnp.mean(values, -1, keepdims=True)
    centered = values - average
    variance = jnp.mean(centered * centered, -1, keepdims=True)
    return centered * lax.rsqrt(variance + EPS)


def sigmoid(values):
    return 0.5 * jnp.tanh(0.5 * values) + 0.5


def swap_blocks(first, second, height):
    lanes = first.shape[-1]
    low = lax.broadcasted_iota(jnp.int32, first.shape, 1) < height
    return (
        jnp.where(low, first, pltpu.roll(second, height, 1)),
        jnp.where(low, pltpu.roll(first, lanes - height, 1), second),
    )


def produce(s, pair, length, gain, left_gate, left_value, right_gate, right_value, message, turned):
    mine = lax.axis_index("row")
    second = lax.axis_index("col") * s.width
    limit = length[0]
    split = (s.rows, s.cols, s.each, s.channels)
    half = s.hidden // s.rows
    for at, weight in enumerate((left_gate, left_value, right_gate, right_value)):
        turned[at] = weight[...].astype(F32).T.reshape(split)
    weights = turned[:, mine].reshape(4 * half, s.channels).astype(BF16)
    token = lax.broadcasted_iota(jnp.int32, (1, s.wide), 1)
    for step in range(s.width):
        normed = normalise(pair[step].astype(F32)) * gain[...]
        if s.wide > s.tokens:
            empty = jnp.zeros((s.wide - s.tokens, s.channels), F32)
            normed = jnp.concatenate([normed, empty], 0)
        normed = normed.astype(BF16)
        out = lax.dot_general(weights, normed, (((1,), (1,)), ((), ())), preferred_element_type=F32)
        mask = ((token < limit) & (second + step < limit)).astype(F32)
        left = sigmoid(out[:half]) * out[half : 2 * half] * mask
        right = sigmoid(out[2 * half : 3 * half]) * out[3 * half :] * mask
        if s.direct:
            split = (s.cols, s.each, s.wide)
            both = jnp.concatenate([left.reshape(split), right.reshape(split)], 1)
            message[:, step] = both.astype(BF16)
        else:
            message[step] = jnp.concatenate([left, right], 0).astype(BF16)


def gate(s, pair, gain, out_gate, out_weight, output_gain, gating, weight, scale, wide):
    for at in range(s.width):
        normed = (normalise(pair[at].astype(F32)) * gain[...]).astype(BF16)
        gating[at] = sigmoid(jnp.dot(normed, out_gate[...], preferred_element_type=F32))
    count = s.hidden // s.pack
    wide[...] = out_weight[...].astype(F32)
    for at in range(s.pack):
        part = wide[pl.ds(at, count, stride=s.pack), :]
        weight[:, at * s.channels : (at + 1) * s.channels] = part.astype(BF16)
    wide[...] = jnp.broadcast_to(output_gain[...], (s.hidden, s.hidden)).T
    parts = [wide[pl.ds(at, count, stride=s.pack), :][:, :1] for at in range(s.pack)]
    block = lax.broadcasted_iota(jnp.int32, (count, s.lanes), 1) // s.height
    total = jnp.broadcast_to(parts[0], (count, s.lanes))
    for at in range(1, s.pack):
        total = jnp.where(block == at, parts[at], total)
    scale[...] = total


def multiply(s, received, message, wide, square, stage):
    depth = s.cols * s.width
    if s.direct:
        span = s.width * 2 * s.each
        for peer in range(s.cols):
            wide[peer * span : (peer + 1) * span] = (
                received[peer].reshape(span, s.wide).astype(F32)
            )

    def operand(at):
        if s.direct:
            return wide[pl.ds(at, depth, stride=2 * s.each), :].astype(BF16)
        return received[at]

    for group in range(s.groups):
        sums = []
        for at in range(s.pack):
            channel = group * s.pack + at
            left, right = operand(channel), operand(s.each + channel)
            sums.append(jnp.dot(right.T, left, preferred_element_type=F32))
        if s.pack == 1:
            shifts = [(s.wide - row * s.height) % s.wide for row in range(s.rows)]
            sums = [(pltpu.roll(sums[0], at, 1) if at else sums[0])[:, : s.lanes] for at in shifts]
        else:
            sums = swap_blocks(*sums, s.height)
        for row in range(s.rows):
            square[group, row] = sums[row]
    for row in range(s.rows):
        for col in range(s.cols):
            peer = row * s.cols + col
            start = col * s.width
            for group in range(s.groups):
                stage[peer, group * s.width : (group + 1) * s.width] = (
                    square[group, row, start : start + s.width]
                )
            message[peer] = stage[peer].astype(BF16)


def finish(s, received, gating, weight, scale, update, wide):
    count = s.hidden // s.pack
    tiles = s.lanes // LANES
    for peer in range(s.peers):
        rows = received[peer].astype(F32)
        for tile in range(tiles):
            wide[tile, peer * rows.shape[0] : (peer + 1) * rows.shape[0]] = (
                rows[:, tile * LANES : (tile + 1) * LANES]
            )

    def average(values):
        total = jnp.sum(values, 0, keepdims=True)
        if s.pack > 1:
            low = lax.broadcasted_iota(jnp.int32, total.shape, 1) < s.height
            up = pltpu.roll(total, s.height, 1)
            down = pltpu.roll(total, s.lanes - s.height, 1)
            total = total + jnp.where(low, down, up)
        return total * (1.0 / s.hidden)

    for at in range(s.width):
        rows = [wide[tile, pl.ds(at, count, stride=s.width), :] for tile in range(tiles)]
        rows = jnp.concatenate(rows, 1)
        rows = rows - average(rows)
        rows = rows * lax.rsqrt(average(rows * rows) + EPS) * scale[...]
        out = jnp.dot(rows.astype(BF16).T, weight[...], preferred_element_type=F32)
        total = out[: s.height, : s.channels]
        for block in range(1, s.pack):
            total += out[
                block * s.height : (block + 1) * s.height,
                block * s.channels : (block + 1) * s.channels,
            ]
        update[at] = (gating[at] * total).astype(BF16)


def call(body, s, out_shape, scratch, flops, *operands):
    def space(operand):
        return pl.BlockSpec(memory_space=pltpu.SMEM if operand.dtype == jnp.int32 else pltpu.VMEM)

    sent = sum(o.size * o.dtype.itemsize for o in operands)
    return pl.pallas_call(
        functools.partial(body, s),
        out_shape=out_shape,
        in_specs=[space(o) for o in operands],
        out_specs=jax.tree.map(lambda _: pl.BlockSpec(memory_space=pltpu.VMEM), out_shape),
        scratch_shapes=scratch,
        compiler_params=pltpu.CompilerParams(vmem_limit_bytes=24 * 1024 * 1024),
        cost_estimate=pl.CostEstimate(flops=flops, bytes_accessed=sent, transcendentals=0),
        name=body.__name__,
    )(*operands)


def exchange(blocks, axes):
    return lax.all_to_all(blocks, axes, split_axis=0, concat_axis=0, tiled=True)


def local(
    mesh,
    pair_state,
    valid_length,
    input_gain,
    left_gate,
    left_value,
    right_gate,
    right_value,
    out_gate,
    output_gain,
    out_weight,
):
    height, width, channels = pair_state.shape
    hidden = left_gate.shape[1]
    s = Sizes(mesh, height, width, channels, hidden)
    shape = jax.ShapeDtypeStruct
    pair = jnp.transpose(pair_state, (1, 0, 2))
    gain = input_gain.reshape(1, channels)
    cells = height * width

    sent = (s.cols, s.width, 2 * s.each, s.wide)
    whole = lax.all_gather(pair, "row", axis=1, tiled=True)
    message = call(
        produce,
        s,
        shape(sent if s.direct else (s.width, 2 * s.cols * s.each, s.wide), BF16),
        [pltpu.VMEM((4, s.rows, s.cols, s.each, channels), F32)],
        8 * cells * channels * hidden,
        whole,
        valid_length,
        gain,
        left_gate,
        left_value,
        right_gate,
        right_value,
    )
    if not s.direct:
        message = message.reshape(s.width, 2, s.cols, s.each, s.wide)
        message = message.transpose(2, 0, 1, 3, 4).reshape(sent)
    received = exchange(message, "col")
    gating, weight, scale = call(
        gate,
        s,
        (
            shape((width, height, channels), F32),
            shape((hidden // s.pack, s.pack * channels), BF16),
            shape((hidden // s.pack, s.lanes), F32),
        ),
        [pltpu.VMEM((hidden, channels), F32)],
        2 * cells * channels * channels,
        pair,
        gain,
        out_gate,
        out_weight,
        output_gain.reshape(1, hidden),
    )
    scratch = (s.cols * s.width * 2 * s.each, s.wide)
    if not s.direct:
        received = received.reshape(s.cols * s.width, 2 * s.each, s.wide).transpose(1, 0, 2)
        scratch = (8, s.wide)
    sums = call(
        multiply,
        s,
        shape((s.peers, s.groups * s.width, s.lanes), BF16),
        [
            pltpu.VMEM(scratch, F32),
            pltpu.VMEM((s.groups, s.rows, s.wide, s.lanes), F32),
            pltpu.VMEM((s.peers, s.groups * s.width, s.lanes), F32),
        ],
        2 * s.each * (s.rows * height) ** 2 * s.cols * width,
        received,
    )
    update = call(
        finish,
        s,
        shape((width, height, channels), BF16),
        [pltpu.VMEM((s.lanes // LANES, hidden // s.pack * width, LANES), F32)],
        2 * cells * channels * hidden,
        exchange(sums, ("row", "col")),
        gating,
        weight,
        scale,
    )
    return jnp.transpose(update, (1, 0, 2))


def solution(mesh):
    return jax.shard_map(
        functools.partial(local, mesh),
        mesh=mesh,
        in_specs=(P(("parts", "row"), "col", None), P("parts")) + (P(),) * 8,
        out_specs=P(("parts", "row"), "col", None),
        check_vma=False,
    )
```

```python
import functools

import jax
import jax.numpy as jnp
from jax import lax
from jax.experimental import pallas as pl
from jax.experimental.pallas import tpu as pltpu
from jax.sharding import PartitionSpec as P

F32 = jnp.float32
BF16 = jnp.bfloat16
EPS = 1e-05
TILE = 16
CHUNK = 56
GROUP = 7


class Sizes:
    def __init__(self, mesh, height, width, channels, hidden):
        self.rows = mesh.shape["row"]
        self.cols = mesh.shape["col"]
        self.height, self.width = height, width
        self.channels, self.hidden = channels, hidden
        self.half = width // 2
        self.slots = -(-width // TILE) * TILE


def column_at(place, cols):
    return jnp.where(place < cols // 2, 2 * place, 2 * (cols - place) - 1)


def place_of(column, cols):
    return jnp.where(column % 2 == 0, column // 2, cols - 1 - column // 2)


def ring(cols):
    return [2 * at if at < cols // 2 else 2 * (cols - at) - 1 for at in range(cols)]


def normalise(values):
    average = jnp.mean(values, -1, keepdims=True)
    centered = values - average
    variance = jnp.mean(centered * centered, -1, keepdims=True)
    return centered * lax.rsqrt(variance + EPS)


def sigmoid(values):
    return 0.5 * jnp.tanh(0.5 * values) + 0.5


def dot(left, right):
    return jnp.dot(left, right, preferred_element_type=F32)


def project(s, sources, gated, length, gain, *refs):
    count = len(sources)
    halves, refs = refs[:count], refs[count:]
    left_gate, left_value, right_gate, right_value, *refs = refs
    if gated:
        out_gate, left, right, gating, rows, picked = refs
    else:
        left, right, rows, picked = refs
    row, col = lax.axis_index("row"), lax.axis_index("col")
    limit = length[0]
    first = row * s.height
    offset = (col % (s.height // s.width)) * s.width
    below = lax.broadcasted_iota(jnp.int32, (s.height, 1), 0) + first < limit
    mine = lax.broadcasted_iota(jnp.int32, (s.slots, 1), 0) + col * s.width < limit
    for index, (distance, start) in enumerate(sources):
        place = (place_of(col, s.cols) + distance + s.cols) % s.cols
        token = column_at(place, s.cols) * s.width + start
        for step in range(s.half):
            at = step * s.height
            rows[at : at + s.height] = normalise(halves[index][step].astype(F32)) * gain[...]
            picked[step * s.slots : (step + 1) * s.slots] = rows[pl.ds(at + offset, s.slots), :]
        span = s.half * s.height
        normed = rows[:span].astype(BF16)
        value = sigmoid(dot(normed, left_gate[...])) * dot(normed, left_value[...])
        for step in range(s.half):
            mask = (below & (token + step < limit)).astype(F32)
            part = value[step * s.height : (step + 1) * s.height] * mask
            left[index * s.half + step] = part.astype(BF16)
        if gated:
            gate = sigmoid(dot(normed, out_gate[...]))
            for step in range(s.half):
                gating[index * s.half + step] = gate[step * s.height : (step + 1) * s.height]
        normed = picked[...].astype(BF16)
        value = sigmoid(dot(normed, right_gate[...])) * dot(normed, right_value[...])
        for step in range(s.half):
            mask = (mine & (token + step < limit)).astype(F32)
            part = value[step * s.slots : (step + 1) * s.slots] * mask
            right[index * s.half + step] = part.astype(BF16)


def accumulate(s, left, right, other, total, partner, fresh):
    row, col = lax.axis_index("row"), lax.axis_index("col")
    owner = col // (s.height // s.width)
    depth = left.shape[0]

    @pl.when(row == owner)
    def _():
        partner[:depth] = right[...].astype(F32)

    @pl.when(row != owner)
    def _():
        partner[:depth] = other[...].astype(F32)

    size = CHUNK if s.height % CHUNK == 0 else s.height
    group = GROUP if s.width % GROUP == 0 else 1

    def chunk(index, carry):
        at = pl.ds(pl.multiple_of(index * size, 8), size)
        for first in range(0, s.width, group):
            members = range(first, first + group)
            if fresh:
                sums = tuple(jnp.zeros((size, s.hidden), F32) for _ in members)
            else:
                sums = tuple(total[j, at] for j in members)

            def step(k, sums):
                value = left[k, at].astype(F32)
                return tuple(
                    so_far + value * partner[k, j : j + 1] for so_far, j in zip(sums, members)
                )

            sums = lax.fori_loop(0, depth, step, sums)
            for so_far, j in zip(sums, members):
                total[j, at] = so_far
        return carry

    lax.fori_loop(0, s.height // size, chunk, 0)


def add_first(s, left, right, other, total, partner):
    accumulate(s, left, right, other, total, partner, True)


def add_more(s, left, right, other, before, total, partner):
    total[...] = before[...]
    accumulate(s, left, right, other, total, partner, False)


def finish(s, left, right, other, before, gating, gain, weight, update, total, partner):
    total[...] = before[...]
    accumulate(s, left, right, other, total, partner, False)
    for at in range(s.width):
        settled = (normalise(total[at]) * gain[...]).astype(BF16)
        update[at] = (gating[at] * dot(settled, weight[...])).astype(BF16)


def call(body, out_shape, scratch, flops, *operands, aliases=None):
    def space(operand):
        return pl.BlockSpec(memory_space=pltpu.SMEM if operand.dtype == jnp.int32 else pltpu.VMEM)

    sent = sum(o.size * o.dtype.itemsize for o in operands)
    return pl.pallas_call(
        body,
        out_shape=out_shape,
        in_specs=[space(o) for o in operands],
        out_specs=jax.tree.map(lambda _: pl.BlockSpec(memory_space=pltpu.VMEM), out_shape),
        scratch_shapes=scratch,
        compiler_params=pltpu.CompilerParams(vmem_limit_bytes=24 * 1024 * 1024),
        cost_estimate=pl.CostEstimate(flops=flops, bytes_accessed=sent, transcendentals=0),
        name=body.func.__name__,
    )(*operands)


def local(
    mesh,
    pair_state,
    valid_length,
    input_gain,
    left_gate,
    left_value,
    right_gate,
    right_value,
    out_gate,
    output_gain,
    out_weight,
):
    height, width, channels = pair_state.shape
    hidden = left_gate.shape[1]
    s = Sizes(mesh, height, width, channels, hidden)
    shape = jax.ShapeDtypeStruct
    pair = jnp.transpose(pair_state, (1, 0, 2))
    gain = input_gain.reshape(1, channels)
    weights = (left_gate, left_value, right_gate, right_value)
    order = ring(s.cols)

    def shift(block, by):
        pairs = [(order[at], order[(at + by) % s.cols]) for at in range(s.cols)]
        return lax.ppermute(block, "col", pairs)

    def swap(block):
        return lax.ppermute(block, "row", [(at, (at + 1) % s.rows) for at in range(s.rows)])

    def run(halves, sources, gated=False):
        depth = len(halves) * s.half
        out = [
            shape((depth, height, hidden), BF16),
            shape((depth, s.slots, hidden), BF16),
        ]
        if gated:
            out.append(shape((width, height, channels), F32))
        left, right, *more = call(
            functools.partial(project, s, sources, gated),
            out,
            [
                pltpu.VMEM((s.half * height + TILE, channels), F32),
                pltpu.VMEM((s.half * s.slots, channels), F32),
            ],
            4 * depth * height * channels * hidden,
            valid_length,
            gain,
            *halves,
            *weights,
            *((out_gate,) if gated else ()),
        )
        return (left, right), more

    low, high = pair[: s.half], pair[s.half :]
    starts = (0, s.half)
    sums = shape((width, height, hidden), F32)

    def add(total, terms):
        left, right = terms
        depth = left.shape[0]
        body, before = (add_first, ()) if total is None else (add_more, (total,))
        return call(
            functools.partial(body, s),
            sums,
            [pltpu.VMEM((depth, s.slots, hidden), F32)],
            16 * depth * height * width * hidden,
            left,
            right,
            swap(right),
            *before,
        )

    blocks, sources, gating = [low, high], [(0, at) for at in starts], None
    travel = [low, high, low, high]
    total = terms = None
    for distance in range(1, s.cols // 2 + 1):
        if distance < s.cols // 2:
            arrived = [shift(block, by) for block, by in zip(travel, (1, 1, -1, -1))]
            after = [(by, at) for by in (-distance, distance) for at in starts]
        else:
            arrived = [shift(travel[0], 1), shift(travel[3], -1)]
            after = [(-distance, 0), (distance, s.half)]
        pending, more = run(blocks, sources, gated=gating is None)
        gating = more[0] if more else gating
        if terms is not None:
            total = add(total, terms)
        terms = pending
        arrived, terms, total = lax.optimization_barrier((arrived, terms, total))
        blocks, sources, travel = arrived, after, arrived
    pending, _ = run(blocks, sources)
    left, right = pending
    other = swap(right)
    total = add(total, terms)
    update = call(
        functools.partial(finish, s),
        shape((width, height, channels), BF16),
        [pltpu.VMEM(sums.shape, F32), pltpu.VMEM((left.shape[0], s.slots, hidden), F32)],
        16 * width * height * width * hidden,
        left,
        right,
        other,
        total,
        gating,
        output_gain.reshape(1, hidden),
        out_weight,
    )
    return jnp.transpose(update, (1, 0, 2))


def solution(mesh):
    return jax.shard_map(
        functools.partial(local, mesh),
        mesh=mesh,
        in_specs=(P(("parts", "row"), "col", None), P("parts")) + (P(),) * 8,
        out_specs=P(("parts", "row"), "col", None),
        check_vma=False,
    )
```

```python
import functools

import jax
import jax.numpy as jnp
from jax import lax
from jax.experimental import pallas as pl
from jax.experimental.pallas import tpu as pltpu
from jax.sharding import PartitionSpec as P

F32 = jnp.float32
BF16 = jnp.bfloat16
EPS = 1e-05
TILE = 16
CHUNK = 56
GROUP = 7


class Sizes:
    def __init__(self, mesh, height, width, channels, hidden):
        self.rows = mesh.shape["row"]
        self.cols = mesh.shape["col"]
        self.height, self.width = height, width
        self.channels, self.hidden = channels, hidden
        self.half = width // 2
        self.slots = -(-width // TILE) * TILE


def column_at(place, cols):
    return jnp.where(place < cols // 2, 2 * place, 2 * (cols - place) - 1)


def place_of(column, cols):
    return jnp.where(column % 2 == 0, column // 2, cols - 1 - column // 2)


def ring(cols):
    return [2 * at if at < cols // 2 else 2 * (cols - at) - 1 for at in range(cols)]


def normalise(values):
    average = jnp.mean(values, -1, keepdims=True)
    centered = values - average
    variance = jnp.mean(centered * centered, -1, keepdims=True)
    return centered * lax.rsqrt(variance + EPS)


def sigmoid(values):
    return 0.5 * jnp.tanh(0.5 * values) + 0.5


def dot(left, right):
    return jnp.dot(left, right, preferred_element_type=F32)


def project(s, sources, gated, length, gain, *refs):
    count = 1 + max(source[0] for source in sources)
    blocks, refs = refs[:count], refs[count:]
    left_gate, left_value, right_gate, right_value, *refs = refs
    if gated:
        out_gate, *later, left, right, gating = refs[:-4]
        for source, target in zip(later, refs[-4:-2]):
            target[...] = source[...]
    else:
        left, right = refs[:-2]
    rows, picked = refs[-2:]
    row, col = lax.axis_index("row"), lax.axis_index("col")
    limit = length[0]
    first = row * s.height
    offset = (col % (s.height // s.width)) * s.width
    below = lax.broadcasted_iota(jnp.int32, (s.height, 1), 0) + first < limit
    mine = lax.broadcasted_iota(jnp.int32, (s.slots, 1), 0) + col * s.width < limit
    for index, (block, inside, distance, start) in enumerate(sources):
        place = (place_of(col, s.cols) + distance + s.cols) % s.cols
        token = column_at(place, s.cols) * s.width + start
        for step in range(s.half):
            at = step * s.height
            rows[at : at + s.height] = normalise(blocks[block][inside + step].astype(F32)) * gain[...]
            picked[step * s.slots : (step + 1) * s.slots] = rows[pl.ds(at + offset, s.slots), :]
        span = s.half * s.height
        normed = rows[:span].astype(BF16)
        value = sigmoid(dot(normed, left_gate[...])) * dot(normed, left_value[...])
        for step in range(s.half):
            mask = (below & (token + step < limit)).astype(F32)
            part = value[step * s.height : (step + 1) * s.height] * mask
            left[index * s.half + step] = part
        if gated:
            gate = sigmoid(dot(normed, out_gate[...]))
            for step in range(s.half):
                gating[index * s.half + step] = gate[step * s.height : (step + 1) * s.height]
        normed = picked[...].astype(BF16)
        value = sigmoid(dot(normed, right_gate[...])) * dot(normed, right_value[...])
        for step in range(s.half):
            mask = (mine & (token + step < limit)).astype(F32)
            part = value[step * s.slots : (step + 1) * s.slots] * mask
            right[index * s.half + step] = part.astype(BF16)


def accumulate(s, left, right, other, total, partner, fresh):
    row, col = lax.axis_index("row"), lax.axis_index("col")
    owner = col // (s.height // s.width)
    depth = left.shape[0]

    @pl.when(row == owner)
    def _():
        partner[:depth] = right[...].astype(F32)

    @pl.when(row != owner)
    def _():
        partner[:depth] = other[...].astype(F32)

    size = CHUNK if s.height % CHUNK == 0 else s.height
    group = GROUP if s.width % GROUP == 0 else 1

    def chunk(index, carry):
        at = pl.ds(pl.multiple_of(index * size, 8), size)
        for first in range(0, s.width, group):
            members = range(first, first + group)
            if fresh:
                sums = tuple(jnp.zeros((size, s.hidden), F32) for _ in members)
            else:
                sums = tuple(total[j, at] for j in members)

            def step(k, sums):
                value = left[k, at]
                return tuple(
                    so_far + value * partner[k, j : j + 1] for so_far, j in zip(sums, members)
                )

            sums = lax.fori_loop(0, depth, step, sums)
            for so_far, j in zip(sums, members):
                total[j, at] = so_far
        return carry

    lax.fori_loop(0, s.height // size, chunk, 0)


def add_first(s, left, right, other, total, partner):
    accumulate(s, left, right, other, total, partner, True)


def add_more(s, left, right, other, before, total, partner):
    total[...] = before[...]
    accumulate(s, left, right, other, total, partner, False)


def finish(s, left, right, other, before, gating, gain, weight, update, total, partner):
    total[...] = before[...]
    accumulate(s, left, right, other, total, partner, False)
    for at in range(s.width):
        settled = (normalise(total[at]) * gain[...]).astype(BF16)
        update[at] = (gating[at] * dot(settled, weight[...])).astype(BF16)


def call(body, out_shape, scratch, flops, *operands, grant=24):
    def space(operand):
        return pl.BlockSpec(memory_space=pltpu.SMEM if operand.dtype == jnp.int32 else pltpu.VMEM)

    sent = sum(o.size * o.dtype.itemsize for o in operands)
    return pl.pallas_call(
        body,
        out_shape=out_shape,
        in_specs=[space(o) for o in operands],
        out_specs=jax.tree.map(lambda _: pl.BlockSpec(memory_space=pltpu.VMEM), out_shape),
        scratch_shapes=scratch,
        compiler_params=pltpu.CompilerParams(vmem_limit_bytes=grant * 1024 * 1024),
        cost_estimate=pl.CostEstimate(flops=flops, bytes_accessed=sent, transcendentals=0),
        name=body.func.__name__,
    )(*operands)


def local(
    mesh,
    pair_state,
    valid_length,
    input_gain,
    left_gate,
    left_value,
    right_gate,
    right_value,
    out_gate,
    output_gain,
    out_weight,
):
    height, width, channels = pair_state.shape
    hidden = left_gate.shape[1]
    s = Sizes(mesh, height, width, channels, hidden)
    shape = jax.ShapeDtypeStruct
    pair = jnp.transpose(pair_state, (1, 0, 2))
    gain = input_gain.reshape(1, channels)
    weights = (left_gate, left_value, right_gate, right_value)
    order = ring(s.cols)

    def shift(block, by):
        pairs = [(order[at], order[(at + by) % s.cols]) for at in range(s.cols)]
        return lax.ppermute(block, "col", pairs)

    def swap(block):
        return lax.ppermute(block, "row", [(at, (at + 1) % s.rows) for at in range(s.rows)])

    def run(blocks, sources, gated=False):
        depth = len(sources) * s.half
        later = (output_gain.reshape(1, hidden), out_weight) if gated else ()
        out = [shape((depth, height, hidden), F32), shape((depth, s.slots, hidden), BF16)]
        if gated:
            out += [shape((width, height, channels), F32)]
            out += [shape(o.shape, o.dtype) for o in later]
        left, right, *more = call(
            functools.partial(project, s, sources, gated),
            out,
            [
                pltpu.VMEM((s.half * height + TILE, channels), F32),
                pltpu.VMEM((s.half * s.slots, channels), F32),
            ],
            4 * depth * height * channels * hidden,
            valid_length,
            gain,
            *blocks,
            *weights,
            *((out_gate, *later) if gated else ()),
            grant=56 if gated else 24,
        )
        return (left, right), more

    starts = (0, s.half)
    sums = shape((width, height, hidden), F32)

    def add(total, terms):
        left, right = terms
        depth = left.shape[0]
        body, before = (add_first, ()) if total is None else (add_more, (total,))
        return call(
            functools.partial(body, s),
            sums,
            [pltpu.VMEM((depth, s.slots, hidden), F32)],
            16 * depth * height * width * hidden,
            left,
            right,
            swap(right),
            *before,
        )

    def whole(distances):
        return [
            (block, at, distance, at) for block, distance in enumerate(distances) for at in starts
        ]

    far = s.cols // 2
    blocks, sources, travel = [pair], whole([0]), [pair, pair]
    total = terms = kept = None
    for distance in range(1, far + 1):
        if distance == far:
            travel = [travel[0][: s.half], travel[1][s.half :]]
        arrived = [shift(block, by) for block, by in zip(travel, (1, -1))]
        pending, more = run(blocks, sources, gated=kept is None)
        kept = more or kept
        if terms is not None:
            total = add(total, terms)
        terms = pending
        done = (terms, total)
        travel = [lax.optimization_barrier((block, done))[0] for block in arrived]
        blocks, sources = arrived, whole([-distance, distance])
    left, right = run(travel, [(0, 0, -far, 0), (1, 0, far, s.half)])[0]
    other = swap(right)
    total = add(total, terms)
    gating, last_gain, last_weight = kept
    update = call(
        functools.partial(finish, s),
        shape((width, height, channels), BF16),
        [pltpu.VMEM(sums.shape, F32), pltpu.VMEM((left.shape[0], s.slots, hidden), F32)],
        16 * width * height * width * hidden,
        left,
        right,
        other,
        total,
        gating,
        last_gain,
        last_weight,
    )
    return jnp.transpose(update, (1, 0, 2))


def solution(mesh):
    return jax.shard_map(
        functools.partial(local, mesh),
        mesh=mesh,
        in_specs=(P(("parts", "row"), "col", None), P("parts")) + (P(),) * 8,
        out_specs=P(("parts", "row"), "col", None),
        check_vma=False,
    )
```

```python
import functools

import jax
import jax.numpy as jnp
from jax import lax
from jax.experimental import pallas as pl
from jax.experimental.pallas import tpu as pltpu
from jax.sharding import PartitionSpec as P

F32 = jnp.float32
BF16 = jnp.bfloat16
EPS = 1e-05
TILE = 16
CHUNK = 56
GROUP = 7


class Sizes:
    def __init__(self, mesh, height, width, channels, hidden):
        self.rows = mesh.shape["row"]
        self.cols = mesh.shape["col"]
        self.height, self.width = height, width
        self.channels, self.hidden = channels, hidden
        self.half = width // 2
        self.slots = -(-width // TILE) * TILE


def column_at(place, cols):
    return jnp.where(place < cols // 2, 2 * place, 2 * (cols - place) - 1)


def place_of(column, cols):
    return jnp.where(column % 2 == 0, column // 2, cols - 1 - column // 2)


def ring(cols):
    return [2 * at if at < cols // 2 else 2 * (cols - at) - 1 for at in range(cols)]


def normalise(values):
    average = jnp.mean(values, -1, keepdims=True)
    centered = values - average
    variance = jnp.mean(centered * centered, -1, keepdims=True)
    return centered * lax.rsqrt(variance + EPS)


def sigmoid(values):
    return 0.5 * jnp.tanh(0.5 * values) + 0.5


def dot(left, right):
    return jnp.dot(left, right, preferred_element_type=F32)


def project(s, sources, length, gain, weight, *refs):
    *blocks, left, right, rows = refs
    row, col = lax.axis_index("row"), lax.axis_index("col")
    limit = length[0]
    offset = (col % (s.height // s.width)) * s.width
    below = lax.broadcasted_iota(jnp.int32, (s.height, 1), 0) + row * s.height < limit
    mine = lax.broadcasted_iota(jnp.int32, (s.slots, 1), 0) + col * s.width < limit
    h = s.hidden
    for index, (block, inside, distance, start) in enumerate(sources):
        place = (place_of(col, s.cols) + distance + s.cols) % s.cols
        token = column_at(place, s.cols) * s.width + start
        normed = []
        for step in range(s.half):
            normed.append(normalise(blocks[block][inside + step].astype(F32)) * gain[...])
            rows[index, step, : s.height] = normed[-1]
        out = dot(jnp.concatenate(normed, 0).astype(BF16), weight[:, : 2 * h])
        value = sigmoid(out[:, :h]) * out[:, h:]
        for step in range(s.half):
            mask = (below & (token + step < limit)).astype(F32)
            left[index * s.half + step] = value[step * s.height : (step + 1) * s.height] * mask
        picked = [rows[index, step, pl.ds(offset, s.slots), :] for step in range(s.half)]
        out = dot(jnp.concatenate(picked, 0).astype(BF16), weight[:, 2 * h :])
        value = sigmoid(out[:, :h]) * out[:, h:]
        for step in range(s.half):
            mask = (mine & (token + step < limit)).astype(F32)
            part = value[step * s.slots : (step + 1) * s.slots] * mask
            right[index * s.half + step] = part.astype(BF16)


def gate(s, pair, gain, out_gate, last_gain, last_weight, gating, kept_gain, kept_weight):
    kept_gain[...] = last_gain[...]
    kept_weight[...] = last_weight[...]
    for start in range(0, s.width, s.half):
        normed = [
            normalise(pair[start + step].astype(F32)) * gain[...] for step in range(s.half)
        ]
        value = sigmoid(dot(jnp.concatenate(normed, 0).astype(BF16), out_gate[...]))
        for step in range(s.half):
            gating[start + step] = value[step * s.height : (step + 1) * s.height]


def accumulate(s, left, right, other, before, total, partner):
    row, col = lax.axis_index("row"), lax.axis_index("col")
    owner = col // (s.height // s.width)
    depth = left.shape[0]

    @pl.when(row == owner)
    def _():
        partner[:depth] = right[...].astype(F32)

    @pl.when(row != owner)
    def _():
        partner[:depth] = other[...].astype(F32)

    size = CHUNK if s.height % CHUNK == 0 else s.height
    group = GROUP if s.width % GROUP == 0 else 1

    def chunk(index, carry):
        at = pl.ds(pl.multiple_of(index * size, 8), size)
        for first in range(0, s.width, group):
            members = range(first, first + group)
            if before is None:
                sums = tuple(jnp.zeros((size, s.hidden), F32) for _ in members)
            else:
                sums = tuple(before[j, at] for j in members)

            def step(k, sums):
                value = left[k, at]
                return tuple(
                    so_far + value * partner[k, j : j + 1] for so_far, j in zip(sums, members)
                )

            sums = lax.fori_loop(0, depth, step, sums, unroll=s.half)
            for so_far, j in zip(sums, members):
                total[j, at] = so_far
        return carry

    lax.fori_loop(0, s.height // size, chunk, 0)


def add_first(s, left, right, other, total, partner):
    accumulate(s, left, right, other, None, total, partner)


def add_more(s, left, right, other, before, total, partner):
    accumulate(s, left, right, other, before, total, partner)


def finish(s, left, right, other, before, gating, gain, weight, update, total, partner):
    accumulate(s, left, right, other, before, total, partner)
    for start in range(0, s.width, s.half):
        settled = [normalise(total[start + step]) * gain[...] for step in range(s.half)]
        value = dot(jnp.concatenate(settled, 0).astype(BF16), weight[...])
        for step in range(s.half):
            part = gating[start + step] * value[step * s.height : (step + 1) * s.height]
            update[start + step] = part.astype(BF16)


def call(body, out_shape, scratch, flops, *operands):
    def space(operand):
        return pl.BlockSpec(memory_space=pltpu.SMEM if operand.dtype == jnp.int32 else pltpu.VMEM)

    sent = sum(o.size * o.dtype.itemsize for o in operands)
    return pl.pallas_call(
        body,
        out_shape=out_shape,
        in_specs=[space(o) for o in operands],
        out_specs=jax.tree.map(lambda _: pl.BlockSpec(memory_space=pltpu.VMEM), out_shape),
        scratch_shapes=scratch,
        compiler_params=pltpu.CompilerParams(vmem_limit_bytes=24 * 1024 * 1024),
        cost_estimate=pl.CostEstimate(flops=flops, bytes_accessed=sent, transcendentals=0),
        name=body.func.__name__,
    )(*operands)


def local(
    mesh,
    pair_state,
    valid_length,
    input_gain,
    left_gate,
    left_value,
    right_gate,
    right_value,
    out_gate,
    output_gain,
    out_weight,
):
    height, width, channels = pair_state.shape
    hidden = left_gate.shape[1]
    s = Sizes(mesh, height, width, channels, hidden)
    shape = jax.ShapeDtypeStruct
    pair = jnp.transpose(pair_state, (1, 0, 2))
    gain = input_gain.reshape(1, channels)
    weights = jnp.concatenate([left_gate, left_value, right_gate, right_value], 1)
    order = ring(s.cols)

    def shift(block, by):
        pairs = [(order[at], order[(at + by) % s.cols]) for at in range(s.cols)]
        return lax.ppermute(block, "col", pairs)

    def swap(block):
        return lax.ppermute(block, "row", [(at, (at + 1) % s.rows) for at in range(s.rows)])

    def run(blocks, sources):
        depth = len(sources) * s.half
        return call(
            functools.partial(project, s, sources),
            [shape((depth, height, hidden), F32), shape((depth, s.slots, hidden), BF16)],
            [pltpu.VMEM((len(sources), s.half, height + TILE, channels), F32)],
            4 * depth * height * channels * hidden,
            valid_length,
            gain,
            weights,
            *blocks,
        )

    starts = (0, s.half)
    sums = shape((width, height, hidden), F32)

    def add(total, terms):
        left, right = terms
        depth = left.shape[0]
        body, before = (add_first, ()) if total is None else (add_more, (total,))
        return call(
            functools.partial(body, s),
            sums,
            [pltpu.VMEM((depth, s.slots, hidden), F32)],
            16 * depth * height * width * hidden,
            left,
            right,
            swap(right),
            *before,
        )

    def whole(distances):
        return [
            (block, at, distance, at) for block, distance in enumerate(distances) for at in starts
        ]

    far = s.cols // 2
    blocks, sources, travel = [pair], whole([0]), [pair, pair]
    total = terms = kept = None
    for distance in range(1, far + 1):
        if distance == far:
            travel = [travel[0][: s.half], travel[1][s.half :]]
        arrived = [shift(block, by) for block, by in zip(travel, (1, -1))]
        pending = run(blocks, sources)
        if distance == 2:
            kept = call(
                functools.partial(gate, s),
                [
                    shape((width, height, channels), F32),
                    shape((1, hidden), F32),
                    shape(out_weight.shape, BF16),
                ],
                [],
                2 * height * width * channels * channels,
                pair,
                gain,
                out_gate,
                output_gain.reshape(1, hidden),
                out_weight,
            )
        if terms is not None:
            total = add(total, terms)
        terms = pending
        done = (terms, total, kept)
        travel = [lax.optimization_barrier((block, done))[0] for block in arrived]
        blocks, sources = arrived, whole([-distance, distance])
    left, right = run(travel, [(0, 0, -far, 0), (1, 0, far, s.half)])
    other = swap(right)
    total = add(total, terms)
    gating, last_gain, last_weight = kept
    update = call(
        functools.partial(finish, s),
        shape((width, height, channels), BF16),
        [pltpu.VMEM(sums.shape, F32), pltpu.VMEM((left.shape[0], s.slots, hidden), F32)],
        16 * width * height * width * hidden,
        left,
        right,
        other,
        total,
        gating,
        last_gain,
        last_weight,
    )
    return jnp.transpose(update, (1, 0, 2))


def solution(mesh):
    return jax.shard_map(
        functools.partial(local, mesh),
        mesh=mesh,
        in_specs=(P(("parts", "row"), "col", None), P("parts")) + (P(),) * 8,
        out_specs=P(("parts", "row"), "col", None),
        check_vma=False,
    )
```

```python
import functools

import jax
import jax.numpy as jnp
from jax import lax
from jax.experimental import pallas as pl
from jax.experimental.pallas import tpu as pltpu
from jax.sharding import PartitionSpec as P

F32 = jnp.float32
BF16 = jnp.bfloat16
EPS = 1e-05
TILE = 16
CHUNK = 56
GROUP = 7


class Sizes:
    def __init__(self, mesh, height, width, channels, hidden):
        self.rows = mesh.shape["row"]
        self.cols = mesh.shape["col"]
        self.height, self.width = height, width
        self.channels, self.hidden = channels, hidden
        self.half = width // 2
        self.slots = -(-width // TILE) * TILE


def column_at(place, cols):
    return jnp.where(place < cols // 2, 2 * place, 2 * (cols - place) - 1)


def place_of(column, cols):
    return jnp.where(column % 2 == 0, column // 2, cols - 1 - column // 2)


def ring(cols):
    return [2 * at if at < cols // 2 else 2 * (cols - at) - 1 for at in range(cols)]


def normalise(values):
    average = jnp.mean(values, -1, keepdims=True)
    centered = values - average
    variance = jnp.mean(centered * centered, -1, keepdims=True)
    return centered * lax.rsqrt(variance + EPS)


def sigmoid(values):
    return 0.5 * jnp.tanh(0.5 * values) + 0.5


def dot(left, right):
    return jnp.dot(left, right, preferred_element_type=F32)


def project(s, sources, length, gain, weight, *refs):
    *blocks, left, right, rows = refs
    row, col = lax.axis_index("row"), lax.axis_index("col")
    limit = length[0]
    offset = (col % (s.height // s.width)) * s.width
    below = lax.broadcasted_iota(jnp.int32, (s.height, 1), 0) + row * s.height < limit
    mine = lax.broadcasted_iota(jnp.int32, (s.slots, 1), 0) + col * s.width < limit
    h = s.hidden
    for index, (block, inside, distance, start) in enumerate(sources):
        place = (place_of(col, s.cols) + distance + s.cols) % s.cols
        token = column_at(place, s.cols) * s.width + start
        normed = []
        for step in range(s.half):
            normed.append(normalise(blocks[block][inside + step].astype(F32)) * gain[...])
            rows[index, step, : s.height] = normed[-1]
        out = dot(jnp.concatenate(normed, 0).astype(BF16), weight[:, : 2 * h])
        value = sigmoid(out[:, :h]) * out[:, h:]
        for step in range(s.half):
            mask = (below & (token + step < limit)).astype(F32)
            left[index * s.half + step] = value[step * s.height : (step + 1) * s.height] * mask
        picked = [rows[index, step, pl.ds(offset, s.slots), :] for step in range(s.half)]
        out = dot(jnp.concatenate(picked, 0).astype(BF16), weight[:, 2 * h :])
        value = sigmoid(out[:, :h]) * out[:, h:]
        for step in range(s.half):
            mask = (mine & (token + step < limit)).astype(F32)
            part = value[step * s.slots : (step + 1) * s.slots] * mask
            right[index * s.half + step] = part.astype(BF16)


def join(left_gate, left_value, right_gate, right_value, weight):
    for at, part in enumerate((left_gate, left_value, right_gate, right_value)):
        weight[:, at * part.shape[1] : (at + 1) * part.shape[1]] = part[...]


def gate(s, pair, gain, out_gate, last_gain, last_weight, gating, kept_gain, kept_weight):
    kept_gain[...] = last_gain[...]
    kept_weight[...] = last_weight[...]
    for start in range(0, s.width, s.half):
        normed = [
            normalise(pair[start + step].astype(F32)) * gain[...] for step in range(s.half)
        ]
        value = sigmoid(dot(jnp.concatenate(normed, 0).astype(BF16), out_gate[...]))
        for step in range(s.half):
            gating[start + step] = value[step * s.height : (step + 1) * s.height]


def accumulate(s, left, right, other, before, total, partner):
    row, col = lax.axis_index("row"), lax.axis_index("col")
    owner = col // (s.height // s.width)
    depth = left.shape[0]

    @pl.when(row == owner)
    def _():
        partner[:depth] = right[...].astype(F32)

    @pl.when(row != owner)
    def _():
        partner[:depth] = other[...].astype(F32)

    size = CHUNK if s.height % CHUNK == 0 else s.height
    group = GROUP if s.width % GROUP == 0 else 1

    def chunk(index, carry):
        at = pl.ds(pl.multiple_of(index * size, 8), size)
        for first in range(0, s.width, group):
            members = range(first, first + group)
            if before is None:
                sums = tuple(jnp.zeros((size, s.hidden), F32) for _ in members)
            else:
                sums = tuple(before[j, at] for j in members)

            def step(k, sums):
                value = left[k, at]
                return tuple(
                    so_far + value * partner[k, j : j + 1] for so_far, j in zip(sums, members)
                )

            sums = lax.fori_loop(0, depth, step, sums, unroll=s.half)
            for so_far, j in zip(sums, members):
                total[j, at] = so_far
        return carry

    lax.fori_loop(0, s.height // size, chunk, 0)


def add_first(s, left, right, other, total, partner):
    accumulate(s, left, right, other, None, total, partner)


def add_more(s, left, right, other, before, total, partner):
    accumulate(s, left, right, other, before, total, partner)


def finish(s, left, right, other, before, gating, gain, weight, update, total, partner):
    accumulate(s, left, right, other, before, total, partner)
    for start in range(0, s.width, s.half):
        settled = [normalise(total[start + step]) * gain[...] for step in range(s.half)]
        value = dot(jnp.concatenate(settled, 0).astype(BF16), weight[...])
        for step in range(s.half):
            part = gating[start + step] * value[step * s.height : (step + 1) * s.height]
            update[start + step] = part.astype(BF16)


def call(body, out_shape, scratch, flops, *operands, grant=24):
    def space(operand):
        return pl.BlockSpec(memory_space=pltpu.SMEM if operand.dtype == jnp.int32 else pltpu.VMEM)

    sent = sum(o.size * o.dtype.itemsize for o in operands)
    return pl.pallas_call(
        body,
        out_shape=out_shape,
        in_specs=[space(o) for o in operands],
        out_specs=jax.tree.map(lambda _: pl.BlockSpec(memory_space=pltpu.VMEM), out_shape),
        scratch_shapes=scratch,
        compiler_params=pltpu.CompilerParams(vmem_limit_bytes=grant * 1024 * 1024),
        cost_estimate=pl.CostEstimate(flops=flops, bytes_accessed=sent, transcendentals=0),
        name=getattr(body, "func", body).__name__,
    )(*operands)


def local(
    mesh,
    pair_state,
    valid_length,
    input_gain,
    left_gate,
    left_value,
    right_gate,
    right_value,
    out_gate,
    output_gain,
    out_weight,
):
    height, width, channels = pair_state.shape
    hidden = left_gate.shape[1]
    s = Sizes(mesh, height, width, channels, hidden)
    shape = jax.ShapeDtypeStruct
    pair = jnp.transpose(pair_state, (1, 0, 2))
    gain = input_gain.reshape(1, channels)
    weights = call(
        join,
        shape((channels, 4 * hidden), BF16),
        [],
        0,
        left_gate,
        left_value,
        right_gate,
        right_value,
        grant=56,
    )
    order = ring(s.cols)

    def shift(block, by):
        pairs = [(order[at], order[(at + by) % s.cols]) for at in range(s.cols)]
        return lax.ppermute(block, "col", pairs)

    def swap(block):
        return lax.ppermute(block, "row", [(at, (at + 1) % s.rows) for at in range(s.rows)])

    def run(blocks, sources):
        depth = len(sources) * s.half
        return call(
            functools.partial(project, s, sources),
            [shape((depth, height, hidden), F32), shape((depth, s.slots, hidden), BF16)],
            [pltpu.VMEM((len(sources), s.half, height + TILE, channels), F32)],
            4 * depth * height * channels * hidden,
            valid_length,
            gain,
            weights,
            *blocks,
        )

    starts = (0, s.half)
    sums = shape((width, height, hidden), F32)

    def add(total, terms):
        left, right = terms
        depth = left.shape[0]
        body, before = (add_first, ()) if total is None else (add_more, (total,))
        return call(
            functools.partial(body, s),
            sums,
            [pltpu.VMEM((depth, s.slots, hidden), F32)],
            16 * depth * height * width * hidden,
            left,
            right,
            swap(right),
            *before,
        )

    def whole(distances):
        return [
            (block, at, distance, at) for block, distance in enumerate(distances) for at in starts
        ]

    far = s.cols // 2
    blocks, sources, travel = [pair], whole([0]), [pair, pair]
    total = kept = last = None
    waiting = []
    for distance in range(1, far):
        arrived = [shift(block, by) for block, by in zip(travel, (1, -1))]
        if distance == far - 1:
            blocks, sources = blocks + [last], sources + [(2, at, far, at) for at in starts]
        waiting.append(run(blocks, sources))
        if distance == 1:
            last = shift(lax.optimization_barrier((pair, waiting[0]))[0], far)
        else:
            if kept is None:
                kept = call(
                    functools.partial(gate, s),
                    [
                        shape((width, height, channels), F32),
                        shape((1, hidden), F32),
                        shape(out_weight.shape, BF16),
                    ],
                    [],
                    2 * height * width * channels * channels,
                    pair,
                    gain,
                    out_gate,
                    output_gain.reshape(1, hidden),
                    out_weight,
                )
            for terms in waiting:
                total = add(total, terms)
            waiting = []
        done = (waiting, total, kept)
        travel = [lax.optimization_barrier((block, done))[0] for block in arrived]
        blocks, sources = travel, whole([-distance, distance])
    for block, way in zip(travel, (1 - far, far - 1)):
        waiting.append(run([block], whole([way])))
    total = add(total, waiting[0])
    left, right = waiting[1]
    gating, last_gain, last_weight = kept
    update = call(
        functools.partial(finish, s),
        shape((width, height, channels), BF16),
        [pltpu.VMEM(sums.shape, F32), pltpu.VMEM((left.shape[0], s.slots, hidden), F32)],
        16 * width * height * width * hidden,
        left,
        right,
        swap(right),
        total,
        gating,
        last_gain,
        last_weight,
    )
    return jnp.transpose(update, (1, 0, 2))


def solution(mesh):
    return jax.shard_map(
        functools.partial(local, mesh),
        mesh=mesh,
        in_specs=(P(("parts", "row"), "col", None), P("parts")) + (P(),) * 8,
        out_specs=P(("parts", "row"), "col", None),
        check_vma=False,
    )
```

```python
import functools

import jax
import jax.numpy as jnp
from jax import lax
from jax.experimental import pallas as pl
from jax.experimental.pallas import tpu as pltpu
from jax.sharding import PartitionSpec as P

F32 = jnp.float32
BF16 = jnp.bfloat16
EPS = 1e-05
TILE = 16
CHUNK = 56
GROUP = 7


class Sizes:
    def __init__(self, mesh, height, width, channels, hidden):
        self.rows = mesh.shape["row"]
        self.cols = mesh.shape["col"]
        self.height, self.width = height, width
        self.channels, self.hidden = channels, hidden
        self.half = width // 2
        self.slots = -(-width // TILE) * TILE


def column_at(place, cols):
    return jnp.where(place < cols // 2, 2 * place, 2 * (cols - place) - 1)


def place_of(column, cols):
    return jnp.where(column % 2 == 0, column // 2, cols - 1 - column // 2)


def ring(cols):
    return [2 * at if at < cols // 2 else 2 * (cols - at) - 1 for at in range(cols)]


def normalise(values):
    average = jnp.mean(values, -1, keepdims=True)
    centered = values - average
    variance = jnp.mean(centered * centered, -1, keepdims=True)
    return centered * lax.rsqrt(variance + EPS)


def sigmoid(values):
    return 0.5 * jnp.tanh(0.5 * values) + 0.5


def dot(left, right):
    return jnp.dot(left, right, preferred_element_type=F32)


def project(s, sources, length, gain, weight, *refs):
    *blocks, left, right, rows = refs
    row, col = lax.axis_index("row"), lax.axis_index("col")
    limit = length[0]
    offset = (col % (s.height // s.width)) * s.width
    below = lax.broadcasted_iota(jnp.int32, (s.height, 1), 0) + row * s.height < limit
    mine = lax.broadcasted_iota(jnp.int32, (s.slots, 1), 0) + col * s.width < limit
    h = s.hidden
    for index, (block, inside, distance, start) in enumerate(sources):
        place = (place_of(col, s.cols) + distance + s.cols) % s.cols
        token = column_at(place, s.cols) * s.width + start
        normed = []
        for step in range(s.half):
            normed.append(normalise(blocks[block][inside + step].astype(F32)) * gain[...])
            rows[index, step, : s.height] = normed[-1]
        out = dot(jnp.concatenate(normed, 0).astype(BF16), weight[:, : 2 * h])
        value = sigmoid(out[:, :h]) * out[:, h:]
        for step in range(s.half):
            mask = (below & (token + step < limit)).astype(F32)
            left[index * s.half + step] = value[step * s.height : (step + 1) * s.height] * mask
        picked = [rows[index, step, pl.ds(offset, s.slots), :] for step in range(s.half)]
        out = dot(jnp.concatenate(picked, 0).astype(BF16), weight[:, 2 * h :])
        value = sigmoid(out[:, :h]) * out[:, h:]
        for step in range(s.half):
            mask = (mine & (token + step < limit)).astype(F32)
            part = value[step * s.slots : (step + 1) * s.slots] * mask
            right[index * s.half + step] = part.astype(BF16)


def gate(s, pair, gain, out_gate, last_gain, last_weight, gating, kept_gain, kept_weight):
    kept_gain[...] = last_gain[...]
    kept_weight[...] = last_weight[...]
    for start in range(0, s.width, s.half):
        normed = [
            normalise(pair[start + step].astype(F32)) * gain[...] for step in range(s.half)
        ]
        value = sigmoid(dot(jnp.concatenate(normed, 0).astype(BF16), out_gate[...]))
        for step in range(s.half):
            gating[start + step] = value[step * s.height : (step + 1) * s.height]


def accumulate(s, left, right, other, before, total, partner):
    row, col = lax.axis_index("row"), lax.axis_index("col")
    owner = col // (s.height // s.width)
    depth = left.shape[0]

    @pl.when(row == owner)
    def _():
        partner[:depth] = right[...].astype(F32)

    @pl.when(row != owner)
    def _():
        partner[:depth] = other[...].astype(F32)

    size = CHUNK if s.height % CHUNK == 0 else s.height
    group = GROUP if s.width % GROUP == 0 else 1

    def chunk(index, carry):
        at = pl.ds(pl.multiple_of(index * size, 8), size)
        for first in range(0, s.width, group):
            members = range(first, first + group)
            if before is None:
                sums = tuple(jnp.zeros((size, s.hidden), F32) for _ in members)
            else:
                sums = tuple(before[j, at] for j in members)

            def step(k, sums):
                value = left[k, at]
                return tuple(
                    so_far + value * partner[k, j : j + 1] for so_far, j in zip(sums, members)
                )

            sums = lax.fori_loop(0, depth, step, sums, unroll=s.half)
            for so_far, j in zip(sums, members):
                total[j, at] = so_far
        return carry

    lax.fori_loop(0, s.height // size, chunk, 0)


def add_first(s, left, right, other, total, partner):
    accumulate(s, left, right, other, None, total, partner)


def add_more(s, left, right, other, before, total, partner):
    accumulate(s, left, right, other, before, total, partner)


def finish(s, left, right, other, before, gating, gain, weight, update, total, partner):
    accumulate(s, left, right, other, before, total, partner)
    for start in range(0, s.width, s.half):
        settled = [normalise(total[start + step]) * gain[...] for step in range(s.half)]
        value = dot(jnp.concatenate(settled, 0).astype(BF16), weight[...])
        for step in range(s.half):
            part = gating[start + step] * value[step * s.height : (step + 1) * s.height]
            update[start + step] = part.astype(BF16)


def call(body, out_shape, scratch, flops, *operands):
    def space(operand):
        return pl.BlockSpec(memory_space=pltpu.SMEM if operand.dtype == jnp.int32 else pltpu.VMEM)

    sent = sum(o.size * o.dtype.itemsize for o in operands)
    return pl.pallas_call(
        body,
        out_shape=out_shape,
        in_specs=[space(o) for o in operands],
        out_specs=jax.tree.map(lambda _: pl.BlockSpec(memory_space=pltpu.VMEM), out_shape),
        scratch_shapes=scratch,
        compiler_params=pltpu.CompilerParams(vmem_limit_bytes=24 * 1024 * 1024),
        cost_estimate=pl.CostEstimate(flops=flops, bytes_accessed=sent, transcendentals=0),
        name=body.func.__name__,
    )(*operands)


def local(
    mesh,
    pair_state,
    valid_length,
    input_gain,
    left_gate,
    left_value,
    right_gate,
    right_value,
    out_gate,
    output_gain,
    out_weight,
):
    height, width, channels = pair_state.shape
    hidden = left_gate.shape[1]
    s = Sizes(mesh, height, width, channels, hidden)
    shape = jax.ShapeDtypeStruct
    pair = jnp.transpose(pair_state, (1, 0, 2))
    gain = input_gain.reshape(1, channels)
    weights = jnp.concatenate([left_gate, left_value, right_gate, right_value], 1)
    order = ring(s.cols)

    def shift(block, by):
        pairs = [(order[at], order[(at + by) % s.cols]) for at in range(s.cols)]
        return lax.ppermute(block, "col", pairs)

    def swap(block):
        return lax.ppermute(block, "row", [(at, (at + 1) % s.rows) for at in range(s.rows)])

    def run(blocks, sources):
        depth = len(sources) * s.half
        return call(
            functools.partial(project, s, sources),
            [shape((depth, height, hidden), F32), shape((depth, s.slots, hidden), BF16)],
            [pltpu.VMEM((len(sources), s.half, height + TILE, channels), F32)],
            4 * depth * height * channels * hidden,
            valid_length,
            gain,
            weights,
            *blocks,
        )

    starts = (0, s.half)
    sums = shape((width, height, hidden), F32)

    def add(total, terms):
        left, right = terms
        depth = left.shape[0]
        body, before = (add_first, ()) if total is None else (add_more, (total,))
        return call(
            functools.partial(body, s),
            sums,
            [pltpu.VMEM((depth, s.slots, hidden), F32)],
            16 * depth * height * width * hidden,
            left,
            right,
            swap(right),
            *before,
        )

    def whole(distances):
        return [
            (block, at, distance, at) for block, distance in enumerate(distances) for at in starts
        ]

    far = s.cols // 2
    blocks, sources, travel = [pair], whole([0]), [pair, pair]
    total = terms = kept = None
    for distance in range(1, far):
        arrived = [shift(block, by) for block, by in zip(travel, (1, -1))]
        if distance == far - 1:
            last = [shift(travel[0][: s.half], 2), shift(travel[1][s.half :], -2)]
        pending = run(blocks, sources)
        if distance == 2:
            kept = call(
                functools.partial(gate, s),
                [
                    shape((width, height, channels), F32),
                    shape((1, hidden), F32),
                    shape(out_weight.shape, BF16),
                ],
                [],
                2 * height * width * channels * channels,
                pair,
                gain,
                out_gate,
                output_gain.reshape(1, hidden),
                out_weight,
            )
        if terms is not None:
            total = add(total, terms)
        terms = pending
        done = (terms, total, kept)
        travel = [lax.optimization_barrier((block, done))[0] for block in arrived]
        blocks, sources = travel, whole([-distance, distance])
    pending = run(blocks, sources)
    total = add(total, terms)
    last, terms, total = lax.optimization_barrier((last, pending, total))
    left, right = run(last, [(0, 0, -far, 0), (1, 0, far, s.half)])
    other = swap(right)
    total = add(total, terms)
    gating, last_gain, last_weight = kept
    update = call(
        functools.partial(finish, s),
        shape((width, height, channels), BF16),
        [pltpu.VMEM(sums.shape, F32), pltpu.VMEM((left.shape[0], s.slots, hidden), F32)],
        16 * width * height * width * hidden,
        left,
        right,
        other,
        total,
        gating,
        last_gain,
        last_weight,
    )
    return jnp.transpose(update, (1, 0, 2))


def solution(mesh):
    return jax.shard_map(
        functools.partial(local, mesh),
        mesh=mesh,
        in_specs=(P(("parts", "row"), "col", None), P("parts")) + (P(),) * 8,
        out_specs=P(("parts", "row"), "col", None),
        check_vma=False,
    )
```

```python
import functools

import jax
import jax.numpy as jnp
from jax import lax
from jax.experimental import pallas as pl
from jax.experimental.pallas import tpu as pltpu
from jax.sharding import PartitionSpec as P

F32 = jnp.float32
BF16 = jnp.bfloat16
EPS = 1e-05
TILE = 16
CHUNK = 56
GROUP = 7


class Sizes:
    def __init__(self, mesh, height, width, channels, hidden):
        self.rows = mesh.shape["row"]
        self.cols = mesh.shape["col"]
        self.height, self.width = height, width
        self.channels, self.hidden = channels, hidden
        self.half = width // 2
        self.slots = -(-width // TILE) * TILE


def column_at(place, cols):
    return jnp.where(place < cols // 2, 2 * place, 2 * (cols - place) - 1)


def place_of(column, cols):
    return jnp.where(column % 2 == 0, column // 2, cols - 1 - column // 2)


def ring(cols):
    return [2 * at if at < cols // 2 else 2 * (cols - at) - 1 for at in range(cols)]


def normalise(values):
    average = jnp.mean(values, -1, keepdims=True)
    centered = values - average
    variance = jnp.mean(centered * centered, -1, keepdims=True)
    return centered * lax.rsqrt(variance + EPS)


def sigmoid(values):
    return 0.5 * jnp.tanh(0.5 * values) + 0.5


def dot(left, right):
    return jnp.dot(left, right, preferred_element_type=F32)


def project(s, sources, length, gain, weight, *refs):
    *blocks, left, right, rows = refs
    row, col = lax.axis_index("row"), lax.axis_index("col")
    limit = length[0]
    offset = (col % (s.height // s.width)) * s.width
    below = lax.broadcasted_iota(jnp.int32, (s.height, 1), 0) + row * s.height < limit
    mine = lax.broadcasted_iota(jnp.int32, (s.slots, 1), 0) + col * s.width < limit
    h = s.hidden
    for index, (block, inside, distance, start) in enumerate(sources):
        place = (place_of(col, s.cols) + distance + s.cols) % s.cols
        token = column_at(place, s.cols) * s.width + start
        normed = []
        for step in range(s.half):
            normed.append(normalise(blocks[block][inside + step].astype(F32)) * gain[...])
            rows[index, step, : s.height] = normed[-1]
        out = dot(jnp.concatenate(normed, 0).astype(BF16), weight[:, : 2 * h])
        value = sigmoid(out[:, :h]) * out[:, h:]
        for step in range(s.half):
            mask = (below & (token + step < limit)).astype(F32)
            left[index * s.half + step] = value[step * s.height : (step + 1) * s.height] * mask
        picked = [rows[index, step, pl.ds(offset, s.slots), :] for step in range(s.half)]
        out = dot(jnp.concatenate(picked, 0).astype(BF16), weight[:, 2 * h :])
        value = sigmoid(out[:, :h]) * out[:, h:]
        for step in range(s.half):
            mask = (mine & (token + step < limit)).astype(F32)
            part = value[step * s.slots : (step + 1) * s.slots] * mask
            right[index * s.half + step] = part.astype(BF16)


def gate(s, pair, gain, out_gate, last_gain, last_weight, gating, kept_gain, kept_weight):
    kept_gain[...] = last_gain[...]
    kept_weight[...] = last_weight[...]
    for start in range(0, s.width, s.half):
        normed = [
            normalise(pair[start + step].astype(F32)) * gain[...] for step in range(s.half)
        ]
        value = sigmoid(dot(jnp.concatenate(normed, 0).astype(BF16), out_gate[...]))
        for step in range(s.half):
            gating[start + step] = value[step * s.height : (step + 1) * s.height]


def accumulate(s, left, partner, before, total):
    depth = left.shape[0]
    size = CHUNK if s.height % CHUNK == 0 else s.height
    group = GROUP if s.width % GROUP == 0 else 1

    def chunk(index, carry):
        at = pl.ds(pl.multiple_of(index * size, 8), size)
        for first in range(0, s.width, group):
            members = range(first, first + group)
            if before is None:
                sums = tuple(jnp.zeros((size, s.hidden), F32) for _ in members)
            else:
                sums = tuple(before[j, at] for j in members)

            def step(k, sums):
                value = left[k, at]
                return tuple(
                    so_far + value * partner[k, j : j + 1] for so_far, j in zip(sums, members)
                )

            sums = lax.fori_loop(0, depth, step, sums, unroll=s.half)
            for so_far, j in zip(sums, members):
                total[j, at] = so_far
        return carry

    lax.fori_loop(0, s.height // size, chunk, 0)


def add_first(s, left, right, other, total, partner):
    row, col = lax.axis_index("row"), lax.axis_index("col")
    choose(row == owner_of(s, col), right, other, partner)
    accumulate(s, left, partner, None, total)


def owner_of(s, col):
    return col // (s.height // s.width)


def choose(first, one, other, target):
    @pl.when(first)
    def _():
        target[...] = one[...].astype(F32)

    @pl.when(jnp.logical_not(first))
    def _():
        target[...] = other[...].astype(F32)


def first_token(s, distance, halved):
    row, col = lax.axis_index("row"), lax.axis_index("col")
    step = distance * (2 * row - 1)
    token = column_at((place_of(col, s.cols) + step + s.cols) % s.cols, s.cols) * s.width
    return token + row * s.half if halved else token


def project_right(s, own, other, token, limit, gain, weight, picked, partner):
    row, col = lax.axis_index("row"), lax.axis_index("col")
    h, depth = s.hidden, own.shape[0]
    choose(row == owner_of(s, col), own, other, picked.at[:, : s.height])
    offset = (col % (s.height // s.width)) * s.width
    mine = lax.broadcasted_iota(jnp.int32, (s.slots, 1), 0) + col * s.width < limit
    for start in range(0, depth, s.half):
        rows = [
            normalise(picked[start + step, pl.ds(offset, s.slots), :]) * gain[...]
            for step in range(s.half)
        ]
        out = dot(jnp.concatenate(rows, 0).astype(BF16), weight[:, 2 * h :])
        value = sigmoid(out[:, :h]) * out[:, h:]
        for step in range(s.half):
            mask = (mine & (token + start + step < limit)).astype(F32)
            partner[start + step] = value[step * s.slots : (step + 1) * s.slots] * mask


def project_left(s, block, row, token, limit, gain, weight, left):
    h = s.hidden
    below = lax.broadcasted_iota(jnp.int32, (s.height, 1), 0) + row * s.height < limit
    for start in range(0, block.shape[0], s.half):
        rows = [
            normalise(block[start + step].astype(F32)) * gain[...] for step in range(s.half)
        ]
        out = dot(jnp.concatenate(rows, 0).astype(BF16), weight[:, : 2 * h])
        value = sigmoid(out[:, :h]) * out[:, h:]
        for step in range(s.half):
            mask = (below & (token + start + step < limit)).astype(F32)
            left[start + step] = value[step * s.height : (step + 1) * s.height] * mask


def add_both(s, distance, length, gain, weight, own, other, *refs):
    before, (mine, theirs, left, right, picked, partner) = refs[:-6], refs[-6:]
    row, limit = lax.axis_index("row"), length[0]
    token = first_token(s, distance, False)
    project_right(s, own, other, token, limit, gain, weight, picked, partner)
    project_left(s, own, row, token, limit, gain, weight, left)
    project_left(s, other, 1 - row, token, limit, gain, weight, right)
    accumulate(s, left, partner, before[0], mine)
    accumulate(s, right, partner, before[1] if len(before) > 1 else None, theirs)


def add_theirs(s, distance, length, gain, weight, own, other, before, theirs, partner, left, picked, total):
    row, limit = lax.axis_index("row"), length[0]
    token = first_token(s, distance, True)
    project_right(s, own, other, token, limit, gain, weight, picked, partner)
    project_left(s, other, 1 - row, token, limit, gain, weight, left)
    accumulate(s, left, partner, before, total)
    theirs[...] = total[...].astype(BF16)


def add_mine(s, distance, length, gain, weight, own, before, partner, mine, left):
    token = first_token(s, distance, True)
    project_left(s, own, lax.axis_index("row"), token, length[0], gain, weight, left)
    accumulate(s, left, partner, before, mine)


def finish(s, mine, given, gating, gain, weight, update):
    for start in range(0, s.width, s.half):
        settled = [
            normalise(mine[start + step] + given[start + step].astype(F32)) * gain[...]
            for step in range(s.half)
        ]
        value = dot(jnp.concatenate(settled, 0).astype(BF16), weight[...])
        for step in range(s.half):
            part = gating[start + step] * value[step * s.height : (step + 1) * s.height]
            update[start + step] = part.astype(BF16)


def call(body, out_shape, scratch, flops, *operands):
    def space(operand):
        return pl.BlockSpec(memory_space=pltpu.SMEM if operand.dtype == jnp.int32 else pltpu.VMEM)

    sent = sum(o.size * o.dtype.itemsize for o in operands)
    return pl.pallas_call(
        body,
        out_shape=out_shape,
        in_specs=[space(o) for o in operands],
        out_specs=jax.tree.map(lambda _: pl.BlockSpec(memory_space=pltpu.VMEM), out_shape),
        scratch_shapes=scratch,
        compiler_params=pltpu.CompilerParams(vmem_limit_bytes=24 * 1024 * 1024),
        cost_estimate=pl.CostEstimate(flops=flops, bytes_accessed=sent, transcendentals=0),
        name=body.func.__name__,
    )(*operands)


def local(
    mesh,
    pair_state,
    valid_length,
    input_gain,
    left_gate,
    left_value,
    right_gate,
    right_value,
    out_gate,
    output_gain,
    out_weight,
):
    height, width, channels = pair_state.shape
    hidden = left_gate.shape[1]
    s = Sizes(mesh, height, width, channels, hidden)
    shape = jax.ShapeDtypeStruct
    pair = jnp.transpose(pair_state, (1, 0, 2))
    gain = input_gain.reshape(1, channels)
    weights = jnp.concatenate([left_gate, left_value, right_gate, right_value], 1)
    order = ring(s.cols)

    def shift(block, crossed=False):
        pairs = []
        for row in range(s.rows):
            target = s.rows - 1 - row if crossed else row
            for at in range(s.cols):
                to = (at + 1 - 2 * target) % s.cols
                pairs.append((row * s.cols + order[at], target * s.cols + order[to]))
        return lax.ppermute(block, ("row", "col"), pairs)

    def swap(block):
        return lax.ppermute(block, "row", [(at, (at + 1) % s.rows) for at in range(s.rows)])

    def run(blocks, sources):
        depth = len(sources) * s.half
        return call(
            functools.partial(project, s, sources),
            [shape((depth, height, hidden), F32), shape((depth, s.slots, hidden), BF16)],
            [pltpu.VMEM((len(sources), s.half, height + TILE, channels), F32)],
            4 * depth * height * channels * hidden,
            valid_length,
            gain,
            weights,
            *blocks,
        )

    starts = (0, s.half)
    sums = shape((width, height, hidden), F32)
    last_row = output_gain.reshape(1, hidden)
    product = 16 * height * width * hidden

    def tokens(depth):
        return pltpu.VMEM((depth, height, hidden), F32)

    def picked(depth):
        return pltpu.VMEM((depth, height + TILE, channels), F32)

    def right(depth):
        return shape((depth, s.slots, hidden), F32)

    def held(depth):
        return pltpu.VMEM(right(depth).shape, F32)

    far = s.cols // 2
    left, partner = run([pair], [(0, at, 0, at) for at in starts])
    own, other = shift(pair), shift(pair, crossed=True)
    given = swap(partner)
    done = (left, partner)
    total = kept = None
    for distance in range(1, far):
        own, other = [lax.optimization_barrier((block, done))[0] for block in (own, other)]
        if distance < far - 1:
            ahead = [shift(own), shift(other)]
        else:
            start = lax.axis_index("row") * s.half
            ahead = [
                shift(lax.dynamic_slice_in_dim(block, start, s.half, 0)) for block in (own, other)
            ]
            kept = call(
                functools.partial(gate, s),
                [shape(sums.shape, F32), shape((1, hidden), F32), shape(out_weight.shape, BF16)],
                [],
                2 * height * width * channels * channels,
                pair,
                gain,
                out_gate,
                last_row,
                out_weight,
            )
        if total is None:
            total = [
                call(
                    functools.partial(add_first, s),
                    sums,
                    [held(width)],
                    width * product,
                    left,
                    partner,
                    given,
                )
            ]
        total = call(
            functools.partial(add_both, s, distance),
            [sums, sums],
            [tokens(width), tokens(width), picked(width), held(width)],
            2 * width * product,
            valid_length,
            gain,
            weights,
            own,
            other,
            *total,
        )
        done = (total, kept)
        own, other = ahead
    own, other, done = lax.optimization_barrier((own, other, done))
    (mine, theirs), (gating, last_gain, last_weight) = done
    theirs, partner = call(
        functools.partial(add_theirs, s, far),
        [shape(sums.shape, BF16), right(s.half)],
        [tokens(s.half), picked(s.half), pltpu.VMEM(sums.shape, F32)],
        s.half * product,
        valid_length,
        gain,
        weights,
        own,
        other,
        theirs,
    )
    given = swap(theirs)
    mine = call(
        functools.partial(add_mine, s, far),
        sums,
        [tokens(s.half)],
        s.half * product,
        valid_length,
        gain,
        weights,
        own,
        mine,
        partner,
    )
    update = call(
        functools.partial(finish, s),
        shape((width, height, channels), BF16),
        [],
        2 * height * width * channels * hidden,
        mine,
        given,
        gating,
        last_gain,
        last_weight,
    )
    return jnp.transpose(update, (1, 0, 2))


def solution(mesh):
    return jax.shard_map(
        functools.partial(local, mesh),
        mesh=mesh,
        in_specs=(P(("parts", "row"), "col", None), P("parts")) + (P(),) * 8,
        out_specs=P(("parts", "row"), "col", None),
        check_vma=False,
    )
```

```python
import functools

import jax
import jax.numpy as jnp
from jax import lax
from jax.experimental import pallas as pl
from jax.experimental.pallas import tpu as pltpu
from jax.sharding import PartitionSpec as P

F32 = jnp.float32
BF16 = jnp.bfloat16
EPS = 1e-05
TILE = 16
CHUNK = 56
GROUP = 7


class Sizes:
    def __init__(self, mesh, height, width, channels, hidden):
        self.rows = mesh.shape["row"]
        self.cols = mesh.shape["col"]
        self.height, self.width = height, width
        self.channels, self.hidden = channels, hidden
        self.half = width // 2
        self.slots = -(-width // TILE) * TILE


def column_at(place, cols):
    return jnp.where(place < cols // 2, 2 * place, 2 * (cols - place) - 1)


def place_of(column, cols):
    return jnp.where(column % 2 == 0, column // 2, cols - 1 - column // 2)


def ring(cols):
    return [2 * at if at < cols // 2 else 2 * (cols - at) - 1 for at in range(cols)]


def normalise(values):
    average = jnp.mean(values, -1, keepdims=True)
    centered = values - average
    variance = jnp.mean(centered * centered, -1, keepdims=True)
    return centered * lax.rsqrt(variance + EPS)


def sigmoid(values):
    return 0.5 * jnp.tanh(0.5 * values) + 0.5


def dot(left, right):
    return jnp.dot(left, right, preferred_element_type=F32)


def project(s, sources, length, gain, weight, *refs):
    *blocks, left, right, rows = refs
    row, col = lax.axis_index("row"), lax.axis_index("col")
    limit = length[0]
    offset = (col % (s.height // s.width)) * s.width
    below = lax.broadcasted_iota(jnp.int32, (s.height, 1), 0) + row * s.height < limit
    mine = lax.broadcasted_iota(jnp.int32, (s.slots, 1), 0) + col * s.width < limit
    h = s.hidden
    for index, (block, inside, distance, start) in enumerate(sources):
        place = (place_of(col, s.cols) + distance * (2 * row - 1) + s.cols) % s.cols
        token = column_at(place, s.cols) * s.width + start
        normed = []
        for step in range(s.half):
            normed.append(normalise(blocks[block][inside + step].astype(F32)) * gain[...])
            rows[index, step, : s.height] = normed[-1]
        out = dot(jnp.concatenate(normed, 0).astype(BF16), weight[:, : 2 * h])
        value = sigmoid(out[:, :h]) * out[:, h:]
        for step in range(s.half):
            mask = (below & (token + step < limit)).astype(F32)
            left[index * s.half + step] = value[step * s.height : (step + 1) * s.height] * mask
        picked = [rows[index, step, pl.ds(offset, s.slots), :] for step in range(s.half)]
        out = dot(jnp.concatenate(picked, 0).astype(BF16), weight[:, 2 * h :])
        value = sigmoid(out[:, :h]) * out[:, h:]
        for step in range(s.half):
            mask = (mine & (token + step < limit)).astype(F32)
            part = value[step * s.slots : (step + 1) * s.slots] * mask
            right[index * s.half + step] = part.astype(BF16)


def gate(s, pair, gain, out_gate, last_gain, last_weight, gating, kept_gain, kept_weight):
    kept_gain[...] = last_gain[...]
    kept_weight[...] = last_weight[...]
    for start in range(0, s.width, s.half):
        normed = [
            normalise(pair[start + step].astype(F32)) * gain[...] for step in range(s.half)
        ]
        value = sigmoid(dot(jnp.concatenate(normed, 0).astype(BF16), out_gate[...]))
        for step in range(s.half):
            gating[start + step] = value[step * s.height : (step + 1) * s.height]


def accumulate(s, left, right, other, before, total, partner):
    row, col = lax.axis_index("row"), lax.axis_index("col")
    owner = col // (s.height // s.width)
    depth = left.shape[0]

    @pl.when(row == owner)
    def _():
        partner[:depth] = right[...].astype(F32)

    @pl.when(row != owner)
    def _():
        for start in range(0, depth, s.width):
            there = depth - s.width - start
            partner[start : start + s.width] = other[there : there + s.width].astype(F32)

    size = CHUNK if s.height % CHUNK == 0 else s.height
    group = GROUP if s.width % GROUP == 0 else 1

    def chunk(index, carry):
        at = pl.ds(pl.multiple_of(index * size, 8), size)
        for first in range(0, s.width, group):
            members = range(first, first + group)
            if before is None:
                sums = tuple(jnp.zeros((size, s.hidden), F32) for _ in members)
            else:
                sums = tuple(before[j, at] for j in members)

            def step(k, sums):
                value = left[k, at]
                return tuple(
                    so_far + value * partner[k, j : j + 1] for so_far, j in zip(sums, members)
                )

            sums = lax.fori_loop(0, depth, step, sums, unroll=s.half)
            for so_far, j in zip(sums, members):
                total[j, at] = so_far
        return carry

    lax.fori_loop(0, s.height // size, chunk, 0)


def add_first(s, left, right, other, total, partner):
    accumulate(s, left, right, other, None, total, partner)


def add_more(s, left, right, other, before, total, partner):
    accumulate(s, left, right, other, before, total, partner)


def finish(s, left, right, other, before, gating, gain, weight, update, total, partner):
    accumulate(s, left, right, other, before, total, partner)
    for start in range(0, s.width, s.half):
        settled = [normalise(total[start + step]) * gain[...] for step in range(s.half)]
        value = dot(jnp.concatenate(settled, 0).astype(BF16), weight[...])
        for step in range(s.half):
            part = gating[start + step] * value[step * s.height : (step + 1) * s.height]
            update[start + step] = part.astype(BF16)


def call(body, out_shape, scratch, flops, *operands):
    def space(operand):
        return pl.BlockSpec(memory_space=pltpu.SMEM if operand.dtype == jnp.int32 else pltpu.VMEM)

    sent = sum(o.size * o.dtype.itemsize for o in operands)
    return pl.pallas_call(
        body,
        out_shape=out_shape,
        in_specs=[space(o) for o in operands],
        out_specs=jax.tree.map(lambda _: pl.BlockSpec(memory_space=pltpu.VMEM), out_shape),
        scratch_shapes=scratch,
        compiler_params=pltpu.CompilerParams(vmem_limit_bytes=24 * 1024 * 1024),
        cost_estimate=pl.CostEstimate(flops=flops, bytes_accessed=sent, transcendentals=0),
        name=body.func.__name__,
    )(*operands)


def local(
    mesh,
    pair_state,
    valid_length,
    input_gain,
    left_gate,
    left_value,
    right_gate,
    right_value,
    out_gate,
    output_gain,
    out_weight,
):
    height, width, channels = pair_state.shape
    hidden = left_gate.shape[1]
    s = Sizes(mesh, height, width, channels, hidden)
    shape = jax.ShapeDtypeStruct
    pair = jnp.transpose(pair_state, (1, 0, 2))
    gain = input_gain.reshape(1, channels)
    weights = jnp.concatenate([left_gate, left_value, right_gate, right_value], 1)
    order = ring(s.cols)

    def shift(block, way):
        pairs = []
        for row in range(s.rows):
            by = way if row == 0 else -way
            for at in range(s.cols):
                to = order[(at + by) % s.cols]
                pairs.append((row * s.cols + order[at], row * s.cols + to))
        return lax.ppermute(block, ("row", "col"), pairs)

    def swap(block):
        return lax.ppermute(block, "row", [(at, (at + 1) % s.rows) for at in range(s.rows)])

    def run(blocks, sources):
        depth = len(sources) * s.half
        return call(
            functools.partial(project, s, sources),
            [shape((depth, height, hidden), F32), shape((depth, s.slots, hidden), BF16)],
            [pltpu.VMEM((len(sources), s.half, height + TILE, channels), F32)],
            4 * depth * height * channels * hidden,
            valid_length,
            gain,
            weights,
            *blocks,
        )

    starts = (0, s.half)
    sums = shape((width, height, hidden), F32)

    def add(total, terms):
        left, right = terms
        depth = left.shape[0]
        body, before = (add_first, ()) if total is None else (add_more, (total,))
        return call(
            functools.partial(body, s),
            sums,
            [pltpu.VMEM((depth, s.slots, hidden), F32)],
            16 * depth * height * width * hidden,
            left,
            right,
            swap(right),
            *before,
        )

    def whole(distances):
        return [
            (block, at, distance, at) for block, distance in enumerate(distances) for at in starts
        ]

    far = s.cols // 2
    blocks, sources, travel = [pair], whole([0]), [pair, pair]
    total = terms = kept = None
    for distance in range(1, far + 1):
        ways = (1, -1) if distance < far else (1,)
        arrived = [shift(block, way) for block, way in zip(travel, ways)]
        pending = run(blocks, sources)
        if distance == 2:
            kept = call(
                functools.partial(gate, s),
                [
                    shape((width, height, channels), F32),
                    shape((1, hidden), F32),
                    shape(out_weight.shape, BF16),
                ],
                [],
                2 * height * width * channels * channels,
                pair,
                gain,
                out_gate,
                output_gain.reshape(1, hidden),
                out_weight,
            )
        if terms is not None:
            total = add(total, terms)
        terms = pending
        done = (terms, total, kept)
        travel = [lax.optimization_barrier((block, done))[0] for block in arrived]
        blocks, sources = travel, whole([distance, -distance])
    left, right = run(travel, whole([far]))
    other = swap(right)
    total = add(total, terms)
    gating, last_gain, last_weight = kept
    update = call(
        functools.partial(finish, s),
        shape((width, height, channels), BF16),
        [pltpu.VMEM(sums.shape, F32), pltpu.VMEM((left.shape[0], s.slots, hidden), F32)],
        16 * width * height * width * hidden,
        left,
        right,
        other,
        total,
        gating,
        last_gain,
        last_weight,
    )
    return jnp.transpose(update, (1, 0, 2))


def solution(mesh):
    return jax.shard_map(
        functools.partial(local, mesh),
        mesh=mesh,
        in_specs=(P(("parts", "row"), "col", None), P("parts")) + (P(),) * 8,
        out_specs=P(("parts", "row"), "col", None),
        check_vma=False,
    )
```

```python
import functools

import jax
import jax.numpy as jnp
from jax import lax
from jax.experimental import pallas as pl
from jax.experimental.pallas import tpu as pltpu
from jax.sharding import PartitionSpec as P

F32 = jnp.float32
BF16 = jnp.bfloat16
EPS = 1e-05
TILE = 16
CHUNK = 56
GROUP = 7


class Sizes:
    def __init__(self, mesh, height, width, channels, hidden):
        self.rows = mesh.shape["row"]
        self.cols = mesh.shape["col"]
        self.height, self.width = height, width
        self.channels, self.hidden = channels, hidden
        self.half = width // 2
        self.slots = -(-width // TILE) * TILE


def column_at(place, cols):
    return jnp.where(place < cols // 2, 2 * place, 2 * (cols - place) - 1)


def place_of(column, cols):
    return jnp.where(column % 2 == 0, column // 2, cols - 1 - column // 2)


def ring(cols):
    return [2 * at if at < cols // 2 else 2 * (cols - at) - 1 for at in range(cols)]


def normalise(values):
    average = jnp.mean(values, -1, keepdims=True)
    centered = values - average
    variance = jnp.mean(centered * centered, -1, keepdims=True)
    return centered * lax.rsqrt(variance + EPS)


def sigmoid(values):
    return 0.5 * jnp.tanh(0.5 * values) + 0.5


def dot(left, right):
    return jnp.dot(left, right, preferred_element_type=F32)


def gate(s, pair, gain, out_gate, last_gain, last_weight, gating, kept_gain, kept_weight):
    kept_gain[...] = last_gain[...]
    kept_weight[...] = last_weight[...]
    for start in range(0, s.width, s.half):
        normed = [
            normalise(pair[start + step].astype(F32)) * gain[...] for step in range(s.half)
        ]
        value = sigmoid(dot(jnp.concatenate(normed, 0).astype(BF16), out_gate[...]))
        for step in range(s.half):
            gating[start + step] = value[step * s.height : (step + 1) * s.height]


def accumulate(s, left, partner, before, total):
    depth = left.shape[0]
    size = CHUNK if s.height % CHUNK == 0 else s.height
    group = GROUP if s.width % GROUP == 0 else 1

    def chunk(index, carry):
        at = pl.ds(pl.multiple_of(index * size, 8), size)
        for first in range(0, s.width, group):
            members = range(first, first + group)
            if before is None:
                sums = tuple(jnp.zeros((size, s.hidden), F32) for _ in members)
            else:
                sums = tuple(before[j, at] for j in members)

            def step(k, sums):
                value = left[k, at]
                return tuple(
                    so_far + value * partner[k, j : j + 1] for so_far, j in zip(sums, members)
                )

            sums = lax.fori_loop(0, depth, step, sums, unroll=s.half)
            for so_far, j in zip(sums, members):
                total[j, at] = so_far
        return carry

    lax.fori_loop(0, s.height // size, chunk, 0)


def owner_of(s, col):
    return col // (s.height // s.width)


def choose(first, one, other, target):
    @pl.when(first)
    def _():
        target[...] = one[...].astype(F32)

    @pl.when(jnp.logical_not(first))
    def _():
        target[...] = other[...].astype(F32)


def offset_in(s, col):
    return (col % (s.height // s.width)) * s.width


def column_from(s, distance):
    row, col = lax.axis_index("row"), lax.axis_index("col")
    step = distance * (2 * row - 1)
    return column_at((place_of(col, s.cols) + step + s.cols) % s.cols, s.cols)


def gated(s, rows, gain, weight, masks):
    h, size = s.hidden, rows[0].shape[0]
    rows = [normalise(row) * gain[...] for row in rows]
    out = dot(jnp.concatenate(rows, 0).astype(BF16), weight)
    value = sigmoid(out[:, :h]) * out[:, h:]
    return [value[at * size : (at + 1) * size] * mask for at, mask in enumerate(masks)]


def project_right(s, rows_of, base, depth, token, limit, gain, weight, partner):
    first = lax.axis_index("col") * s.width
    mine = lax.broadcasted_iota(jnp.int32, (s.slots, 1), 0) + first < limit
    for start in range(0, depth, s.half):
        steps = range(start, start + s.half)
        masks = [(mine & (token + step < limit)).astype(F32) for step in steps]
        rows = [rows_of(base + step) for step in steps]
        for step, part in zip(steps, gated(s, rows, gain, weight[:, 2 * s.hidden :], masks)):
            partner[step] = part


def project_left(s, block, row, base, depth, token, limit, gain, weight, left):
    below = lax.broadcasted_iota(jnp.int32, (s.height, 1), 0) + row * s.height < limit
    for start in range(0, depth, s.half):
        steps = range(start, start + s.half)
        masks = [(below & (token + step < limit)).astype(F32) for step in steps]
        rows = [block[base + step].astype(F32) for step in steps]
        for step, part in zip(steps, gated(s, rows, gain, weight[:, : 2 * s.hidden], masks)):
            left[step] = part


def add_both(s, distance, narrow, length, gain, weight, own, other, *refs):
    before, (mine, theirs, left, right, picked, partner) = refs[:-6], refs[-6:]
    row, col, limit = lax.axis_index("row"), lax.axis_index("col"), length[0]
    depth = left.shape[0]
    base = row * s.half if distance == 0 else 0
    token = column_from(s, distance) * s.width + base
    choose(row == owner_of(s, col), own, other, picked.at[:, : s.height])

    def rows_of(at):
        return picked[at, pl.ds(offset_in(s, col), s.slots), :]

    project_right(s, rows_of, base, depth, token, limit, gain, weight, partner)
    project_left(s, own, row, base, depth, token, limit, gain, weight, left)
    project_left(s, other, 1 - row, base, depth, token, limit, gain, weight, right)
    old_mine, old_theirs = before if before else (None, None)
    accumulate(s, left, partner, old_mine, mine)
    if not narrow:
        accumulate(s, right, partner, old_theirs, theirs)
    else:
        accumulate(s, right, partner, old_theirs, picked)
        theirs[...] = picked[:, : s.height].astype(BF16)


def pick(s, own, other, rows, picked):
    col = column_from(s, -2)
    choose(lax.axis_index("row") == owner_of(s, col), own, other, picked.at[:, : s.height])
    for step in range(s.width):
        rows[step] = picked[step, pl.ds(offset_in(s, col), s.slots), :].astype(BF16)


def finish(s, length, gain, weight, own, rows, mine, given, gating, last_gain, last_weight, *refs):
    update, left, partner, total = refs
    token = column_from(s, s.cols // 2) * s.width
    limit, row = length[0], lax.axis_index("row")
    project_right(
        s, lambda at: rows[at].astype(F32), 0, s.width, token, limit, gain, weight, partner
    )
    project_left(s, own, row, 0, s.width, token, limit, gain, weight, left)
    accumulate(s, left, partner, mine, total)
    for start in range(0, s.width, s.half):
        settled = [
            normalise(total[start + step] + given[start + step].astype(F32)) * last_gain[...]
            for step in range(s.half)
        ]
        value = dot(jnp.concatenate(settled, 0).astype(BF16), last_weight[...])
        for step in range(s.half):
            part = gating[start + step] * value[step * s.height : (step + 1) * s.height]
            update[start + step] = part.astype(BF16)


def call(body, out_shape, scratch, flops, *operands):
    def space(operand):
        return pl.BlockSpec(memory_space=pltpu.SMEM if operand.dtype == jnp.int32 else pltpu.VMEM)

    sent = sum(o.size * o.dtype.itemsize for o in operands)
    return pl.pallas_call(
        body,
        out_shape=out_shape,
        in_specs=[space(o) for o in operands],
        out_specs=jax.tree.map(lambda _: pl.BlockSpec(memory_space=pltpu.VMEM), out_shape),
        scratch_shapes=scratch,
        compiler_params=pltpu.CompilerParams(vmem_limit_bytes=24 * 1024 * 1024),
        cost_estimate=pl.CostEstimate(flops=flops, bytes_accessed=sent, transcendentals=0),
        name=body.func.__name__,
    )(*operands)


def local(
    mesh,
    pair_state,
    valid_length,
    input_gain,
    left_gate,
    left_value,
    right_gate,
    right_value,
    out_gate,
    output_gain,
    out_weight,
):
    height, width, channels = pair_state.shape
    hidden = left_gate.shape[1]
    s = Sizes(mesh, height, width, channels, hidden)
    shape = jax.ShapeDtypeStruct
    pair = jnp.transpose(pair_state, (1, 0, 2))
    gain = input_gain.reshape(1, channels)
    weights = jnp.concatenate([left_gate, left_value, right_gate, right_value], 1)
    order = ring(s.cols)

    def shift(block, crossed=False, by=1):
        pairs = []
        for row in range(s.rows):
            target = s.rows - 1 - row if crossed else row
            for at in range(s.cols):
                to = (at + by * (1 - 2 * target)) % s.cols
                pairs.append((row * s.cols + order[at], target * s.cols + order[to]))
        return lax.ppermute(block, ("row", "col"), pairs)

    def swap(block):
        return lax.ppermute(block, "row", [(at, (at + 1) % s.rows) for at in range(s.rows)])

    sums = shape((width, height, hidden), F32)
    common = (valid_length, gain, weights)
    product = 16 * height * width * hidden
    tokens = pltpu.VMEM((width, height, hidden), F32)
    halved = pltpu.VMEM((s.half, height, hidden), F32)
    padded = pltpu.VMEM((width, height + TILE, channels), F32)
    partner = pltpu.VMEM((width, s.slots, hidden), F32)
    few = pltpu.VMEM((s.half, s.slots, hidden), F32)

    def add(distance, own, other, before, narrow=False):
        left, right = (halved, few) if distance == 0 else (tokens, partner)
        return call(
            functools.partial(add_both, s, distance, narrow),
            [sums, shape(sums.shape, BF16) if narrow else sums],
            [left, left, padded, right],
            2 * left.shape[0] * product,
            *common,
            own,
            other,
            *before,
        )

    def in_turn(other, own, done):
        own = lax.optimization_barrier((own, done))[0]
        return lax.optimization_barrier((other, own))[0], own

    far = s.cols // 2
    other = shift(pair, crossed=True)
    own = shift(pair)
    total = add(0, pair, swap(pair), ())
    other, own = in_turn(other, own, weights)
    rows = ()
    for distance in range(1, far - 1):
        ahead = [shift(other), shift(own)]
        if distance == far - 2:
            rows = call(
                functools.partial(pick, s),
                shape((width, s.slots, channels), BF16),
                [padded],
                0,
                own,
                other,
            )
            rows = shift(rows, by=2)
        total = add(distance, own, other, total)
        done = (total, rows)
        other, own = in_turn(*ahead, done)
    last = shift(own)
    gating = call(
        functools.partial(gate, s),
        [sums, shape((1, hidden), F32), shape(out_weight.shape, BF16)],
        [],
        2 * height * width * channels * channels,
        pair,
        gain,
        out_gate,
        output_gain.reshape(1, hidden),
        out_weight,
    )
    mine, theirs = add(far - 1, own, other, total, narrow=True)
    given = swap(theirs)
    last, mine, gating = lax.optimization_barrier((last, mine, gating))
    update = call(
        functools.partial(finish, s),
        shape((width, height, channels), BF16),
        [tokens, partner, pltpu.VMEM(sums.shape, F32)],
        width * product,
        *common,
        last,
        rows,
        mine,
        given,
        *gating,
    )
    return jnp.transpose(update, (1, 0, 2))


def solution(mesh):
    return jax.shard_map(
        functools.partial(local, mesh),
        mesh=mesh,
        in_specs=(P(("parts", "row"), "col", None), P("parts")) + (P(),) * 8,
        out_specs=P(("parts", "row"), "col", None),
        check_vma=False,
    )
```

```python
import functools

import jax
import jax.numpy as jnp
from jax import lax
from jax.experimental import pallas as pl
from jax.experimental.pallas import tpu as pltpu
from jax.sharding import PartitionSpec as P

F32 = jnp.float32
BF16 = jnp.bfloat16
EPS = 1e-05
TILE = 16
CHUNK = 56
GROUP = 7


class Sizes:
    def __init__(self, mesh, height, width, channels, hidden):
        self.rows = mesh.shape["row"]
        self.cols = mesh.shape["col"]
        self.height, self.width = height, width
        self.channels, self.hidden = channels, hidden
        self.half = width // 2
        self.slots = -(-width // TILE) * TILE


def column_at(place, cols):
    return jnp.where(place < cols // 2, 2 * place, 2 * (cols - place) - 1)


def place_of(column, cols):
    return jnp.where(column % 2 == 0, column // 2, cols - 1 - column // 2)


def ring(cols):
    return [2 * at if at < cols // 2 else 2 * (cols - at) - 1 for at in range(cols)]


def normalise(values):
    average = jnp.mean(values, -1, keepdims=True)
    centered = values - average
    variance = jnp.mean(centered * centered, -1, keepdims=True)
    return centered * lax.rsqrt(variance + EPS)


def sigmoid(values):
    return 0.5 * jnp.tanh(0.5 * values) + 0.5


def dot(left, right):
    return jnp.dot(left, right, preferred_element_type=F32)


def gate(s, pair, shared, out_gate, last_gain, last_weight, gating, kept_gain, kept_weight):
    gain = Shared(s, shared).gain
    kept_gain[...] = last_gain[...]
    kept_weight[...] = last_weight[...]
    for start in range(0, s.width, s.half):
        normed = [
            normalise(pair[start + step].astype(F32)) * gain for step in range(s.half)
        ]
        value = sigmoid(dot(jnp.concatenate(normed, 0).astype(BF16), out_gate[...]))
        for step in range(s.half):
            gating[start + step] = value[step * s.height : (step + 1) * s.height]


def accumulate(s, left, partner, before, total):
    depth = left.shape[0]
    size = CHUNK if s.height % CHUNK == 0 else s.height
    group = GROUP if s.width % GROUP == 0 else 1

    def chunk(index, carry):
        at = pl.ds(pl.multiple_of(index * size, 8), size)
        for first in range(0, s.width, group):
            members = range(first, first + group)
            if before is None:
                sums = tuple(jnp.zeros((size, s.hidden), F32) for _ in members)
            else:
                sums = tuple(before[j, at] for j in members)

            def step(k, sums):
                value = left[k, at]
                return tuple(
                    so_far + value * partner[k, j : j + 1] for so_far, j in zip(sums, members)
                )

            sums = lax.fori_loop(0, depth, step, sums, unroll=s.half)
            for so_far, j in zip(sums, members):
                total[j, at] = so_far
        return carry

    lax.fori_loop(0, s.height // size, chunk, 0)


def owner_of(s, col):
    return col // (s.height // s.width)


def choose(first, one, other, target):
    @pl.when(first)
    def _():
        target[...] = one[...].astype(F32)

    @pl.when(jnp.logical_not(first))
    def _():
        target[...] = other[...].astype(F32)


def offset_in(s, col):
    return (col % (s.height // s.width)) * s.width


def column_from(s, distance):
    row, col = lax.axis_index("row"), lax.axis_index("col")
    step = distance * (2 * row - 1)
    return column_at((place_of(col, s.cols) + step + s.cols) % s.cols, s.cols)


class Shared:
    def __init__(self, s, ref):
        h = s.hidden
        self.left = ref[: s.channels, : 2 * h].astype(BF16)
        self.right = ref[: s.channels, 2 * h :].astype(BF16)
        self.gain = ref[s.channels : s.channels + 1, : s.channels]
        self.limit = ref[s.channels + 1 : s.channels + 2, :1].astype(jnp.int32)


def join(s, length, gain, left_gate, left_value, right_gate, right_value, shared):
    h = s.hidden
    for at, part in enumerate((left_gate, left_value, right_gate, right_value)):
        shared[: s.channels, at * h : (at + 1) * h] = part[...].astype(F32)
    shared[s.channels : s.channels + 1, : s.channels] = gain[...]
    shared[s.channels + 1 : s.channels + 2, :] = jnp.full((1, 4 * h), length[0]).astype(F32)


def gated(s, rows, gain, weight, masks):
    h, size = s.hidden, rows[0].shape[0]
    rows = [normalise(row) * gain for row in rows]
    out = dot(jnp.concatenate(rows, 0).astype(BF16), weight)
    value = sigmoid(out[:, :h]) * out[:, h:]
    return [value[at * size : (at + 1) * size] * mask for at, mask in enumerate(masks)]


def masks_of(tokens, first, count, limit):
    below = (lax.broadcasted_iota(jnp.int32, (count, 1), 0) + first < limit).astype(F32)
    return [below * (token < limit).astype(F32) for token in tokens]


def project_right(s, rows_of, base, depth, token, shared, partner):
    first = lax.axis_index("col") * s.width
    for start in range(0, depth, s.half):
        steps = range(start, start + s.half)
        masks = masks_of([token + step for step in steps], first, s.slots, shared.limit)
        rows = [rows_of(base + step) for step in steps]
        for step, part in zip(steps, gated(s, rows, shared.gain, shared.right, masks)):
            partner[step] = part


def project_left(s, block, row, base, depth, token, shared, left):
    first = row * s.height
    for start in range(0, depth, s.half):
        steps = range(start, start + s.half)
        masks = masks_of([token + step for step in steps], first, s.height, shared.limit)
        rows = [block[base + step].astype(F32) for step in steps]
        for step, part in zip(steps, gated(s, rows, shared.gain, shared.left, masks)):
            left[step] = part


def add_both(s, distance, narrow, shared, own, other, *refs):
    before, (mine, theirs, left, right, picked, partner) = refs[:-6], refs[-6:]
    row, col = lax.axis_index("row"), lax.axis_index("col")
    shared = Shared(s, shared)
    depth = left.shape[0]
    base = row * s.half if distance == 0 else 0
    token = column_from(s, distance) * s.width + base
    choose(row == owner_of(s, col), own, other, picked.at[:, : s.height])

    def rows_of(at):
        return picked[at, pl.ds(offset_in(s, col), s.slots), :]

    project_right(s, rows_of, base, depth, token, shared, partner)
    project_left(s, own, row, base, depth, token, shared, left)
    project_left(s, other, 1 - row, base, depth, token, shared, right)
    old_mine, old_theirs = before if before else (None, None)
    accumulate(s, left, partner, old_mine, mine)
    if not narrow:
        accumulate(s, right, partner, old_theirs, theirs)
    else:
        accumulate(s, right, partner, old_theirs, picked)
        theirs[...] = picked[:, : s.height].astype(BF16)


def pick(s, own, other, rows, picked):
    col = column_from(s, -2)
    choose(lax.axis_index("row") == owner_of(s, col), own, other, picked.at[:, : s.height])
    for step in range(s.width):
        rows[step] = picked[step, pl.ds(offset_in(s, col), s.slots), :].astype(BF16)


def finish(s, shared, own, rows, mine, given, gating, last_gain, last_weight, *refs):
    update, left, partner, total = refs
    token = column_from(s, s.cols // 2) * s.width
    shared = Shared(s, shared)
    project_right(s, lambda at: rows[at].astype(F32), 0, s.width, token, shared, partner)
    project_left(s, own, lax.axis_index("row"), 0, s.width, token, shared, left)
    accumulate(s, left, partner, mine, total)
    for start in range(0, s.width, s.half):
        settled = [
            normalise(total[start + step] + given[start + step].astype(F32)) * last_gain[...]
            for step in range(s.half)
        ]
        value = dot(jnp.concatenate(settled, 0).astype(BF16), last_weight[...])
        for step in range(s.half):
            part = gating[start + step] * value[step * s.height : (step + 1) * s.height]
            update[start + step] = part.astype(BF16)


def call(body, out_shape, scratch, flops, *operands, grant=24):
    def space(operand):
        return pl.BlockSpec(memory_space=pltpu.SMEM if operand.dtype == jnp.int32 else pltpu.VMEM)

    sent = sum(o.size * o.dtype.itemsize for o in operands)
    return pl.pallas_call(
        body,
        out_shape=out_shape,
        in_specs=[space(o) for o in operands],
        out_specs=jax.tree.map(lambda _: pl.BlockSpec(memory_space=pltpu.VMEM), out_shape),
        scratch_shapes=scratch,
        compiler_params=pltpu.CompilerParams(vmem_limit_bytes=grant * 1024 * 1024),
        cost_estimate=pl.CostEstimate(flops=flops, bytes_accessed=sent, transcendentals=0),
        name=body.func.__name__,
    )(*operands)


def local(
    mesh,
    pair_state,
    valid_length,
    input_gain,
    left_gate,
    left_value,
    right_gate,
    right_value,
    out_gate,
    output_gain,
    out_weight,
):
    height, width, channels = pair_state.shape
    hidden = left_gate.shape[1]
    s = Sizes(mesh, height, width, channels, hidden)
    shape = jax.ShapeDtypeStruct
    pair = jnp.transpose(pair_state, (1, 0, 2))
    gain = input_gain.reshape(1, channels)
    shared = call(
        functools.partial(join, s),
        shape((channels + 8, 4 * hidden), F32),
        [],
        0,
        valid_length,
        gain,
        left_gate,
        left_value,
        right_gate,
        right_value,
        grant=56,
    )
    order = ring(s.cols)

    def shift(block, crossed=False, by=1):
        pairs = []
        for row in range(s.rows):
            target = s.rows - 1 - row if crossed else row
            for at in range(s.cols):
                to = (at + by * (1 - 2 * target)) % s.cols
                pairs.append((row * s.cols + order[at], target * s.cols + order[to]))
        return lax.ppermute(block, ("row", "col"), pairs)

    def swap(block):
        return lax.ppermute(block, "row", [(at, (at + 1) % s.rows) for at in range(s.rows)])

    sums = shape((width, height, hidden), F32)
    product = 16 * height * width * hidden
    tokens = pltpu.VMEM((width, height, hidden), F32)
    halved = pltpu.VMEM((s.half, height, hidden), F32)
    padded = pltpu.VMEM((width, height + TILE, channels), F32)
    partner = pltpu.VMEM((width, s.slots, hidden), F32)
    few = pltpu.VMEM((s.half, s.slots, hidden), F32)

    def add(distance, own, other, before, narrow=False):
        left, right = (halved, few) if distance == 0 else (tokens, partner)
        return call(
            functools.partial(add_both, s, distance, narrow),
            [sums, shape(sums.shape, BF16) if narrow else sums],
            [left, left, padded, right],
            2 * left.shape[0] * product,
            shared,
            own,
            other,
            *before,
        )

    def in_turn(other, own, done):
        own = lax.optimization_barrier((own, done))[0]
        return lax.optimization_barrier((other, own))[0], own

    far = s.cols // 2
    other = shift(pair, crossed=True)
    own = shift(pair)
    total = add(0, pair, swap(pair), ())
    other, own = in_turn(other, own, total)
    rows = ()
    for distance in range(1, far - 1):
        ahead = [shift(other), shift(own)]
        if distance == far - 2:
            rows = call(
                functools.partial(pick, s),
                shape((width, s.slots, channels), BF16),
                [padded],
                0,
                own,
                other,
            )
            rows = shift(rows, by=2)
        total = add(distance, own, other, total)
        other, own = in_turn(*ahead, total)
    last = shift(own)
    gating = call(
        functools.partial(gate, s),
        [sums, shape((1, hidden), F32), shape(out_weight.shape, BF16)],
        [],
        2 * height * width * channels * channels,
        pair,
        shared,
        out_gate,
        output_gain.reshape(1, hidden),
        out_weight,
    )
    own, other, rows = lax.optimization_barrier((own, other, rows))
    mine, theirs = add(far - 1, own, other, total, narrow=True)
    given = swap(theirs)
    last, mine, gating = lax.optimization_barrier((last, mine, gating))
    update = call(
        functools.partial(finish, s),
        shape((width, height, channels), BF16),
        [tokens, partner, pltpu.VMEM(sums.shape, F32)],
        width * product,
        shared,
        last,
        rows,
        mine,
        given,
        *gating,
    )
    return jnp.transpose(update, (1, 0, 2))


def solution(mesh):
    return jax.shard_map(
        functools.partial(local, mesh),
        mesh=mesh,
        in_specs=(P(("parts", "row"), "col", None), P("parts")) + (P(),) * 8,
        out_specs=P(("parts", "row"), "col", None),
        check_vma=False,
    )
```

```python
import functools

import jax
import jax.numpy as jnp
from jax import lax
from jax.experimental import pallas as pl
from jax.experimental.pallas import tpu as pltpu
from jax.sharding import PartitionSpec as P

F32 = jnp.float32
BF16 = jnp.bfloat16
EPS = 1e-05
TILE = 16
CHUNK = 56
GROUP = 7


class Sizes:
    def __init__(self, mesh, height, width, channels, hidden):
        self.rows = mesh.shape["row"]
        self.cols = mesh.shape["col"]
        self.height, self.width = height, width
        self.channels, self.hidden = channels, hidden
        self.half = width // 2
        self.slots = -(-width // TILE) * TILE


def column_at(place, cols):
    return jnp.where(place < cols // 2, 2 * place, 2 * (cols - place) - 1)


def place_of(column, cols):
    return jnp.where(column % 2 == 0, column // 2, cols - 1 - column // 2)


def ring(cols):
    return [2 * at if at < cols // 2 else 2 * (cols - at) - 1 for at in range(cols)]


def normalise(values):
    average = jnp.mean(values, -1, keepdims=True)
    centered = values - average
    variance = jnp.mean(centered * centered, -1, keepdims=True)
    return centered * lax.rsqrt(variance + EPS)


def sigmoid(values):
    return 0.5 * jnp.tanh(0.5 * values) + 0.5


def dot(left, right):
    return jnp.dot(left, right, preferred_element_type=F32)


def gate(s, length, shared, pair, out_gate, last_gain, last_weight, gating, kept_gain, kept_weight):
    gain = Shared(s, length, shared).gain
    kept_gain[...] = last_gain[...]
    kept_weight[...] = last_weight[...]
    for start in range(0, s.width, s.half):
        normed = [
            normalise(pair[start + step].astype(F32)) * gain for step in range(s.half)
        ]
        value = sigmoid(dot(jnp.concatenate(normed, 0).astype(BF16), out_gate[...]))
        for step in range(s.half):
            gating[start + step] = value[step * s.height : (step + 1) * s.height]


def accumulate(s, left, partner, before, total):
    depth = left.shape[0]
    size = CHUNK if s.height % CHUNK == 0 else s.height
    group = GROUP if s.width % GROUP == 0 else 1

    def chunk(index, carry):
        at = pl.ds(pl.multiple_of(index * size, 8), size)
        for first in range(0, s.width, group):
            members = range(first, first + group)
            if before is None:
                sums = tuple(jnp.zeros((size, s.hidden), F32) for _ in members)
            else:
                sums = tuple(before[j, at] for j in members)

            def step(k, sums):
                value = left[k, at]
                return tuple(
                    so_far + value * partner[k, j : j + 1] for so_far, j in zip(sums, members)
                )

            sums = lax.fori_loop(0, depth, step, sums, unroll=s.half)
            for so_far, j in zip(sums, members):
                total[j, at] = so_far
        return carry

    lax.fori_loop(0, s.height // size, chunk, 0)


def owner_of(s, col):
    return col // (s.height // s.width)


def choose(first, one, other, target):
    @pl.when(first)
    def _():
        target[...] = one[...].astype(F32)

    @pl.when(jnp.logical_not(first))
    def _():
        target[...] = other[...].astype(F32)


def offset_in(s, col):
    return (col % (s.height // s.width)) * s.width


def column_from(s, distance):
    row, col = lax.axis_index("row"), lax.axis_index("col")
    step = distance * (2 * row - 1)
    return column_at((place_of(col, s.cols) + step + s.cols) % s.cols, s.cols)


class Shared:
    def __init__(self, s, length, ref):
        h = s.hidden
        self.left = ref[: s.channels, : 2 * h].astype(BF16)
        self.right = ref[: s.channels, 2 * h :].astype(BF16)
        self.gain = ref[s.channels : s.channels + 1, : s.channels]
        self.limit = length[0]


def join(s, gain, left_gate, left_value, right_gate, right_value, shared):
    h = s.hidden
    for at, part in enumerate((left_gate, left_value, right_gate, right_value)):
        shared[: s.channels, at * h : (at + 1) * h] = part[...].astype(F32)
    shared[s.channels : s.channels + 1, : s.channels] = gain[...]


def gated(s, rows, gain, weight, masks):
    h, size = s.hidden, rows[0].shape[0]
    rows = [normalise(row) * gain for row in rows]
    out = dot(jnp.concatenate(rows, 0).astype(BF16), weight)
    value = sigmoid(out[:, :h]) * out[:, h:]
    return [value[at * size : (at + 1) * size] * mask for at, mask in enumerate(masks)]


def masks_of(tokens, first, count, limit):
    below = lax.broadcasted_iota(jnp.int32, (count, 1), 0) + first < limit
    return [(below & (token < limit)).astype(F32) for token in tokens]


def project_right(s, rows_of, base, depth, token, shared, partner):
    first = lax.axis_index("col") * s.width
    for start in range(0, depth, s.half):
        steps = range(start, start + s.half)
        masks = masks_of([token + step for step in steps], first, s.slots, shared.limit)
        rows = [rows_of(base + step) for step in steps]
        for step, part in zip(steps, gated(s, rows, shared.gain, shared.right, masks)):
            partner[step] = part


def project_left(s, block, row, base, depth, token, shared, left):
    first = row * s.height
    for start in range(0, depth, s.half):
        steps = range(start, start + s.half)
        masks = masks_of([token + step for step in steps], first, s.height, shared.limit)
        rows = [block[base + step].astype(F32) for step in steps]
        for step, part in zip(steps, gated(s, rows, shared.gain, shared.left, masks)):
            left[step] = part


def add_both(s, distance, narrow, length, shared, own, other, *refs):
    before, (mine, theirs, left, right, picked, partner) = refs[:-6], refs[-6:]
    row, col = lax.axis_index("row"), lax.axis_index("col")
    shared = Shared(s, length, shared)
    depth = left.shape[0]
    base = row * s.half if distance == 0 else 0
    token = column_from(s, distance) * s.width + base
    choose(row == owner_of(s, col), own, other, picked.at[:, : s.height])

    def rows_of(at):
        return picked[at, pl.ds(offset_in(s, col), s.slots), :]

    project_right(s, rows_of, base, depth, token, shared, partner)
    project_left(s, own, row, base, depth, token, shared, left)
    project_left(s, other, 1 - row, base, depth, token, shared, right)
    old_mine, old_theirs = before if before else (None, None)
    accumulate(s, left, partner, old_mine, mine)
    if not narrow:
        accumulate(s, right, partner, old_theirs, theirs)
    else:
        accumulate(s, right, partner, old_theirs, picked)
        theirs[...] = picked[:, : s.height].astype(BF16)


def pick(s, own, other, rows, picked):
    col = column_from(s, -2)
    choose(lax.axis_index("row") == owner_of(s, col), own, other, picked.at[:, : s.height])
    for step in range(s.width):
        rows[step] = picked[step, pl.ds(offset_in(s, col), s.slots), :].astype(BF16)


def finish(s, length, shared, own, rows, mine, given, gating, last_gain, last_weight, *refs):
    update, left, partner, total = refs
    token = column_from(s, s.cols // 2) * s.width
    shared = Shared(s, length, shared)
    project_right(s, lambda at: rows[at].astype(F32), 0, s.width, token, shared, partner)
    project_left(s, own, lax.axis_index("row"), 0, s.width, token, shared, left)
    accumulate(s, left, partner, mine, total)
    for start in range(0, s.width, s.half):
        settled = [
            normalise(total[start + step] + given[start + step].astype(F32)) * last_gain[...]
            for step in range(s.half)
        ]
        value = dot(jnp.concatenate(settled, 0).astype(BF16), last_weight[...])
        for step in range(s.half):
            part = gating[start + step] * value[step * s.height : (step + 1) * s.height]
            update[start + step] = part.astype(BF16)


def call(body, out_shape, scratch, flops, *operands, grant=24):
    def space(operand):
        return pl.BlockSpec(memory_space=pltpu.SMEM if operand.dtype == jnp.int32 else pltpu.VMEM)

    sent = sum(o.size * o.dtype.itemsize for o in operands)
    return pl.pallas_call(
        body,
        out_shape=out_shape,
        in_specs=[space(o) for o in operands],
        out_specs=jax.tree.map(lambda _: pl.BlockSpec(memory_space=pltpu.VMEM), out_shape),
        scratch_shapes=scratch,
        compiler_params=pltpu.CompilerParams(vmem_limit_bytes=grant * 1024 * 1024),
        cost_estimate=pl.CostEstimate(flops=flops, bytes_accessed=sent, transcendentals=0),
        name=body.func.__name__,
    )(*operands)


def local(
    mesh,
    pair_state,
    valid_length,
    input_gain,
    left_gate,
    left_value,
    right_gate,
    right_value,
    out_gate,
    output_gain,
    out_weight,
):
    height, width, channels = pair_state.shape
    hidden = left_gate.shape[1]
    s = Sizes(mesh, height, width, channels, hidden)
    shape = jax.ShapeDtypeStruct
    pair = jnp.transpose(pair_state, (1, 0, 2))
    gain = input_gain.reshape(1, channels)
    shared = call(
        functools.partial(join, s),
        shape((channels + 8, 4 * hidden), F32),
        [],
        0,
        gain,
        left_gate,
        left_value,
        right_gate,
        right_value,
        grant=56,
    )
    shared = (valid_length, shared)
    order = ring(s.cols)

    def shift(block, crossed=False, by=1):
        pairs = []
        for row in range(s.rows):
            target = s.rows - 1 - row if crossed else row
            for at in range(s.cols):
                to = (at + by * (1 - 2 * target)) % s.cols
                pairs.append((row * s.cols + order[at], target * s.cols + order[to]))
        return lax.ppermute(block, ("row", "col"), pairs)

    def swap(block):
        return lax.ppermute(block, "row", [(at, (at + 1) % s.rows) for at in range(s.rows)])

    sums = shape((width, height, hidden), F32)
    product = 16 * height * width * hidden
    tokens = pltpu.VMEM((width, height, hidden), F32)
    halved = pltpu.VMEM((s.half, height, hidden), F32)
    padded = pltpu.VMEM((width, height + TILE, channels), F32)
    partner = pltpu.VMEM((width, s.slots, hidden), F32)
    few = pltpu.VMEM((s.half, s.slots, hidden), F32)

    def add(distance, own, other, before, narrow=False):
        left, right = (halved, few) if distance == 0 else (tokens, partner)
        return call(
            functools.partial(add_both, s, distance, narrow),
            [sums, shape(sums.shape, BF16) if narrow else sums],
            [left, left, padded, right],
            2 * left.shape[0] * product,
            *shared,
            own,
            other,
            *before,
        )

    def in_turn(other, own, done):
        own = lax.optimization_barrier((own, done))[0]
        return lax.optimization_barrier((other, own))[0], own

    far = s.cols // 2
    other = shift(pair, crossed=True)
    own = shift(pair)
    total = add(0, pair, swap(pair), ())
    other, own = in_turn(other, own, total)
    rows = ()
    for distance in range(1, far - 1):
        ahead = [shift(other), shift(own)]
        if distance == far - 2:
            rows = call(
                functools.partial(pick, s),
                shape((width, s.slots, channels), BF16),
                [padded],
                0,
                own,
                other,
            )
            rows = shift(rows, by=2)
        total = add(distance, own, other, total)
        other, own = in_turn(*ahead, total)
    last = shift(own)
    gating = call(
        functools.partial(gate, s),
        [sums, shape((1, hidden), F32), shape(out_weight.shape, BF16)],
        [],
        2 * height * width * channels * channels,
        *shared,
        pair,
        out_gate,
        output_gain.reshape(1, hidden),
        out_weight,
    )
    own, other, rows = lax.optimization_barrier((own, other, rows))
    mine, theirs = add(far - 1, own, other, total, narrow=True)
    given = swap(theirs)
    last, mine, gating = lax.optimization_barrier((last, mine, gating))
    update = call(
        functools.partial(finish, s),
        shape((width, height, channels), BF16),
        [tokens, partner, pltpu.VMEM(sums.shape, F32)],
        width * product,
        *shared,
        last,
        rows,
        mine,
        given,
        *gating,
    )
    return jnp.transpose(update, (1, 0, 2))


def solution(mesh):
    return jax.shard_map(
        functools.partial(local, mesh),
        mesh=mesh,
        in_specs=(P(("parts", "row"), "col", None), P("parts")) + (P(),) * 8,
        out_specs=P(("parts", "row"), "col", None),
        check_vma=False,
    )
```

```python
import functools

import jax
import jax.numpy as jnp
from jax import lax
from jax.experimental import pallas as pl
from jax.experimental.pallas import tpu as pltpu
from jax.sharding import PartitionSpec as P

F32 = jnp.float32
BF16 = jnp.bfloat16
EPS = 1e-05
TILE = 16
CHUNK = 56
GROUP = 7


class Sizes:
    def __init__(self, mesh, height, width, channels, hidden):
        self.rows = mesh.shape["row"]
        self.cols = mesh.shape["col"]
        self.height, self.width = height, width
        self.channels, self.hidden = channels, hidden
        self.half = width // 2
        self.slots = -(-width // TILE) * TILE


def column_at(place, cols):
    return jnp.where(place < cols // 2, 2 * place, 2 * (cols - place) - 1)


def place_of(column, cols):
    return jnp.where(column % 2 == 0, column // 2, cols - 1 - column // 2)


def ring(cols):
    return [2 * at if at < cols // 2 else 2 * (cols - at) - 1 for at in range(cols)]


def normalise(values):
    average = jnp.mean(values, -1, keepdims=True)
    centered = values - average
    variance = jnp.mean(centered * centered, -1, keepdims=True)
    return centered * lax.rsqrt(variance + EPS)


def sigmoid(values):
    return 0.5 * jnp.tanh(0.5 * values) + 0.5


def dot(left, right):
    return jnp.dot(left, right, preferred_element_type=F32)


def gate(s, length, shared, pair, out_gate, last_gain, last_weight, gating, kept_gain, kept_weight):
    gain = Shared(s, length, shared).gain
    kept_gain[...] = last_gain[...]
    kept_weight[...] = last_weight[...]
    for start in range(0, s.width, s.half):
        normed = [
            normalise(pair[start + step].astype(F32)) * gain for step in range(s.half)
        ]
        value = sigmoid(dot(jnp.concatenate(normed, 0).astype(BF16), out_gate[...]))
        for step in range(s.half):
            gating[start + step] = value[step * s.height : (step + 1) * s.height]


def accumulate(s, left, partner, before, total):
    depth = left.shape[0]
    size = CHUNK if s.height % CHUNK == 0 else s.height
    group = GROUP if s.width % GROUP == 0 else 1

    def chunk(index, carry):
        at = pl.ds(pl.multiple_of(index * size, 8), size)
        for first in range(0, s.width, group):
            members = range(first, first + group)
            if before is None:
                sums = tuple(jnp.zeros((size, s.hidden), F32) for _ in members)
            else:
                sums = tuple(before[j, at] for j in members)

            def step(k, sums):
                value = left[k, at]
                return tuple(
                    so_far + value * partner[k, j : j + 1] for so_far, j in zip(sums, members)
                )

            sums = lax.fori_loop(0, depth, step, sums, unroll=s.half)
            for so_far, j in zip(sums, members):
                total[j, at] = so_far
        return carry

    lax.fori_loop(0, s.height // size, chunk, 0)


def owner_of(s, col):
    return col // (s.height // s.width)


def choose(first, one, other, target):
    @pl.when(first)
    def _():
        target[...] = one[...].astype(F32)

    @pl.when(jnp.logical_not(first))
    def _():
        target[...] = other[...].astype(F32)


def offset_in(s, col):
    return (col % (s.height // s.width)) * s.width


def column_from(s, distance):
    row, col = lax.axis_index("row"), lax.axis_index("col")
    step = distance * (2 * row - 1)
    return column_at((place_of(col, s.cols) + step + s.cols) % s.cols, s.cols)


class Shared:
    def __init__(self, s, length, ref):
        h = s.hidden
        self.left = ref[: s.channels, : 2 * h].astype(BF16)
        self.right = ref[: s.channels, 2 * h :].astype(BF16)
        self.gain = ref[s.channels : s.channels + 1, : s.channels]
        self.limit = length[0]


def join(s, gain, left_gate, left_value, right_gate, right_value, shared):
    h = s.hidden
    for at, part in enumerate((left_gate, left_value, right_gate, right_value)):
        shared[: s.channels, at * h : (at + 1) * h] = part[...].astype(F32)
    shared[s.channels : s.channels + 1, : s.channels] = gain[...]


def gated(s, rows, gain, weight, masks):
    h, size = s.hidden, rows[0].shape[0]
    rows = [normalise(row) * gain for row in rows]
    out = dot(jnp.concatenate(rows, 0).astype(BF16), weight)
    value = sigmoid(out[:, :h]) * out[:, h:]
    return [value[at * size : (at + 1) * size] * mask for at, mask in enumerate(masks)]


def masks_of(tokens, first, count, limit):
    below = lax.broadcasted_iota(jnp.int32, (count, 1), 0) + first < limit
    return [(below & (token < limit)).astype(F32) for token in tokens]


def project_right(s, rows_of, base, depth, token, shared, partner):
    first = lax.axis_index("col") * s.width
    for start in range(0, depth, s.half):
        steps = range(start, start + s.half)
        masks = masks_of([token + step for step in steps], first, s.slots, shared.limit)
        rows = [rows_of(base + step) for step in steps]
        for step, part in zip(steps, gated(s, rows, shared.gain, shared.right, masks)):
            partner[step] = part


def project_left(s, block, row, base, depth, token, shared, left):
    first = row * s.height
    for start in range(0, depth, s.half):
        steps = range(start, start + s.half)
        masks = masks_of([token + step for step in steps], first, s.height, shared.limit)
        rows = [block[base + step].astype(F32) for step in steps]
        for step, part in zip(steps, gated(s, rows, shared.gain, shared.left, masks)):
            left[step] = part


def add_both(s, distance, narrow, length, shared, own, other, *refs):
    before, (mine, theirs, left, right, picked, partner) = refs[:-6], refs[-6:]
    row, col = lax.axis_index("row"), lax.axis_index("col")
    shared = Shared(s, length, shared)
    depth = left.shape[0]
    base = row * s.half if distance == 0 else 0
    token = column_from(s, distance) * s.width + base
    choose(row == owner_of(s, col), own, other, picked.at[:, : s.height])

    def rows_of(at):
        return picked[at, pl.ds(offset_in(s, col), s.slots), :]

    project_right(s, rows_of, base, depth, token, shared, partner)
    project_left(s, own, row, base, depth, token, shared, left)
    project_left(s, other, 1 - row, base, depth, token, shared, right)
    old_mine, old_theirs = before if before else (None, None)
    accumulate(s, left, partner, old_mine, mine)
    if not narrow:
        accumulate(s, right, partner, old_theirs, theirs)
    else:
        accumulate(s, right, partner, old_theirs, picked)
        theirs[...] = picked[:, : s.height].astype(BF16)


def pick(s, ahead, own, other, rows, picked):
    col = column_from(s, -ahead)
    choose(lax.axis_index("row") == owner_of(s, col), own, other, picked.at[:, : s.height])
    for step in range(s.width):
        rows[step] = picked[step, pl.ds(offset_in(s, col), s.slots), :].astype(BF16)


def finish(s, length, shared, own, rows, mine, given, gating, last_gain, last_weight, *refs):
    update, left, partner, total = refs
    token = column_from(s, s.cols // 2) * s.width
    shared = Shared(s, length, shared)
    project_right(s, lambda at: rows[at].astype(F32), 0, s.width, token, shared, partner)
    project_left(s, own, lax.axis_index("row"), 0, s.width, token, shared, left)
    accumulate(s, left, partner, mine, total)
    for start in range(0, s.width, s.half):
        settled = [
            normalise(total[start + step] + given[start + step].astype(F32)) * last_gain[...]
            for step in range(s.half)
        ]
        value = dot(jnp.concatenate(settled, 0).astype(BF16), last_weight[...])
        for step in range(s.half):
            part = gating[start + step] * value[step * s.height : (step + 1) * s.height]
            update[start + step] = part.astype(BF16)


def call(body, out_shape, scratch, flops, *operands, grant=24):
    def space(operand):
        return pl.BlockSpec(memory_space=pltpu.SMEM if operand.dtype == jnp.int32 else pltpu.VMEM)

    sent = sum(o.size * o.dtype.itemsize for o in operands)
    return pl.pallas_call(
        body,
        out_shape=out_shape,
        in_specs=[space(o) for o in operands],
        out_specs=jax.tree.map(lambda _: pl.BlockSpec(memory_space=pltpu.VMEM), out_shape),
        scratch_shapes=scratch,
        compiler_params=pltpu.CompilerParams(vmem_limit_bytes=grant * 1024 * 1024),
        cost_estimate=pl.CostEstimate(flops=flops, bytes_accessed=sent, transcendentals=0),
        name=body.func.__name__,
    )(*operands)


def local(
    mesh,
    pair_state,
    valid_length,
    input_gain,
    left_gate,
    left_value,
    right_gate,
    right_value,
    out_gate,
    output_gain,
    out_weight,
):
    height, width, channels = pair_state.shape
    hidden = left_gate.shape[1]
    s = Sizes(mesh, height, width, channels, hidden)
    shape = jax.ShapeDtypeStruct
    pair = jnp.transpose(pair_state, (1, 0, 2))
    gain = input_gain.reshape(1, channels)
    shared = call(
        functools.partial(join, s),
        shape((channels + 8, 4 * hidden), F32),
        [],
        0,
        gain,
        left_gate,
        left_value,
        right_gate,
        right_value,
        grant=56,
    )
    shared = (valid_length, shared)
    order = ring(s.cols)

    def shift(block, crossed=False, by=1):
        pairs = []
        for row in range(s.rows):
            target = s.rows - 1 - row if crossed else row
            for at in range(s.cols):
                to = (at + by * (1 - 2 * target)) % s.cols
                pairs.append((row * s.cols + order[at], target * s.cols + order[to]))
        return lax.ppermute(block, ("row", "col"), pairs)

    def swap(block):
        return lax.ppermute(block, "row", [(at, (at + 1) % s.rows) for at in range(s.rows)])

    sums = shape((width, height, hidden), F32)
    product = 16 * height * width * hidden
    tokens = pltpu.VMEM((width, height, hidden), F32)
    halved = pltpu.VMEM((s.half, height, hidden), F32)
    padded = pltpu.VMEM((width, height + TILE, channels), F32)
    partner = pltpu.VMEM((width, s.slots, hidden), F32)
    few = pltpu.VMEM((s.half, s.slots, hidden), F32)

    def add(distance, own, other, before, narrow=False):
        left, right = (halved, few) if distance == 0 else (tokens, partner)
        return call(
            functools.partial(add_both, s, distance, narrow),
            [sums, shape(sums.shape, BF16) if narrow else sums],
            [left, left, padded, right],
            2 * left.shape[0] * product,
            *shared,
            own,
            other,
            *before,
        )

    def in_turn(other, own, done):
        own = lax.optimization_barrier((own, done))[0]
        return lax.optimization_barrier((other, own))[0], own

    far = s.cols // 2
    other = shift(pair, crossed=True)
    own = shift(pair)
    total = add(0, pair, swap(pair), ())
    other, own = in_turn(other, own, total)
    early = min(3, far - 1)
    for distance in range(1, far - 1):
        ahead = [shift(other), shift(own)]
        if distance == far - early:
            rows = call(
                functools.partial(pick, s, early),
                shape((width, s.slots, channels), BF16),
                [padded],
                0,
                own,
                other,
            )
            rows = shift(rows, by=early)
        total = add(distance, own, other, total)
        other, own = in_turn(*ahead, total)
        if distance == far - early:
            later = lax.optimization_barrier((pair, own))[0]
            gating = call(
                functools.partial(gate, s),
                [sums, shape((1, hidden), F32), shape(out_weight.shape, BF16)],
                [],
                2 * height * width * channels * channels,
                *shared,
                later,
                out_gate,
                output_gain.reshape(1, hidden),
                out_weight,
            )
            other, rows, gating = lax.optimization_barrier((other, rows, gating))
    last = shift(own)
    mine, theirs = add(far - 1, own, other, total, narrow=True)
    given = swap(theirs)
    last, mine, gating = lax.optimization_barrier((last, mine, gating))
    update = call(
        functools.partial(finish, s),
        shape((width, height, channels), BF16),
        [tokens, partner, pltpu.VMEM(sums.shape, F32)],
        width * product,
        *shared,
        last,
        rows,
        mine,
        given,
        *gating,
    )
    return jnp.transpose(update, (1, 0, 2))


def solution(mesh):
    return jax.shard_map(
        functools.partial(local, mesh),
        mesh=mesh,
        in_specs=(P(("parts", "row"), "col", None), P("parts")) + (P(),) * 8,
        out_specs=P(("parts", "row"), "col", None),
        check_vma=False,
    )
```

```python
import functools

import jax
import jax.numpy as jnp
from jax import lax
from jax.experimental import pallas as pl
from jax.experimental.pallas import tpu as pltpu
from jax.sharding import PartitionSpec as P

F32 = jnp.float32
BF16 = jnp.bfloat16
EPS = 1e-05
TILE = 16
CHUNK = 56
GROUP = 7


class Sizes:
    def __init__(self, mesh, height, width, channels, hidden):
        self.rows = mesh.shape["row"]
        self.cols = mesh.shape["col"]
        self.height, self.width = height, width
        self.channels, self.hidden = channels, hidden
        self.half = width // 2
        self.slots = -(-width // TILE) * TILE


def column_at(place, cols):
    return jnp.where(place < cols // 2, 2 * place, 2 * (cols - place) - 1)


def place_of(column, cols):
    return jnp.where(column % 2 == 0, column // 2, cols - 1 - column // 2)


def ring(cols):
    return [2 * at if at < cols // 2 else 2 * (cols - at) - 1 for at in range(cols)]


def normalise(values):
    average = jnp.mean(values, -1, keepdims=True)
    centered = values - average
    variance = jnp.mean(centered * centered, -1, keepdims=True)
    return centered * lax.rsqrt(variance + EPS)


def sigmoid(values):
    return 0.5 * jnp.tanh(0.5 * values) + 0.5


def dot(left, right):
    return jnp.dot(left, right, preferred_element_type=F32)


def gate(s, length, shared, pair, out_gate, last_gain, last_weight, gating, kept_gain, kept_weight):
    gain = Shared(s, length, shared).gain
    kept_gain[...] = last_gain[...]
    kept_weight[...] = last_weight[...]
    for start in range(0, s.width, s.half):
        normed = [
            normalise(pair[start + step].astype(F32)) * gain for step in range(s.half)
        ]
        value = sigmoid(dot(jnp.concatenate(normed, 0).astype(BF16), out_gate[...]))
        for step in range(s.half):
            gating[start + step] = value[step * s.height : (step + 1) * s.height]


def accumulate(s, left, partner, before, total):
    depth = left.shape[0]
    size = CHUNK if s.height % CHUNK == 0 else s.height
    group = GROUP if s.width % GROUP == 0 else 1

    def chunk(index, carry):
        at = pl.ds(pl.multiple_of(index * size, 8), size)
        for first in range(0, s.width, group):
            members = range(first, first + group)
            if before is None:
                sums = tuple(jnp.zeros((size, s.hidden), F32) for _ in members)
            else:
                sums = tuple(before[j, at] for j in members)

            def step(k, sums):
                value = left[k, at]
                return tuple(
                    so_far + value * partner[k, j : j + 1] for so_far, j in zip(sums, members)
                )

            sums = lax.fori_loop(0, depth, step, sums, unroll=s.half)
            for so_far, j in zip(sums, members):
                total[j, at] = so_far
        return carry

    lax.fori_loop(0, s.height // size, chunk, 0)


def owner_of(s, col):
    return col // (s.height // s.width)


def choose(first, one, other, target):
    @pl.when(first)
    def _():
        target[...] = one[...].astype(F32)

    @pl.when(jnp.logical_not(first))
    def _():
        target[...] = other[...].astype(F32)


def offset_in(s, col):
    return (col % (s.height // s.width)) * s.width


def column_from(s, distance):
    row, col = lax.axis_index("row"), lax.axis_index("col")
    step = distance * (2 * row - 1)
    return column_at((place_of(col, s.cols) + step + s.cols) % s.cols, s.cols)


class Shared:
    def __init__(self, s, length, ref):
        h = s.hidden
        self.left = ref[: s.channels, : 2 * h].astype(BF16)
        self.right = ref[: s.channels, 2 * h :].astype(BF16)
        self.gain = ref[s.channels : s.channels + 1, : s.channels]
        self.limit = length[0]


def join(s, gain, left_gate, left_value, right_gate, right_value, shared):
    h = s.hidden
    for at, part in enumerate((left_gate, left_value, right_gate, right_value)):
        shared[: s.channels, at * h : (at + 1) * h] = part[...].astype(F32)
    shared[s.channels : s.channels + 1, : s.channels] = gain[...]


def gated(s, rows, gain, weight, masks):
    h, size = s.hidden, rows[0].shape[0]
    rows = [normalise(row) * gain for row in rows]
    out = dot(jnp.concatenate(rows, 0).astype(BF16), weight)
    value = sigmoid(out[:, :h]) * out[:, h:]
    return [value[at * size : (at + 1) * size] * mask for at, mask in enumerate(masks)]


def masks_of(tokens, first, count, limit):
    below = lax.broadcasted_iota(jnp.int32, (count, 1), 0) + first < limit
    return [(below & (token < limit)).astype(F32) for token in tokens]


def project_right(s, rows_of, base, depth, token, shared, partner):
    first = lax.axis_index("col") * s.width
    for start in range(0, depth, s.half):
        steps = range(start, start + s.half)
        masks = masks_of([token + step for step in steps], first, s.slots, shared.limit)
        rows = [rows_of(base + step) for step in steps]
        for step, part in zip(steps, gated(s, rows, shared.gain, shared.right, masks)):
            partner[step] = part


def project_left(s, block, row, base, depth, token, shared, left):
    first = row * s.height
    for start in range(0, depth, s.half):
        steps = range(start, start + s.half)
        masks = masks_of([token + step for step in steps], first, s.height, shared.limit)
        rows = [block[base + step].astype(F32) for step in steps]
        for step, part in zip(steps, gated(s, rows, shared.gain, shared.left, masks)):
            left[step] = part


def add_both(s, distance, narrow, length, shared, own, other, *refs):
    before, (mine, theirs, left, right, picked, partner) = refs[:-6], refs[-6:]
    row, col = lax.axis_index("row"), lax.axis_index("col")
    shared = Shared(s, length, shared)
    depth = left.shape[0]
    base = row * s.half if distance == 0 else 0
    token = column_from(s, distance) * s.width + base
    choose(row == owner_of(s, col), own, other, picked.at[:, : s.height])

    def rows_of(at):
        return picked[at, pl.ds(offset_in(s, col), s.slots), :]

    project_right(s, rows_of, base, depth, token, shared, partner)
    project_left(s, own, row, base, depth, token, shared, left)
    project_left(s, other, 1 - row, base, depth, token, shared, right)
    old_mine, old_theirs = before if before else (None, None)
    accumulate(s, left, partner, old_mine, mine)
    if not narrow:
        accumulate(s, right, partner, old_theirs, theirs)
    else:
        accumulate(s, right, partner, old_theirs, picked)
        theirs[...] = picked[:, : s.height].astype(BF16)


def last_right(s, length, shared, own, right, picked, partner):
    shared = Shared(s, length, shared)
    picked[:, : s.height] = own[...].astype(F32)
    offset = offset_in(s, lax.axis_index("col"))
    token = column_from(s, s.cols // 2) * s.width

    def rows_of(at):
        return picked[at, pl.ds(offset, s.slots), :]

    project_right(s, rows_of, 0, s.width, token, shared, partner)
    right[...] = partner[...].astype(BF16)


def last_left(s, length, shared, own, left):
    shared = Shared(s, length, shared)
    token = column_from(s, s.cols // 2) * s.width
    project_left(s, own, lax.axis_index("row"), 0, s.width, token, shared, left)


def finish(s, left, right, other, mine, given, gating, last_gain, last_weight, *refs):
    update, partner, total = refs
    choose(lax.axis_index("row") == owner_of(s, lax.axis_index("col")), right, other, partner)
    accumulate(s, left, partner, mine, total)
    for start in range(0, s.width, s.half):
        settled = [
            normalise(total[start + step] + given[start + step].astype(F32)) * last_gain[...]
            for step in range(s.half)
        ]
        value = dot(jnp.concatenate(settled, 0).astype(BF16), last_weight[...])
        for step in range(s.half):
            part = gating[start + step] * value[step * s.height : (step + 1) * s.height]
            update[start + step] = part.astype(BF16)


def call(body, out_shape, scratch, flops, *operands, grant=24):
    def space(operand):
        return pl.BlockSpec(memory_space=pltpu.SMEM if operand.dtype == jnp.int32 else pltpu.VMEM)

    sent = sum(o.size * o.dtype.itemsize for o in operands)
    return pl.pallas_call(
        body,
        out_shape=out_shape,
        in_specs=[space(o) for o in operands],
        out_specs=jax.tree.map(lambda _: pl.BlockSpec(memory_space=pltpu.VMEM), out_shape),
        scratch_shapes=scratch,
        compiler_params=pltpu.CompilerParams(vmem_limit_bytes=grant * 1024 * 1024),
        cost_estimate=pl.CostEstimate(flops=flops, bytes_accessed=sent, transcendentals=0),
        name=body.func.__name__,
    )(*operands)


def local(
    mesh,
    pair_state,
    valid_length,
    input_gain,
    left_gate,
    left_value,
    right_gate,
    right_value,
    out_gate,
    output_gain,
    out_weight,
):
    height, width, channels = pair_state.shape
    hidden = left_gate.shape[1]
    s = Sizes(mesh, height, width, channels, hidden)
    shape = jax.ShapeDtypeStruct
    pair = jnp.transpose(pair_state, (1, 0, 2))
    gain = input_gain.reshape(1, channels)
    shared = call(
        functools.partial(join, s),
        shape((channels + 8, 4 * hidden), F32),
        [],
        0,
        gain,
        left_gate,
        left_value,
        right_gate,
        right_value,
        grant=56,
    )
    shared = (valid_length, shared)
    order = ring(s.cols)

    def shift(block, crossed=False, by=1):
        pairs = []
        for row in range(s.rows):
            target = s.rows - 1 - row if crossed else row
            for at in range(s.cols):
                to = (at + by * (1 - 2 * target)) % s.cols
                pairs.append((row * s.cols + order[at], target * s.cols + order[to]))
        return lax.ppermute(block, ("row", "col"), pairs)

    def swap(block):
        return lax.ppermute(block, "row", [(at, (at + 1) % s.rows) for at in range(s.rows)])

    sums = shape((width, height, hidden), F32)
    product = 16 * height * width * hidden
    tokens = pltpu.VMEM((width, height, hidden), F32)
    halved = pltpu.VMEM((s.half, height, hidden), F32)
    padded = pltpu.VMEM((width, height + TILE, channels), F32)
    partner = pltpu.VMEM((width, s.slots, hidden), F32)
    few = pltpu.VMEM((s.half, s.slots, hidden), F32)

    def add(distance, own, other, before, narrow=False):
        left, right = (halved, few) if distance == 0 else (tokens, partner)
        return call(
            functools.partial(add_both, s, distance, narrow),
            [sums, shape(sums.shape, BF16) if narrow else sums],
            [left, left, padded, right],
            2 * left.shape[0] * product,
            *shared,
            own,
            other,
            *before,
        )

    def in_turn(other, own, done):
        own = lax.optimization_barrier((own, done))[0]
        return lax.optimization_barrier((other, own))[0], own

    far = s.cols // 2
    other = shift(pair, crossed=True)
    own = shift(pair)
    total = add(0, pair, swap(pair), ())
    other, own = in_turn(other, own, total)
    for distance in range(1, far - 1):
        ahead = [shift(other), shift(own)]
        total = add(distance, own, other, total)
        if distance == 1:
            gating = call(
                functools.partial(gate, s),
                [sums, shape((1, hidden), F32), shape(out_weight.shape, BF16)],
                [],
                2 * height * width * channels * channels,
                *shared,
                pair,
                out_gate,
                output_gain.reshape(1, hidden),
                out_weight,
            )
        other, own = in_turn(*ahead, (total, gating))
    last = shift(own)
    mine, theirs = add(far - 1, own, other, total, narrow=True)
    given = swap(theirs)
    last, mine, gating = lax.optimization_barrier((last, mine, gating))
    right = call(
        functools.partial(last_right, s),
        shape((width, s.slots, hidden), BF16),
        [padded, partner],
        0,
        *shared,
        last,
    )
    swapped = swap(right)
    left = call(functools.partial(last_left, s), sums, [], 0, *shared, last)
    update = call(
        functools.partial(finish, s),
        shape((width, height, channels), BF16),
        [partner, pltpu.VMEM(sums.shape, F32)],
        width * product,
        left,
        right,
        swapped,
        mine,
        given,
        *gating,
    )
    return jnp.transpose(update, (1, 0, 2))


def solution(mesh):
    return jax.shard_map(
        functools.partial(local, mesh),
        mesh=mesh,
        in_specs=(P(("parts", "row"), "col", None), P("parts")) + (P(),) * 8,
        out_specs=P(("parts", "row"), "col", None),
        check_vma=False,
    )
```

```python
import functools

import jax
import jax.numpy as jnp
from jax import lax
from jax.experimental import pallas as pl
from jax.experimental.pallas import tpu as pltpu
from jax.sharding import PartitionSpec as P

F32 = jnp.float32
BF16 = jnp.bfloat16
EPS = 1e-05
TILE = 16
CHUNK = 56
GROUP = 7


class Sizes:
    def __init__(self, mesh, height, width, channels, hidden):
        self.rows = mesh.shape["row"]
        self.cols = mesh.shape["col"]
        self.height, self.width = height, width
        self.channels, self.hidden = channels, hidden
        self.half = width // 2
        self.slots = -(-width // TILE) * TILE


def column_at(place, cols):
    return jnp.where(place < cols // 2, 2 * place, 2 * (cols - place) - 1)


def place_of(column, cols):
    return jnp.where(column % 2 == 0, column // 2, cols - 1 - column // 2)


def ring(cols):
    return [2 * at if at < cols // 2 else 2 * (cols - at) - 1 for at in range(cols)]


def normalise(values):
    average = jnp.mean(values, -1, keepdims=True)
    centered = values - average
    variance = jnp.mean(centered * centered, -1, keepdims=True)
    return centered * lax.rsqrt(variance + EPS)


def normalise_tokens(values):
    channels = values.shape[-1]
    mean = jnp.full((channels, channels), 1.0 / channels, BF16)
    centered = values - dot(values.astype(BF16), mean)
    variance = dot((centered * centered).astype(BF16), mean)
    return centered * lax.rsqrt(variance + EPS)


def sigmoid(values):
    return 0.5 * jnp.tanh(0.5 * values) + 0.5


def dot(left, right):
    return jnp.dot(left, right, preferred_element_type=F32)


def gate(s, length, shared, pair, out_gate, last_gain, last_weight, gating, kept_gain, kept_weight):
    gain = Shared(s, length, shared).gain
    kept_gain[...] = last_gain[...]
    kept_weight[...] = last_weight[...]
    for start in range(0, s.width, s.half):
        rows = jnp.concatenate([pair[start + step].astype(F32) for step in range(s.half)], 0)
        value = sigmoid(dot((normalise_tokens(rows) * gain).astype(BF16), out_gate[...]))
        for step in range(s.half):
            gating[start + step] = value[step * s.height : (step + 1) * s.height]


def accumulate(s, left, partner, before, total):
    depth = left.shape[0]
    size = CHUNK if s.height % CHUNK == 0 else s.height
    group = GROUP if s.width % GROUP == 0 else 1

    def chunk(index, carry):
        at = pl.ds(pl.multiple_of(index * size, 8), size)
        for first in range(0, s.width, group):
            members = range(first, first + group)
            if before is None:
                sums = tuple(jnp.zeros((size, s.hidden), F32) for _ in members)
            else:
                sums = tuple(before[j, at] for j in members)

            def step(k, sums):
                value = left[k, at]
                return tuple(
                    so_far + value * partner[k, j : j + 1] for so_far, j in zip(sums, members)
                )

            sums = lax.fori_loop(0, depth, step, sums, unroll=s.half)
            for so_far, j in zip(sums, members):
                total[j, at] = so_far
        return carry

    lax.fori_loop(0, s.height // size, chunk, 0)


def owner_of(s, col):
    return col // (s.height // s.width)


def choose(first, one, other, target):
    @pl.when(first)
    def _():
        target[...] = one[...].astype(F32)

    @pl.when(jnp.logical_not(first))
    def _():
        target[...] = other[...].astype(F32)


def offset_in(s, col):
    return (col % (s.height // s.width)) * s.width


def column_from(s, distance):
    row, col = lax.axis_index("row"), lax.axis_index("col")
    step = distance * (2 * row - 1)
    return column_at((place_of(col, s.cols) + step + s.cols) % s.cols, s.cols)


class Shared:
    def __init__(self, s, length, ref):
        h = s.hidden
        self.left = ref[: s.channels, : 2 * h].astype(BF16)
        self.right = ref[: s.channels, 2 * h :].astype(BF16)
        self.gain = ref[s.channels : s.channels + 1, : s.channels]
        self.limit = length[0]


def join(s, gain, left_gate, left_value, right_gate, right_value, shared):
    h = s.hidden
    for at, part in enumerate((left_gate, left_value, right_gate, right_value)):
        shared[: s.channels, at * h : (at + 1) * h] = 0.5 * part[...].astype(F32)
    shared[s.channels : s.channels + 1, : s.channels] = gain[...]


def gated(s, rows, gain, weight, masks):
    h, size = s.hidden, rows[0].shape[0]
    rows = normalise_tokens(jnp.concatenate(rows, 0)) * gain
    out = dot(rows.astype(BF16), weight)
    value = (jnp.tanh(out[:, :h]) + 1.0) * out[:, h:]
    return [value[at * size : (at + 1) * size] * mask for at, mask in enumerate(masks)]


def masks_of(tokens, first, count, limit):
    below = lax.broadcasted_iota(jnp.int32, (count, 1), 0) + first < limit
    return [(below & (token < limit)).astype(F32) for token in tokens]


def project_right(s, rows_of, base, depth, token, shared, partner):
    first = lax.axis_index("col") * s.width
    for start in range(0, depth, s.half):
        steps = range(start, start + s.half)
        masks = masks_of([token + step for step in steps], first, s.slots, shared.limit)
        rows = [rows_of(base + step) for step in steps]
        for step, part in zip(steps, gated(s, rows, shared.gain, shared.right, masks)):
            partner[step] = part


def project_left(s, block, row, base, depth, token, shared, left):
    first = row * s.height
    for start in range(0, depth, s.half):
        steps = range(start, start + s.half)
        masks = masks_of([token + step for step in steps], first, s.height, shared.limit)
        rows = [block[base + step].astype(F32) for step in steps]
        for step, part in zip(steps, gated(s, rows, shared.gain, shared.left, masks)):
            left[step] = part


def add_both(s, distance, narrow, length, shared, own, other, *refs):
    before, (mine, theirs, left, right, picked, partner) = refs[:-6], refs[-6:]
    row, col = lax.axis_index("row"), lax.axis_index("col")
    shared = Shared(s, length, shared)
    depth = left.shape[0]
    base = row * s.half if distance == 0 else 0
    token = column_from(s, distance) * s.width + base
    choose(row == owner_of(s, col), own, other, picked.at[:, : s.height])

    def rows_of(at):
        return picked[at, pl.ds(offset_in(s, col), s.slots), :]

    project_right(s, rows_of, base, depth, token, shared, partner)
    project_left(s, own, row, base, depth, token, shared, left)
    project_left(s, other, 1 - row, base, depth, token, shared, right)
    old_mine, old_theirs = before if before else (None, None)
    accumulate(s, left, partner, old_mine, mine)
    if not narrow:
        accumulate(s, right, partner, old_theirs, theirs)
    else:
        accumulate(s, right, partner, old_theirs, picked)
        theirs[...] = picked[:, : s.height].astype(BF16)


def last_right(s, length, shared, own, right, picked, partner):
    shared = Shared(s, length, shared)
    picked[:, : s.height] = own[...].astype(F32)
    offset = offset_in(s, lax.axis_index("col"))
    token = column_from(s, s.cols // 2) * s.width

    def rows_of(at):
        return picked[at, pl.ds(offset, s.slots), :]

    project_right(s, rows_of, 0, s.width, token, shared, partner)
    right[...] = partner[...].astype(BF16)


def last_left(s, length, shared, own, left):
    shared = Shared(s, length, shared)
    token = column_from(s, s.cols // 2) * s.width
    project_left(s, own, lax.axis_index("row"), 0, s.width, token, shared, left)


def finish(s, left, right, other, mine, given, gating, last_gain, last_weight, *refs):
    update, partner, total = refs
    choose(lax.axis_index("row") == owner_of(s, lax.axis_index("col")), right, other, partner)
    accumulate(s, left, partner, mine, total)
    for start in range(0, s.width, s.half):
        settled = [
            normalise(total[start + step] + given[start + step].astype(F32)) * last_gain[...]
            for step in range(s.half)
        ]
        value = dot(jnp.concatenate(settled, 0).astype(BF16), last_weight[...])
        for step in range(s.half):
            part = gating[start + step] * value[step * s.height : (step + 1) * s.height]
            update[start + step] = part.astype(BF16)


def call(body, out_shape, scratch, flops, *operands, grant=24):
    def space(operand):
        return pl.BlockSpec(memory_space=pltpu.SMEM if operand.dtype == jnp.int32 else pltpu.VMEM)

    sent = sum(o.size * o.dtype.itemsize for o in operands)
    return pl.pallas_call(
        body,
        out_shape=out_shape,
        in_specs=[space(o) for o in operands],
        out_specs=jax.tree.map(lambda _: pl.BlockSpec(memory_space=pltpu.VMEM), out_shape),
        scratch_shapes=scratch,
        compiler_params=pltpu.CompilerParams(vmem_limit_bytes=grant * 1024 * 1024),
        cost_estimate=pl.CostEstimate(flops=flops, bytes_accessed=sent, transcendentals=0),
        name=body.func.__name__,
    )(*operands)


def local(
    mesh,
    pair_state,
    valid_length,
    input_gain,
    left_gate,
    left_value,
    right_gate,
    right_value,
    out_gate,
    output_gain,
    out_weight,
):
    height, width, channels = pair_state.shape
    hidden = left_gate.shape[1]
    s = Sizes(mesh, height, width, channels, hidden)
    shape = jax.ShapeDtypeStruct
    pair = jnp.transpose(pair_state, (1, 0, 2))
    gain = input_gain.reshape(1, channels)
    shared = call(
        functools.partial(join, s),
        shape((channels + 8, 4 * hidden), F32),
        [],
        0,
        gain,
        left_gate,
        left_value,
        right_gate,
        right_value,
        grant=56,
    )
    shared = (valid_length, shared)
    order = ring(s.cols)

    def shift(block, crossed=False, by=1):
        pairs = []
        for row in range(s.rows):
            target = s.rows - 1 - row if crossed else row
            for at in range(s.cols):
                to = (at + by * (1 - 2 * target)) % s.cols
                pairs.append((row * s.cols + order[at], target * s.cols + order[to]))
        return lax.ppermute(block, ("row", "col"), pairs)

    def swap(block):
        return lax.ppermute(block, "row", [(at, (at + 1) % s.rows) for at in range(s.rows)])

    sums = shape((width, height, hidden), F32)
    product = 16 * height * width * hidden
    tokens = pltpu.VMEM((width, height, hidden), F32)
    halved = pltpu.VMEM((s.half, height, hidden), F32)
    padded = pltpu.VMEM((width, height + TILE, channels), F32)
    partner = pltpu.VMEM((width, s.slots, hidden), F32)
    few = pltpu.VMEM((s.half, s.slots, hidden), F32)

    def add(distance, own, other, before, narrow=False):
        left, right = (halved, few) if distance == 0 else (tokens, partner)
        return call(
            functools.partial(add_both, s, distance, narrow),
            [sums, shape(sums.shape, BF16) if narrow else sums],
            [left, left, padded, right],
            2 * left.shape[0] * product,
            *shared,
            own,
            other,
            *before,
        )

    def in_turn(other, own, done):
        own = lax.optimization_barrier((own, done))[0]
        return lax.optimization_barrier((other, own))[0], own

    far = s.cols // 2
    other = shift(pair, crossed=True)
    own = shift(pair)
    total = add(0, pair, swap(pair), ())
    other, own = in_turn(other, own, total)
    for distance in range(1, far - 1):
        ahead = [shift(other), shift(own)]
        total = add(distance, own, other, total)
        if distance == 1:
            gating = call(
                functools.partial(gate, s),
                [sums, shape((1, hidden), F32), shape(out_weight.shape, BF16)],
                [],
                2 * height * width * channels * channels,
                *shared,
                pair,
                out_gate,
                output_gain.reshape(1, hidden),
                out_weight,
            )
        other, own = in_turn(*ahead, (total, gating))
    last = shift(own)
    mine, theirs = add(far - 1, own, other, total, narrow=True)
    given = swap(theirs)
    last, mine, gating = lax.optimization_barrier((last, mine, gating))
    right = call(
        functools.partial(last_right, s),
        shape((width, s.slots, hidden), BF16),
        [padded, partner],
        0,
        *shared,
        last,
    )
    swapped = swap(right)
    left = call(functools.partial(last_left, s), sums, [], 0, *shared, last)
    update = call(
        functools.partial(finish, s),
        shape((width, height, channels), BF16),
        [partner, pltpu.VMEM(sums.shape, F32)],
        width * product,
        left,
        right,
        swapped,
        mine,
        given,
        *gating,
    )
    return jnp.transpose(update, (1, 0, 2))


def solution(mesh):
    return jax.shard_map(
        functools.partial(local, mesh),
        mesh=mesh,
        in_specs=(P(("parts", "row"), "col", None), P("parts")) + (P(),) * 8,
        out_specs=P(("parts", "row"), "col", None),
        check_vma=False,
    )
```

```python
import functools

import jax
import jax.numpy as jnp
from jax import lax
from jax.experimental import pallas as pl
from jax.experimental.pallas import tpu as pltpu
from jax.sharding import PartitionSpec as P

F32 = jnp.float32
BF16 = jnp.bfloat16
EPS = 1e-05
TILE = 16
CHUNK = 56
GROUP = 7


class Sizes:
    def __init__(self, mesh, height, width, channels, hidden):
        self.rows = mesh.shape["row"]
        self.cols = mesh.shape["col"]
        self.height, self.width = height, width
        self.channels, self.hidden = channels, hidden
        self.half = width // 2
        self.slots = -(-width // TILE) * TILE


def column_at(place, cols):
    return jnp.where(place < cols // 2, 2 * place, 2 * (cols - place) - 1)


def place_of(column, cols):
    return jnp.where(column % 2 == 0, column // 2, cols - 1 - column // 2)


def ring(cols):
    return [2 * at if at < cols // 2 else 2 * (cols - at) - 1 for at in range(cols)]


def normalise(values):
    average = jnp.mean(values, -1, keepdims=True)
    centered = values - average
    variance = jnp.mean(centered * centered, -1, keepdims=True)
    return centered * lax.rsqrt(variance + EPS)


def sigmoid(values):
    return 0.5 * jnp.tanh(0.5 * values) + 0.5


def dot(left, right):
    return jnp.dot(left, right, preferred_element_type=F32)


def gate(s, length, shared, pair, out_gate, last_gain, last_weight, gating, kept_gain, kept_weight):
    gain = Shared(s, length, shared).gain
    kept_gain[...] = last_gain[...]
    kept_weight[...] = last_weight[...]
    for start in range(0, s.width, s.half):
        normed = [
            normalise(pair[start + step].astype(F32)) * gain for step in range(s.half)
        ]
        value = sigmoid(dot(jnp.concatenate(normed, 0).astype(BF16), out_gate[...]))
        for step in range(s.half):
            gating[start + step] = value[step * s.height : (step + 1) * s.height]


def accumulate(s, left, partner, before, total):
    depth = left.shape[0]
    size = CHUNK if s.height % CHUNK == 0 else s.height
    group = GROUP if s.width % GROUP == 0 else 1

    def chunk(index, carry):
        at = pl.ds(pl.multiple_of(index * size, 8), size)
        for first in range(0, s.width, group):
            members = range(first, first + group)
            if before is None:
                sums = tuple(jnp.zeros((size, s.hidden), F32) for _ in members)
            else:
                sums = tuple(before[j, at] for j in members)

            def step(k, sums):
                value = left[k, at]
                return tuple(
                    so_far + value * partner[k, j : j + 1] for so_far, j in zip(sums, members)
                )

            sums = lax.fori_loop(0, depth, step, sums, unroll=s.half)
            for so_far, j in zip(sums, members):
                total[j, at] = so_far
        return carry

    lax.fori_loop(0, s.height // size, chunk, 0)


def owner_of(s, col):
    return col // (s.height // s.width)


def choose(first, one, other, target):
    @pl.when(first)
    def _():
        target[...] = one[...].astype(F32)

    @pl.when(jnp.logical_not(first))
    def _():
        target[...] = other[...].astype(F32)


def offset_in(s, col):
    return (col % (s.height // s.width)) * s.width


def column_from(s, distance):
    row, col = lax.axis_index("row"), lax.axis_index("col")
    step = distance * (2 * row - 1)
    return column_at((place_of(col, s.cols) + step + s.cols) % s.cols, s.cols)


class Shared:
    def __init__(self, s, length, ref):
        h = s.hidden
        self.left = ref[: s.channels, : 2 * h].astype(BF16)
        self.right = ref[: s.channels, 2 * h :].astype(BF16)
        self.gain = ref[s.channels : s.channels + 1, : s.channels]
        self.limit = length[0]


def join(s, gain, left_gate, left_value, right_gate, right_value, shared):
    h = s.hidden
    for at, part in enumerate((left_gate, left_value, right_gate, right_value)):
        shared[: s.channels, at * h : (at + 1) * h] = 0.5 * part[...].astype(F32)
    shared[s.channels : s.channels + 1, : s.channels] = gain[...]


def gated(s, rows, gain, weight, masks):
    h, size = s.hidden, rows[0].shape[0]
    rows = [normalise(row) * gain for row in rows]
    out = dot(jnp.concatenate(rows, 0).astype(BF16), weight)
    value = (jnp.tanh(out[:, :h]) + 1.0) * out[:, h:]
    return [value[at * size : (at + 1) * size] * mask for at, mask in enumerate(masks)]


def masks_of(tokens, first, count, limit):
    below = lax.broadcasted_iota(jnp.int32, (count, 1), 0) + first < limit
    return [(below & (token < limit)).astype(F32) for token in tokens]


def project_right(s, rows_of, base, depth, token, shared, partner):
    first = lax.axis_index("col") * s.width
    for start in range(0, depth, s.half):
        steps = range(start, start + s.half)
        masks = masks_of([token + step for step in steps], first, s.slots, shared.limit)
        rows = [rows_of(base + step) for step in steps]
        for step, part in zip(steps, gated(s, rows, shared.gain, shared.right, masks)):
            partner[step] = part


def project_left(s, block, row, base, depth, token, shared, left):
    first = row * s.height
    for start in range(0, depth, s.half):
        steps = range(start, start + s.half)
        masks = masks_of([token + step for step in steps], first, s.height, shared.limit)
        rows = [block[base + step].astype(F32) for step in steps]
        for step, part in zip(steps, gated(s, rows, shared.gain, shared.left, masks)):
            left[step] = part


def add_both(s, distance, narrow, length, shared, own, other, *refs):
    before, (mine, theirs, left, right, picked, partner) = refs[:-6], refs[-6:]
    row, col = lax.axis_index("row"), lax.axis_index("col")
    shared = Shared(s, length, shared)
    depth = left.shape[0]
    base = row * s.half if distance == 0 else 0
    token = column_from(s, distance) * s.width + base
    choose(row == owner_of(s, col), own, other, picked.at[:, : s.height])

    def rows_of(at):
        return picked[at, pl.ds(offset_in(s, col), s.slots), :]

    project_right(s, rows_of, base, depth, token, shared, partner)
    project_left(s, own, row, base, depth, token, shared, left)
    project_left(s, other, 1 - row, base, depth, token, shared, right)
    old_mine, old_theirs = before if before else (None, None)
    accumulate(s, left, partner, old_mine, mine)
    if not narrow:
        accumulate(s, right, partner, old_theirs, theirs)
    else:
        accumulate(s, right, partner, old_theirs, picked)
        theirs[...] = picked[:, : s.height].astype(BF16)


def last_right(s, length, shared, own, right, picked, partner):
    shared = Shared(s, length, shared)
    picked[:, : s.height] = own[...].astype(F32)
    offset = offset_in(s, lax.axis_index("col"))
    token = column_from(s, s.cols // 2) * s.width

    def rows_of(at):
        return picked[at, pl.ds(offset, s.slots), :]

    project_right(s, rows_of, 0, s.width, token, shared, partner)
    right[...] = partner[...].astype(BF16)


def last_left(s, length, shared, own, left):
    shared = Shared(s, length, shared)
    token = column_from(s, s.cols // 2) * s.width
    project_left(s, own, lax.axis_index("row"), 0, s.width, token, shared, left)


def finish(s, left, right, other, mine, given, gating, last_gain, last_weight, *refs):
    update, partner, total = refs
    choose(lax.axis_index("row") == owner_of(s, lax.axis_index("col")), right, other, partner)
    accumulate(s, left, partner, mine, total)
    for start in range(0, s.width, s.half):
        settled = [
            normalise(total[start + step] + given[start + step].astype(F32)) * last_gain[...]
            for step in range(s.half)
        ]
        value = dot(jnp.concatenate(settled, 0).astype(BF16), last_weight[...])
        for step in range(s.half):
            part = gating[start + step] * value[step * s.height : (step + 1) * s.height]
            update[start + step] = part.astype(BF16)


def call(body, out_shape, scratch, flops, *operands, grant=24):
    def space(operand):
        return pl.BlockSpec(memory_space=pltpu.SMEM if operand.dtype == jnp.int32 else pltpu.VMEM)

    sent = sum(o.size * o.dtype.itemsize for o in operands)
    return pl.pallas_call(
        body,
        out_shape=out_shape,
        in_specs=[space(o) for o in operands],
        out_specs=jax.tree.map(lambda _: pl.BlockSpec(memory_space=pltpu.VMEM), out_shape),
        scratch_shapes=scratch,
        compiler_params=pltpu.CompilerParams(vmem_limit_bytes=grant * 1024 * 1024),
        cost_estimate=pl.CostEstimate(flops=flops, bytes_accessed=sent, transcendentals=0),
        name=body.func.__name__,
    )(*operands)


def local(
    mesh,
    pair_state,
    valid_length,
    input_gain,
    left_gate,
    left_value,
    right_gate,
    right_value,
    out_gate,
    output_gain,
    out_weight,
):
    height, width, channels = pair_state.shape
    hidden = left_gate.shape[1]
    s = Sizes(mesh, height, width, channels, hidden)
    shape = jax.ShapeDtypeStruct
    pair = jnp.transpose(pair_state, (1, 0, 2))
    gain = input_gain.reshape(1, channels)
    shared = call(
        functools.partial(join, s),
        shape((channels + 8, 4 * hidden), F32),
        [],
        0,
        gain,
        left_gate,
        left_value,
        right_gate,
        right_value,
        grant=56,
    )
    shared = (valid_length, shared)
    order = ring(s.cols)

    def shift(block, crossed=False, by=1):
        pairs = []
        for row in range(s.rows):
            target = s.rows - 1 - row if crossed else row
            for at in range(s.cols):
                to = (at + by * (1 - 2 * target)) % s.cols
                pairs.append((row * s.cols + order[at], target * s.cols + order[to]))
        return lax.ppermute(block, ("row", "col"), pairs)

    def swap(block):
        return lax.ppermute(block, "row", [(at, (at + 1) % s.rows) for at in range(s.rows)])

    sums = shape((width, height, hidden), F32)
    product = 16 * height * width * hidden
    tokens = pltpu.VMEM((width, height, hidden), F32)
    halved = pltpu.VMEM((s.half, height, hidden), F32)
    padded = pltpu.VMEM((width, height + TILE, channels), F32)
    partner = pltpu.VMEM((width, s.slots, hidden), F32)
    few = pltpu.VMEM((s.half, s.slots, hidden), F32)

    def add(distance, own, other, before, narrow=False):
        left, right = (halved, few) if distance == 0 else (tokens, partner)
        return call(
            functools.partial(add_both, s, distance, narrow),
            [sums, shape(sums.shape, BF16) if narrow else sums],
            [left, left, padded, right],
            2 * left.shape[0] * product,
            *shared,
            own,
            other,
            *before,
        )

    def in_turn(other, own, done):
        own = lax.optimization_barrier((own, done))[0]
        return lax.optimization_barrier((other, own))[0], own

    far = s.cols // 2
    given = swap(pair)
    other = shift(pair, crossed=True)
    own = shift(pair)
    total = add(0, pair, given, ())
    other, own = in_turn(other, own, total)
    for distance in range(1, far - 1):
        ahead = [shift(other), shift(own)]
        if distance == 1:
            gating = call(
                functools.partial(gate, s),
                [sums, shape((1, hidden), F32), shape(out_weight.shape, BF16)],
                [],
                2 * height * width * channels * channels,
                *shared,
                pair,
                out_gate,
                output_gain.reshape(1, hidden),
                out_weight,
            )
        total = add(distance, own, other, total)
        other, own = in_turn(*ahead, (total, gating))
    last = shift(own)
    mine, theirs = add(far - 1, own, other, total, narrow=True)
    given = swap(theirs)
    last, mine, gating = lax.optimization_barrier((last, mine, gating))
    right = call(
        functools.partial(last_right, s),
        shape((width, s.slots, hidden), BF16),
        [padded, partner],
        0,
        *shared,
        last,
    )
    swapped = swap(right)
    left = call(functools.partial(last_left, s), sums, [], 0, *shared, last)
    update = call(
        functools.partial(finish, s),
        shape((width, height, channels), BF16),
        [partner, pltpu.VMEM(sums.shape, F32)],
        width * product,
        left,
        right,
        swapped,
        mine,
        given,
        *gating,
    )
    return jnp.transpose(update, (1, 0, 2))


def solution(mesh):
    return jax.shard_map(
        functools.partial(local, mesh),
        mesh=mesh,
        in_specs=(P(("parts", "row"), "col", None), P("parts")) + (P(),) * 8,
        out_specs=P(("parts", "row"), "col", None),
        check_vma=False,
    )
```

```python
import functools

import jax
import jax.numpy as jnp
from jax import lax
from jax.experimental import pallas as pl
from jax.experimental.pallas import tpu as pltpu
from jax.sharding import PartitionSpec as P

F32 = jnp.float32
BF16 = jnp.bfloat16
EPS = 1e-05
TILE = 16
CHUNK = 56
GROUP = 7


class Sizes:
    def __init__(self, mesh, height, width, channels, hidden):
        self.rows = mesh.shape["row"]
        self.cols = mesh.shape["col"]
        self.height, self.width = height, width
        self.channels, self.hidden = channels, hidden
        self.half = width // 2
        self.slots = -(-width // TILE) * TILE


def column_at(place, cols):
    return jnp.where(place < cols // 2, 2 * place, 2 * (cols - place) - 1)


def place_of(column, cols):
    return jnp.where(column % 2 == 0, column // 2, cols - 1 - column // 2)


def ring(cols):
    return [2 * at if at < cols // 2 else 2 * (cols - at) - 1 for at in range(cols)]


def normalise(values):
    average = jnp.mean(values, -1, keepdims=True)
    centered = values - average
    variance = jnp.mean(centered * centered, -1, keepdims=True)
    return centered * lax.rsqrt(variance + EPS)


def sigmoid(values):
    return 0.5 * jnp.tanh(0.5 * values) + 0.5


def dot(left, right):
    return jnp.dot(left, right, preferred_element_type=F32)


def gate(s, length, shared, pair, out_gate, last_gain, last_weight, gating, kept_gain, kept_weight):
    gain = Shared(s, length, shared).gain
    kept_gain[...] = last_gain[...]
    kept_weight[...] = last_weight[...]
    for start in range(0, s.width, s.half):
        normed = [
            normalise(pair[start + step].astype(F32)) * gain for step in range(s.half)
        ]
        value = sigmoid(dot(jnp.concatenate(normed, 0).astype(BF16), out_gate[...]))
        for step in range(s.half):
            gating[start + step] = value[step * s.height : (step + 1) * s.height]


def accumulate(s, left, partner, before, total):
    depth = left.shape[0]
    size = CHUNK if s.height % CHUNK == 0 else s.height
    group = GROUP if s.width % GROUP == 0 else 1

    def chunk(index, carry):
        at = pl.ds(pl.multiple_of(index * size, 8), size)
        for first in range(0, s.width, group):
            members = range(first, first + group)
            if before is None:
                sums = tuple(jnp.zeros((size, s.hidden), F32) for _ in members)
            else:
                sums = tuple(before[j, at] for j in members)

            def step(k, sums):
                value = left[k, at]
                return tuple(
                    so_far + value * partner[k, j : j + 1] for so_far, j in zip(sums, members)
                )

            sums = lax.fori_loop(0, depth, step, sums, unroll=s.half)
            for so_far, j in zip(sums, members):
                total[j, at] = so_far
        return carry

    lax.fori_loop(0, s.height // size, chunk, 0)


def owner_of(s, col):
    return col // (s.height // s.width)


def choose(first, one, other, target):
    @pl.when(first)
    def _():
        target[...] = one[...].astype(F32)

    @pl.when(jnp.logical_not(first))
    def _():
        target[...] = other[...].astype(F32)


def offset_in(s, col):
    return (col % (s.height // s.width)) * s.width


def column_from(s, distance):
    row, col = lax.axis_index("row"), lax.axis_index("col")
    step = distance * (2 * row - 1)
    return column_at((place_of(col, s.cols) + step + s.cols) % s.cols, s.cols)


class Shared:
    def __init__(self, s, length, ref):
        h = s.hidden
        self.left = ref[: s.channels, : 2 * h].astype(BF16)
        self.right = ref[: s.channels, 2 * h :].astype(BF16)
        self.gain = ref[s.channels : s.channels + 1, : s.channels]
        self.limit = length[0]


def join(s, gain, left_gate, left_value, right_gate, right_value, shared):
    h = s.hidden
    for at, part in enumerate((left_gate, left_value, right_gate, right_value)):
        shared[: s.channels, at * h : (at + 1) * h] = part[...].astype(F32)
    shared[s.channels : s.channels + 1, : s.channels] = gain[...]


def gated(s, rows, gain, weight, masks):
    h, size = s.hidden, rows[0].shape[0]
    rows = [normalise(row) * gain for row in rows]
    out = dot(jnp.concatenate(rows, 0).astype(BF16), weight)
    value = sigmoid(out[:, :h]) * out[:, h:]
    return [value[at * size : (at + 1) * size] * mask for at, mask in enumerate(masks)]


def masks_of(tokens, first, count, limit):
    below = lax.broadcasted_iota(jnp.int32, (count, 1), 0) + first < limit
    return [(below & (token < limit)).astype(F32) for token in tokens]


def project_right(s, rows_of, base, depth, token, shared, partner):
    first = lax.axis_index("col") * s.width
    for start in range(0, depth, s.half):
        steps = range(start, start + s.half)
        masks = masks_of([token + step for step in steps], first, s.slots, shared.limit)
        rows = [rows_of(base + step) for step in steps]
        for step, part in zip(steps, gated(s, rows, shared.gain, shared.right, masks)):
            partner[step] = part


def project_left(s, block, row, base, depth, token, shared, left):
    first = row * s.height
    for start in range(0, depth, s.half):
        steps = range(start, start + s.half)
        masks = masks_of([token + step for step in steps], first, s.height, shared.limit)
        rows = [block[base + step].astype(F32) for step in steps]
        for step, part in zip(steps, gated(s, rows, shared.gain, shared.left, masks)):
            left[step] = part


def add_both(s, distance, narrow, length, shared, own, other, *refs):
    before, (mine, theirs, left, right, picked, partner) = refs[:-6], refs[-6:]
    row, col = lax.axis_index("row"), lax.axis_index("col")
    shared = Shared(s, length, shared)
    depth = left.shape[0]
    token = column_from(s, distance) * s.width
    choose(row == owner_of(s, col), own, other, picked.at[:, : s.height])

    def rows_of(at):
        return picked[at, pl.ds(offset_in(s, col), s.slots), :]

    project_right(s, rows_of, 0, depth, token, shared, partner)
    project_left(s, own, row, 0, depth, token, shared, left)
    project_left(s, other, 1 - row, 0, depth, token, shared, right)
    old_mine, old_theirs = before if before else (None, None)
    accumulate(s, left, partner, old_mine, mine)
    if not narrow:
        accumulate(s, right, partner, old_theirs, theirs)
    else:
        accumulate(s, right, partner, old_theirs, picked)
        theirs[...] = picked[:, : s.height].astype(BF16)


def own_right(s, distance, length, shared, own, right, picked, partner):
    shared = Shared(s, length, shared)
    picked[:, : s.height] = own[...].astype(F32)
    offset = offset_in(s, lax.axis_index("col"))
    token = column_from(s, distance) * s.width

    def rows_of(at):
        return picked[at, pl.ds(offset, s.slots), :]

    project_right(s, rows_of, 0, s.width, token, shared, partner)
    right[...] = partner[...].astype(BF16)


def own_left(s, distance, length, shared, own, left):
    shared = Shared(s, length, shared)
    token = column_from(s, distance) * s.width
    project_left(s, own, lax.axis_index("row"), 0, s.width, token, shared, left)


def add_own(s, left, right, other, before, mine, partner):
    choose(lax.axis_index("row") == owner_of(s, lax.axis_index("col")), right, other, partner)
    accumulate(s, left, partner, before, mine)


def finish(s, left, right, other, mine, given, gating, last_gain, last_weight, *refs):
    update, partner, total = refs
    choose(lax.axis_index("row") == owner_of(s, lax.axis_index("col")), right, other, partner)
    accumulate(s, left, partner, mine, total)
    for start in range(0, s.width, s.half):
        settled = [
            normalise(total[start + step] + given[start + step].astype(F32)) * last_gain[...]
            for step in range(s.half)
        ]
        value = dot(jnp.concatenate(settled, 0).astype(BF16), last_weight[...])
        for step in range(s.half):
            part = gating[start + step] * value[step * s.height : (step + 1) * s.height]
            update[start + step] = part.astype(BF16)


def call(body, out_shape, scratch, flops, *operands, grant=24):
    def space(operand):
        return pl.BlockSpec(memory_space=pltpu.SMEM if operand.dtype == jnp.int32 else pltpu.VMEM)

    sent = sum(o.size * o.dtype.itemsize for o in operands)
    return pl.pallas_call(
        body,
        out_shape=out_shape,
        in_specs=[space(o) for o in operands],
        out_specs=jax.tree.map(lambda _: pl.BlockSpec(memory_space=pltpu.VMEM), out_shape),
        scratch_shapes=scratch,
        compiler_params=pltpu.CompilerParams(vmem_limit_bytes=grant * 1024 * 1024),
        cost_estimate=pl.CostEstimate(flops=flops, bytes_accessed=sent, transcendentals=0),
        name=body.func.__name__,
    )(*operands)


def local(
    mesh,
    pair_state,
    valid_length,
    input_gain,
    left_gate,
    left_value,
    right_gate,
    right_value,
    out_gate,
    output_gain,
    out_weight,
):
    height, width, channels = pair_state.shape
    hidden = left_gate.shape[1]
    s = Sizes(mesh, height, width, channels, hidden)
    shape = jax.ShapeDtypeStruct
    pair = jnp.transpose(pair_state, (1, 0, 2))
    gain = input_gain.reshape(1, channels)
    shared = call(
        functools.partial(join, s),
        shape((channels + 8, 4 * hidden), F32),
        [],
        0,
        gain,
        left_gate,
        left_value,
        right_gate,
        right_value,
        grant=56,
    )
    shared = (valid_length, shared)
    order = ring(s.cols)

    def shift(block, crossed=False, by=1):
        pairs = []
        for row in range(s.rows):
            target = s.rows - 1 - row if crossed else row
            for at in range(s.cols):
                to = (at + by * (1 - 2 * target)) % s.cols
                pairs.append((row * s.cols + order[at], target * s.cols + order[to]))
        return lax.ppermute(block, ("row", "col"), pairs)

    def swap(block):
        return lax.ppermute(block, "row", [(at, (at + 1) % s.rows) for at in range(s.rows)])

    sums = shape((width, height, hidden), F32)
    product = 16 * height * width * hidden
    tokens = pltpu.VMEM((width, height, hidden), F32)
    padded = pltpu.VMEM((width, height + TILE, channels), F32)
    partner = pltpu.VMEM((width, s.slots, hidden), F32)

    def add(distance, own, other, before, narrow=False):
        return call(
            functools.partial(add_both, s, distance, narrow),
            [sums, shape(sums.shape, BF16) if narrow else sums],
            [tokens, tokens, padded, partner],
            2 * width * product,
            *shared,
            own,
            other,
            *before,
        )

    def in_turn(other, own, done):
        own = lax.optimization_barrier((own, done))[0]
        return lax.optimization_barrier((other, own))[0], own

    far = s.cols // 2
    def right_of(distance, block):
        out = shape((width, s.slots, hidden), BF16)
        body = functools.partial(own_right, s, distance)
        return call(body, out, [padded, partner], 0, *shared, block)

    def left_of(distance, block):
        return call(functools.partial(own_left, s, distance), sums, [], 0, *shared, block)

    other = shift(pair, crossed=True)
    own = shift(pair)
    right = right_of(0, pair)
    swapped = swap(right)
    other, own = in_turn(other, own, right)
    total = ()
    for distance in range(1, far - 1):
        ahead = [shift(other), shift(own)]
        if distance == 1:
            left = left_of(0, pair)
            gating = call(
                functools.partial(gate, s),
                [sums, shape((1, hidden), F32), shape(out_weight.shape, BF16)],
                [],
                2 * height * width * channels * channels,
                *shared,
                pair,
                out_gate,
                output_gain.reshape(1, hidden),
                out_weight,
            )
        elif distance == 2:
            mine = call(
                functools.partial(add_own, s),
                sums,
                [partner],
                width * product,
                left,
                right,
                swapped,
                lax.optimization_barrier((total[0], own))[0],
            )
            total = mine, total[1]
        total = add(distance, own, other, total)
        other, own = in_turn(*ahead, (total, gating))
    last = shift(own)
    mine, theirs = add(far - 1, own, other, total, narrow=True)
    given = swap(theirs)
    last, mine, gating = lax.optimization_barrier((last, mine, gating))
    right = right_of(far, last)
    swapped = swap(right)
    left = left_of(far, last)
    update = call(
        functools.partial(finish, s),
        shape((width, height, channels), BF16),
        [partner, pltpu.VMEM(sums.shape, F32)],
        width * product,
        left,
        right,
        swapped,
        mine,
        given,
        *gating,
    )
    return jnp.transpose(update, (1, 0, 2))


def solution(mesh):
    return jax.shard_map(
        functools.partial(local, mesh),
        mesh=mesh,
        in_specs=(P(("parts", "row"), "col", None), P("parts")) + (P(),) * 8,
        out_specs=P(("parts", "row"), "col", None),
        check_vma=False,
    )
```

```python
import functools

import jax
import jax.numpy as jnp
from jax import lax
from jax.experimental import pallas as pl
from jax.experimental.pallas import tpu as pltpu
from jax.sharding import PartitionSpec as P

F32 = jnp.float32
BF16 = jnp.bfloat16
EPS = 1e-05
TILE = 16
CHUNK = 56
GROUP = 7


class Sizes:
    def __init__(self, mesh, height, width, channels, hidden):
        self.rows = mesh.shape["row"]
        self.cols = mesh.shape["col"]
        self.height, self.width = height, width
        self.channels, self.hidden = channels, hidden
        self.half = width // 2
        self.slots = -(-width // TILE) * TILE
        self.both = 2 * width


def normalise(values):
    average = jnp.mean(values, -1, keepdims=True)
    centered = values - average
    variance = jnp.mean(centered * centered, -1, keepdims=True)
    return centered * lax.rsqrt(variance + EPS)


def sigmoid(values):
    return 0.5 * jnp.tanh(0.5 * values) + 0.5


def dot(left, right):
    return jnp.dot(left, right, preferred_element_type=F32)


def gate(s, length, shared, pair, out_gate, last_gain, last_weight, gating, kept_gain, kept_weight):
    gain = Shared(s, length, shared).gain
    kept_gain[...] = last_gain[...]
    kept_weight[...] = last_weight[...]
    for start in range(0, s.width, s.half):
        normed = [
            normalise(pair[start + step].astype(F32)) * gain for step in range(s.half)
        ]
        value = sigmoid(dot(jnp.concatenate(normed, 0).astype(BF16), out_gate[...]))
        for step in range(s.half):
            gating[start + step] = value[step * s.height : (step + 1) * s.height]


def accumulate(s, left, partner, shift, before, total):
    depth = left.shape[0]
    size = CHUNK if s.height % CHUNK == 0 else s.height
    group = GROUP if s.width % GROUP == 0 else 1

    def chunk(index, carry):
        at = pl.ds(pl.multiple_of(index * size, 8), size)
        for first in range(0, s.width, group):
            members = range(first, first + group)
            if before is None:
                sums = tuple(jnp.zeros((size, s.hidden), F32) for _ in members)
            else:
                sums = tuple(before[j, at] for j in members)

            def step(k, sums):
                value = left[k, at]
                return tuple(
                    so_far + value * partner[k, shift + j : shift + j + 1] for so_far, j in zip(sums, members)
                )

            sums = lax.fori_loop(0, depth, step, sums, unroll=s.half)
            for so_far, j in zip(sums, members):
                total[j, at] = so_far
        return carry

    lax.fori_loop(0, s.height // size, chunk, 0)


def split(s):
    col = lax.axis_index("col")
    return col // 2, col % 2


def choose(s, right, other, partner):
    hi, _ = split(s)
    mine = lax.axis_index("row") == hi // (s.height // s.both)

    @pl.when(mine)
    def _():
        partner[...] = right[...].astype(F32)

    @pl.when(jnp.logical_not(mine))
    def _():
        partner[...] = other[...].astype(F32)


class Shared:
    def __init__(self, s, length, ref):
        h = s.hidden
        self.left = ref[: s.channels, : 2 * h].astype(BF16)
        self.right = ref[: s.channels, 2 * h :].astype(BF16)
        self.gain = ref[s.channels : s.channels + 1, : s.channels]
        self.limit = length[0]


def join(s, gain, left_gate, left_value, right_gate, right_value, shared):
    h = s.hidden
    for at, part in enumerate((left_gate, left_value, right_gate, right_value)):
        shared[: s.channels, at * h : (at + 1) * h] = part[...].astype(F32)
    shared[s.channels : s.channels + 1, : s.channels] = gain[...]


def gated(s, rows, gain, weight, masks):
    h, size = s.hidden, rows[0].shape[0]
    rows = [normalise(row) * gain for row in rows]
    out = dot(jnp.concatenate(rows, 0).astype(BF16), weight)
    value = sigmoid(out[:, :h]) * out[:, h:]
    return [value[at * size : (at + 1) * size] * mask for at, mask in enumerate(masks)]


def masks_of(tokens, first, count, limit):
    below = lax.broadcasted_iota(jnp.int32, (count, 1), 0) + first < limit
    return [(below & (token < limit)).astype(F32) for token in tokens]


def project_left(s, block, row, base, depth, token, shared, left):
    first = row * s.height
    for start in range(0, depth, s.half):
        steps = range(start, start + s.half)
        masks = masks_of([token + step for step in steps], first, s.height, shared.limit)
        rows = [block[base + step].astype(F32) for step in steps]
        for step, part in zip(steps, gated(s, rows, shared.gain, shared.left, masks)):
            left[step] = part


def project(s, mask, length, shared, block, left, right, picked):
    hi, lo = split(s)
    shared = Shared(s, length, shared)
    token = ((hi ^ mask) * 2 + lo) * s.width
    project_left(s, block, lax.axis_index("row"), 0, s.width, token, shared, left)
    picked[:, : s.height] = block[...].astype(F32)
    offset = (hi % (s.height // s.both)) * s.both
    for side, which in enumerate((lo, 1 - lo)):
        first = hi * s.both + which * s.width
        place = pl.ds(offset + which * s.width, s.slots)
        for start in range(0, s.width, s.half):
            steps = range(start, start + s.half)
            masks = masks_of([token + step for step in steps], first, s.slots, shared.limit)
            rows = [picked[step, place, :] for step in steps]
            for step, part in zip(steps, gated(s, rows, shared.gain, shared.right, masks)):
                right[step, side * s.slots : (side + 1) * s.slots] = part.astype(BF16)


def add(s, left, right, other, *refs):
    *before, mine, theirs, partner = refs
    choose(s, right, other, partner)
    old_mine, old_theirs = before if before else (None, None)
    accumulate(s, left, partner, 0, old_mine, mine)
    accumulate(s, left, partner, s.slots, old_theirs, theirs)


def add_theirs(s, left, right, other, before, theirs, partner, total):
    choose(s, right, other, partner)
    accumulate(s, left, partner, s.slots, before, total)
    theirs[...] = total[...].astype(BF16)


def add_mine(s, left, right, other, before, mine, partner):
    choose(s, right, other, partner)
    accumulate(s, left, partner, 0, before, mine)


def finish(s, mine, given, gating, last_gain, last_weight, update):
    for start in range(0, s.width, s.half):
        settled = [
            normalise(mine[start + step] + given[start + step].astype(F32)) * last_gain[...]
            for step in range(s.half)
        ]
        value = dot(jnp.concatenate(settled, 0).astype(BF16), last_weight[...])
        for step in range(s.half):
            part = gating[start + step] * value[step * s.height : (step + 1) * s.height]
            update[start + step] = part.astype(BF16)


def call(body, out_shape, scratch, flops, *operands, grant=24):
    def space(operand):
        return pl.BlockSpec(memory_space=pltpu.SMEM if operand.dtype == jnp.int32 else pltpu.VMEM)

    sent = sum(o.size * o.dtype.itemsize for o in operands)
    return pl.pallas_call(
        body,
        out_shape=out_shape,
        in_specs=[space(o) for o in operands],
        out_specs=jax.tree.map(lambda _: pl.BlockSpec(memory_space=pltpu.VMEM), out_shape),
        scratch_shapes=scratch,
        compiler_params=pltpu.CompilerParams(vmem_limit_bytes=grant * 1024 * 1024),
        cost_estimate=pl.CostEstimate(flops=flops, bytes_accessed=sent, transcendentals=0),
        name=body.func.__name__,
    )(*operands)


def local(
    mesh,
    pair_state,
    valid_length,
    input_gain,
    left_gate,
    left_value,
    right_gate,
    right_value,
    out_gate,
    output_gain,
    out_weight,
):
    height, width, channels = pair_state.shape
    hidden = left_gate.shape[1]
    s = Sizes(mesh, height, width, channels, hidden)
    shape = jax.ShapeDtypeStruct
    pair = jnp.transpose(pair_state, (1, 0, 2))
    gain = input_gain.reshape(1, channels)
    shared = call(
        functools.partial(join, s),
        shape((channels + 8, 4 * hidden), F32),
        [],
        0,
        gain,
        left_gate,
        left_value,
        right_gate,
        right_value,
        grant=56,
    )
    shared = (valid_length, shared)
    def xor(block, mask):
        return lax.ppermute(block, "col", [(at, at ^ mask) for at in range(s.cols)])

    def swap(block):
        return lax.ppermute(block, "row", [(at, (at + 1) % s.rows) for at in range(s.rows)])

    sums = shape((width, height, hidden), F32)
    sent = shape(sums.shape, BF16)
    partner = pltpu.VMEM((width, 2 * s.slots, hidden), F32)
    picked = pltpu.VMEM((width, height + TILE, channels), F32)
    product = 16 * width * height * width * hidden

    blocks = [pair] + [xor(pair, 2 * mask) for mask in range(1, s.cols // 2)]
    total, terms = (), None
    for mask, block in enumerate(blocks):
        if total:
            block, total = lax.optimization_barrier((block, total))
        left, right = call(
            functools.partial(project, s, mask),
            [sums, shape((width, 2 * s.slots, hidden), BF16)],
            [picked],
            4 * width * height * channels * hidden,
            *shared,
            block,
        )
        before, terms = terms, (left, right, swap(right))
        if before:
            total = call(
                functools.partial(add, s), [sums, sums], [partner], 2 * product, *before, *total
            )
    theirs = call(
        functools.partial(add_theirs, s),
        sent,
        [partner, pltpu.VMEM(sums.shape, F32)],
        product,
        *terms,
        total[1],
    )
    given = xor(theirs, 1)
    mine = call(functools.partial(add_mine, s), sums, [partner], product, *terms, total[0])
    gating = call(
        functools.partial(gate, s),
        [sums, shape((1, hidden), F32), shape(out_weight.shape, BF16)],
        [],
        2 * height * width * channels * channels,
        *shared,
        pair,
        out_gate,
        output_gain.reshape(1, hidden),
        out_weight,
    )
    update = call(
        functools.partial(finish, s),
        shape((width, height, channels), BF16),
        [],
        2 * height * width * channels * hidden,
        mine,
        given,
        *gating,
    )
    return jnp.transpose(update, (1, 0, 2))


def solution(mesh):
    return jax.shard_map(
        functools.partial(local, mesh),
        mesh=mesh,
        in_specs=(P(("parts", "row"), "col", None), P("parts")) + (P(),) * 8,
        out_specs=P(("parts", "row"), "col", None),
        check_vma=False,
    )
```

```python
import functools

import jax
import jax.numpy as jnp
from jax import lax
from jax.experimental import pallas as pl
from jax.experimental.pallas import tpu as pltpu
from jax.sharding import PartitionSpec as P

F32 = jnp.float32
BF16 = jnp.bfloat16
EPS = 1e-05
TILE = 16
CHUNK = 56
GROUP = 7


class Sizes:
    def __init__(self, mesh, height, width, channels, hidden):
        self.rows = mesh.shape["row"]
        self.cols = mesh.shape["col"]
        self.height, self.width = height, width
        self.channels, self.hidden = channels, hidden
        self.half = width // 2
        self.slots = -(-width // TILE) * TILE


def column_at(place, cols):
    return jnp.where(place < cols // 2, 2 * place, 2 * (cols - place) - 1)


def place_of(column, cols):
    return jnp.where(column % 2 == 0, column // 2, cols - 1 - column // 2)


def ring(cols):
    return [2 * at if at < cols // 2 else 2 * (cols - at) - 1 for at in range(cols)]


def normalise(values):
    average = jnp.mean(values, -1, keepdims=True)
    centered = values - average
    variance = jnp.mean(centered * centered, -1, keepdims=True)
    return centered * lax.rsqrt(variance + EPS)


def sigmoid(values):
    return 0.5 * jnp.tanh(0.5 * values) + 0.5


def dot(left, right):
    return jnp.dot(left, right, preferred_element_type=F32)


def gate(s, length, shared, pair, out_gate, last_gain, last_weight, gating, kept_gain, kept_weight):
    gain = Shared(s, length, shared).gain
    kept_gain[...] = last_gain[...]
    kept_weight[...] = last_weight[...]
    for start in range(0, s.width, s.half):
        normed = [
            normalise(pair[start + step].astype(F32)) * gain for step in range(s.half)
        ]
        value = sigmoid(dot(jnp.concatenate(normed, 0).astype(BF16), out_gate[...]))
        for step in range(s.half):
            gating[start + step] = value[step * s.height : (step + 1) * s.height]


def accumulate(s, left, partner, before, total):
    depth = left.shape[0]
    size = CHUNK if s.height % CHUNK == 0 else s.height
    group = GROUP if s.width % GROUP == 0 else 1

    def chunk(index, carry):
        at = pl.ds(pl.multiple_of(index * size, 8), size)
        for first in range(0, s.width, group):
            members = range(first, first + group)
            if before is None:
                sums = tuple(jnp.zeros((size, s.hidden), F32) for _ in members)
            else:
                sums = tuple(before[j, at] for j in members)

            def step(k, sums):
                value = left[k, at]
                return tuple(
                    so_far + value * partner[k, j : j + 1] for so_far, j in zip(sums, members)
                )

            sums = lax.fori_loop(0, depth, step, sums, unroll=s.half)
            for so_far, j in zip(sums, members):
                total[j, at] = so_far
        return carry

    lax.fori_loop(0, s.height // size, chunk, 0)


def owner_of(s, col):
    return col // (s.height // s.width)


def choose(first, one, other, target):
    @pl.when(first)
    def _():
        target[...] = one[...].astype(F32)

    @pl.when(jnp.logical_not(first))
    def _():
        target[...] = other[...].astype(F32)


def offset_in(s, col):
    return (col % (s.height // s.width)) * s.width


def column_from(s, distance):
    row, col = lax.axis_index("row"), lax.axis_index("col")
    step = distance * (2 * row - 1)
    return column_at((place_of(col, s.cols) + step + s.cols) % s.cols, s.cols)


class Shared:
    def __init__(self, s, length, ref):
        h = s.hidden
        self.left = ref[: s.channels, : 2 * h].astype(BF16)
        self.right = ref[: s.channels, 2 * h :].astype(BF16)
        self.gain = ref[s.channels : s.channels + 1, : s.channels]
        self.limit = length[0]


def join(s, gain, left_gate, left_value, right_gate, right_value, shared):
    h = s.hidden
    for at, part in enumerate((left_gate, left_value, right_gate, right_value)):
        shared[: s.channels, at * h : (at + 1) * h] = part[...].astype(F32)
    shared[s.channels : s.channels + 1, : s.channels] = gain[...]


def gated(s, rows, gain, weight, masks):
    h, size = s.hidden, rows[0].shape[0]
    rows = [normalise(row) * gain for row in rows]
    out = dot(jnp.concatenate(rows, 0).astype(BF16), weight)
    value = sigmoid(out[:, :h]) * out[:, h:]
    return [value[at * size : (at + 1) * size] * mask for at, mask in enumerate(masks)]


def masks_of(tokens, first, count, limit):
    below = lax.broadcasted_iota(jnp.int32, (count, 1), 0) + first < limit
    return [(below & (token < limit)).astype(F32) for token in tokens]


def project_right(s, rows_of, base, depth, token, shared, partner):
    first = lax.axis_index("col") * s.width
    for start in range(0, depth, s.half):
        steps = range(start, start + s.half)
        masks = masks_of([token + step for step in steps], first, s.slots, shared.limit)
        rows = [rows_of(base + step) for step in steps]
        for step, part in zip(steps, gated(s, rows, shared.gain, shared.right, masks)):
            partner[step] = part


def project_left(s, block, row, base, depth, token, shared, left):
    first = row * s.height
    for start in range(0, depth, s.half):
        steps = range(start, start + s.half)
        masks = masks_of([token + step for step in steps], first, s.height, shared.limit)
        rows = [block[base + step].astype(F32) for step in steps]
        for step, part in zip(steps, gated(s, rows, shared.gain, shared.left, masks)):
            left[step] = part


def add_both(s, distance, narrow, length, shared, own, other, *refs):
    before, (mine, theirs, left, right, picked, partner) = refs[:-6], refs[-6:]
    row, col = lax.axis_index("row"), lax.axis_index("col")
    shared = Shared(s, length, shared)
    depth = left.shape[0]
    token = column_from(s, distance) * s.width
    choose(row == owner_of(s, col), own, other, picked.at[:, : s.height])

    def rows_of(at):
        return picked[at, pl.ds(offset_in(s, col), s.slots), :]

    project_right(s, rows_of, 0, depth, token, shared, partner)
    project_left(s, own, row, 0, depth, token, shared, left)
    project_left(s, other, 1 - row, 0, depth, token, shared, right)
    old_mine, old_theirs = before if before else (None, None)
    accumulate(s, left, partner, old_mine, mine)
    if not narrow:
        accumulate(s, right, partner, old_theirs, theirs)
    else:
        accumulate(s, right, partner, old_theirs, picked)
        theirs[...] = picked[:, : s.height].astype(BF16)


def own_right(s, distance, length, shared, own, right, picked, partner):
    shared = Shared(s, length, shared)
    picked[:, : s.height] = own[...].astype(F32)
    offset = offset_in(s, lax.axis_index("col"))
    token = column_from(s, distance) * s.width

    def rows_of(at):
        return picked[at, pl.ds(offset, s.slots), :]

    project_right(s, rows_of, 0, s.width, token, shared, partner)
    right[...] = partner[...].astype(BF16)


def own_left(s, distance, length, shared, own, left):
    shared = Shared(s, length, shared)
    token = column_from(s, distance) * s.width
    project_left(s, own, lax.axis_index("row"), 0, s.width, token, shared, left)


def add_own(s, left, right, other, before, mine, partner):
    choose(lax.axis_index("row") == owner_of(s, lax.axis_index("col")), right, other, partner)
    accumulate(s, left, partner, before, mine)


def finish(s, left, right, other, mine, given, gating, last_gain, last_weight, *refs):
    update, partner, total = refs
    choose(lax.axis_index("row") == owner_of(s, lax.axis_index("col")), right, other, partner)
    accumulate(s, left, partner, mine, total)
    for start in range(0, s.width, s.half):
        settled = [
            normalise(total[start + step] + given[start + step].astype(F32)) * last_gain[...]
            for step in range(s.half)
        ]
        value = dot(jnp.concatenate(settled, 0).astype(BF16), last_weight[...])
        for step in range(s.half):
            part = gating[start + step] * value[step * s.height : (step + 1) * s.height]
            update[start + step] = part.astype(BF16)


def call(body, out_shape, scratch, flops, *operands, grant=24):
    def space(operand):
        return pl.BlockSpec(memory_space=pltpu.SMEM if operand.dtype == jnp.int32 else pltpu.VMEM)

    sent = sum(o.size * o.dtype.itemsize for o in operands)
    return pl.pallas_call(
        body,
        out_shape=out_shape,
        in_specs=[space(o) for o in operands],
        out_specs=jax.tree.map(lambda _: pl.BlockSpec(memory_space=pltpu.VMEM), out_shape),
        scratch_shapes=scratch,
        compiler_params=pltpu.CompilerParams(vmem_limit_bytes=grant * 1024 * 1024),
        cost_estimate=pl.CostEstimate(flops=flops, bytes_accessed=sent, transcendentals=0),
        name=body.func.__name__,
    )(*operands)


def local(
    mesh,
    pair_state,
    valid_length,
    input_gain,
    left_gate,
    left_value,
    right_gate,
    right_value,
    out_gate,
    output_gain,
    out_weight,
):
    height, width, channels = pair_state.shape
    hidden = left_gate.shape[1]
    s = Sizes(mesh, height, width, channels, hidden)
    shape = jax.ShapeDtypeStruct
    pair = jnp.transpose(pair_state, (1, 0, 2))
    gain = input_gain.reshape(1, channels)
    shared = call(
        functools.partial(join, s),
        shape((channels + 8, 4 * hidden), F32),
        [],
        0,
        gain,
        left_gate,
        left_value,
        right_gate,
        right_value,
        grant=56,
    )
    shared = (valid_length, shared)
    order = ring(s.cols)

    def shift(block, crossed=False, by=1):
        pairs = []
        for row in range(s.rows):
            target = s.rows - 1 - row if crossed else row
            for at in range(s.cols):
                to = (at + by * (1 - 2 * target)) % s.cols
                pairs.append((row * s.cols + order[at], target * s.cols + order[to]))
        return lax.ppermute(block, ("row", "col"), pairs)

    def swap(block):
        return lax.ppermute(block, "row", [(at, (at + 1) % s.rows) for at in range(s.rows)])

    sums = shape((width, height, hidden), F32)
    product = 16 * height * width * hidden
    tokens = pltpu.VMEM((width, height, hidden), F32)
    padded = pltpu.VMEM((width, height + TILE, channels), F32)
    partner = pltpu.VMEM((width, s.slots, hidden), F32)

    def add(distance, own, other, before, narrow=False):
        return call(
            functools.partial(add_both, s, distance, narrow),
            [sums, shape(sums.shape, BF16) if narrow else sums],
            [tokens, tokens, padded, partner],
            2 * width * product,
            *shared,
            own,
            other,
            *before,
        )

    def in_turn(other, own, done):
        own = lax.optimization_barrier((own, done))[0]
        return lax.optimization_barrier((other, own))[0], own

    far = s.cols // 2
    def right_of(distance, block):
        out = shape((width, s.slots, hidden), BF16)
        body = functools.partial(own_right, s, distance)
        return call(body, out, [padded, partner], 0, *shared, block)

    def left_of(distance, block):
        return call(functools.partial(own_left, s, distance), sums, [], 0, *shared, block)

    other = shift(pair, crossed=True)
    own = shift(pair)
    right = right_of(0, pair)
    gating = call(
        functools.partial(gate, s),
        [sums, shape((1, hidden), F32), shape(out_weight.shape, BF16)],
        [],
        2 * height * width * channels * channels,
        *shared,
        pair,
        out_gate,
        output_gain.reshape(1, hidden),
        out_weight,
    )
    other, own = in_turn(other, own, (right, gating))
    total = ()
    for distance in range(1, far - 1):
        ahead = [shift(other), shift(own)]
        if distance == 1:
            left, swapped = left_of(0, pair), swap(lax.optimization_barrier((right, own))[0])
        elif distance == 2:
            mine = call(
                functools.partial(add_own, s),
                sums,
                [partner],
                width * product,
                left,
                right,
                swapped,
                lax.optimization_barrier((total[0], own))[0],
            )
            total = mine, total[1]
        total = add(distance, own, other, total)
        other, own = in_turn(*ahead, (total, left))
        if distance == 1:
            other, swapped = lax.optimization_barrier((other, swapped))
    last = shift(own)
    mine, theirs = add(far - 1, own, other, total, narrow=True)
    given = swap(theirs)
    last, mine, gating = lax.optimization_barrier((last, mine, gating))
    right = right_of(far, last)
    swapped = swap(right)
    left = left_of(far, last)
    update = call(
        functools.partial(finish, s),
        shape((width, height, channels), BF16),
        [partner, pltpu.VMEM(sums.shape, F32)],
        width * product,
        left,
        right,
        swapped,
        mine,
        given,
        *gating,
    )
    return jnp.transpose(update, (1, 0, 2))


def solution(mesh):
    return jax.shard_map(
        functools.partial(local, mesh),
        mesh=mesh,
        in_specs=(P(("parts", "row"), "col", None), P("parts")) + (P(),) * 8,
        out_specs=P(("parts", "row"), "col", None),
        check_vma=False,
    )
```

```python
import functools

import jax
import jax.numpy as jnp
from jax import lax
from jax.experimental import pallas as pl
from jax.experimental.pallas import tpu as pltpu
from jax.sharding import PartitionSpec as P

F32 = jnp.float32
BF16 = jnp.bfloat16
EPS = 1e-05
TILE = 16
CHUNK = 56
GROUP = 7


class Sizes:
    def __init__(self, mesh, height, width, channels, hidden):
        self.rows = mesh.shape["row"]
        self.cols = mesh.shape["col"]
        self.height, self.width = height, width
        self.channels, self.hidden = channels, hidden
        self.half = width // 2
        self.slots = -(-width // TILE) * TILE


def column_at(place, cols):
    return jnp.where(place < cols // 2, 2 * place, 2 * (cols - place) - 1)


def place_of(column, cols):
    return jnp.where(column % 2 == 0, column // 2, cols - 1 - column // 2)


def ring(cols):
    return [2 * at if at < cols // 2 else 2 * (cols - at) - 1 for at in range(cols)]


def normalise(values):
    average = jnp.mean(values, -1, keepdims=True)
    centered = values - average
    variance = jnp.mean(centered * centered, -1, keepdims=True)
    return centered * lax.rsqrt(variance + EPS)


def sigmoid(values):
    return 0.5 * jnp.tanh(0.5 * values) + 0.5


def dot(left, right):
    return jnp.dot(left, right, preferred_element_type=F32)


def gate(s, length, shared, pair, out_gate, last_gain, last_weight, gating, kept_gain, kept_weight):
    gain = Shared(s, length, shared).gain
    kept_gain[...] = last_gain[...]
    kept_weight[...] = last_weight[...]
    for start in range(0, s.width, s.half):
        normed = [
            normalise(pair[start + step].astype(F32)) * gain for step in range(s.half)
        ]
        value = sigmoid(dot(jnp.concatenate(normed, 0).astype(BF16), out_gate[...]))
        for step in range(s.half):
            gating[start + step] = value[step * s.height : (step + 1) * s.height]


def accumulate(s, left, partner, before, total):
    depth = left.shape[0]
    size = CHUNK if s.height % CHUNK == 0 else s.height
    group = GROUP if s.width % GROUP == 0 else 1

    def chunk(index, carry):
        at = pl.ds(pl.multiple_of(index * size, 8), size)
        for first in range(0, s.width, group):
            members = range(first, first + group)
            if before is None:
                sums = tuple(jnp.zeros((size, s.hidden), F32) for _ in members)
            else:
                sums = tuple(before[j, at] for j in members)

            def step(k, sums):
                value = left[k, at]
                return tuple(
                    so_far + value * partner[k, j : j + 1] for so_far, j in zip(sums, members)
                )

            sums = lax.fori_loop(0, depth, step, sums, unroll=s.half)
            for so_far, j in zip(sums, members):
                total[j, at] = so_far
        return carry

    lax.fori_loop(0, s.height // size, chunk, 0)


def owner_of(s, col):
    return col // (s.height // s.width)


def choose(first, one, other, target):
    @pl.when(first)
    def _():
        target[...] = one[...].astype(F32)

    @pl.when(jnp.logical_not(first))
    def _():
        target[...] = other[...].astype(F32)


def offset_in(s, col):
    return (col % (s.height // s.width)) * s.width


def column_from(s, distance):
    row, col = lax.axis_index("row"), lax.axis_index("col")
    step = distance * (2 * row - 1)
    return column_at((place_of(col, s.cols) + step + s.cols) % s.cols, s.cols)


class Shared:
    def __init__(self, s, length, ref):
        h = s.hidden
        self.left = ref[: s.channels, : 2 * h].astype(BF16)
        self.right = ref[: s.channels, 2 * h :].astype(BF16)
        self.gain = ref[s.channels : s.channels + 1, : s.channels]
        self.limit = length[0]


def join(s, gain, left_gate, left_value, right_gate, right_value, shared):
    h = s.hidden
    for at, part in enumerate((left_gate, left_value, right_gate, right_value)):
        shared[: s.channels, at * h : (at + 1) * h] = part[...].astype(F32)
    shared[s.channels : s.channels + 1, : s.channels] = gain[...]


def gated(s, rows, gain, weight, masks):
    h, size = s.hidden, rows[0].shape[0]
    rows = [normalise(row) * gain for row in rows]
    out = dot(jnp.concatenate(rows, 0).astype(BF16), weight)
    value = sigmoid(out[:, :h]) * out[:, h:]
    return [value[at * size : (at + 1) * size] * mask for at, mask in enumerate(masks)]


def masks_of(tokens, first, count, limit):
    below = lax.broadcasted_iota(jnp.int32, (count, 1), 0) + first < limit
    return [(below & (token < limit)).astype(F32) for token in tokens]


def project_right(s, rows_of, base, depth, token, shared, partner):
    first = lax.axis_index("col") * s.width
    for start in range(0, depth, s.half):
        steps = range(start, start + s.half)
        masks = masks_of([token + step for step in steps], first, s.slots, shared.limit)
        rows = [rows_of(base + step) for step in steps]
        for step, part in zip(steps, gated(s, rows, shared.gain, shared.right, masks)):
            partner[step] = part


def project_left(s, block, row, base, depth, token, shared, left):
    first = row * s.height
    for start in range(0, depth, s.half):
        steps = range(start, start + s.half)
        masks = masks_of([token + step for step in steps], first, s.height, shared.limit)
        rows = [block[base + step].astype(F32) for step in steps]
        for step, part in zip(steps, gated(s, rows, shared.gain, shared.left, masks)):
            left[step] = part


def add_both(s, distance, narrow, length, shared, own, other, *refs):
    before, (mine, theirs, left, right, picked, partner) = refs[:-6], refs[-6:]
    row, col = lax.axis_index("row"), lax.axis_index("col")
    shared = Shared(s, length, shared)
    depth = left.shape[0]
    token = column_from(s, distance) * s.width
    choose(row == owner_of(s, col), own, other, picked.at[:, : s.height])

    def rows_of(at):
        return picked[at, pl.ds(offset_in(s, col), s.slots), :]

    project_right(s, rows_of, 0, depth, token, shared, partner)
    project_left(s, own, row, 0, depth, token, shared, left)
    project_left(s, other, 1 - row, 0, depth, token, shared, right)
    old_mine, old_theirs = before if before else (None, None)
    accumulate(s, left, partner, old_mine, mine)
    if not narrow:
        accumulate(s, right, partner, old_theirs, theirs)
    else:
        accumulate(s, right, partner, old_theirs, picked)
        theirs[...] = picked[:, : s.height].astype(BF16)


def own_right(s, distance, length, shared, own, right, picked, partner):
    shared = Shared(s, length, shared)
    picked[:, : s.height] = own[...].astype(F32)
    offset = offset_in(s, lax.axis_index("col"))
    token = column_from(s, distance) * s.width

    def rows_of(at):
        return picked[at, pl.ds(offset, s.slots), :]

    project_right(s, rows_of, 0, s.width, token, shared, partner)
    right[...] = partner[...].astype(BF16)


def own_left(s, distance, length, shared, own, left):
    shared = Shared(s, length, shared)
    token = column_from(s, distance) * s.width
    project_left(s, own, lax.axis_index("row"), 0, s.width, token, shared, left)


def add_own(s, left, right, other, before, mine, partner):
    choose(lax.axis_index("row") == owner_of(s, lax.axis_index("col")), right, other, partner)
    accumulate(s, left, partner, before, mine)


def finish(s, left, right, other, mine, given, gating, last_gain, last_weight, *refs):
    update, partner, total = refs
    choose(lax.axis_index("row") == owner_of(s, lax.axis_index("col")), right, other, partner)
    accumulate(s, left, partner, mine, total)
    for start in range(0, s.width, s.half):
        settled = [
            normalise(total[start + step] + given[start + step].astype(F32)) * last_gain[...]
            for step in range(s.half)
        ]
        value = dot(jnp.concatenate(settled, 0).astype(BF16), last_weight[...])
        for step in range(s.half):
            part = gating[start + step] * value[step * s.height : (step + 1) * s.height]
            update[start + step] = part.astype(BF16)


def call(body, out_shape, scratch, flops, *operands, grant=24):
    def space(operand):
        return pl.BlockSpec(memory_space=pltpu.SMEM if operand.dtype == jnp.int32 else pltpu.VMEM)

    sent = sum(o.size * o.dtype.itemsize for o in operands)
    return pl.pallas_call(
        body,
        out_shape=out_shape,
        in_specs=[space(o) for o in operands],
        out_specs=jax.tree.map(lambda _: pl.BlockSpec(memory_space=pltpu.VMEM), out_shape),
        scratch_shapes=scratch,
        compiler_params=pltpu.CompilerParams(vmem_limit_bytes=grant * 1024 * 1024),
        cost_estimate=pl.CostEstimate(flops=flops, bytes_accessed=sent, transcendentals=0),
        name=body.func.__name__,
    )(*operands)


def local(
    mesh,
    pair_state,
    valid_length,
    input_gain,
    left_gate,
    left_value,
    right_gate,
    right_value,
    out_gate,
    output_gain,
    out_weight,
):
    height, width, channels = pair_state.shape
    hidden = left_gate.shape[1]
    s = Sizes(mesh, height, width, channels, hidden)
    shape = jax.ShapeDtypeStruct
    pair = jnp.transpose(pair_state, (1, 0, 2))
    gain = input_gain.reshape(1, channels)
    shared = call(
        functools.partial(join, s),
        shape((channels + 8, 4 * hidden), F32),
        [],
        0,
        gain,
        left_gate,
        left_value,
        right_gate,
        right_value,
        grant=56,
    )
    shared = (valid_length, shared)
    order = ring(s.cols)

    def shift(block, crossed=False, by=1):
        pairs = []
        for row in range(s.rows):
            target = s.rows - 1 - row if crossed else row
            for at in range(s.cols):
                to = (at + by * (1 - 2 * target)) % s.cols
                pairs.append((row * s.cols + order[at], target * s.cols + order[to]))
        return lax.ppermute(block, ("row", "col"), pairs)

    def swap(block):
        return lax.ppermute(block, "row", [(at, (at + 1) % s.rows) for at in range(s.rows)])

    sums = shape((width, height, hidden), F32)
    product = 16 * height * width * hidden
    tokens = pltpu.VMEM((width, height, hidden), F32)
    padded = pltpu.VMEM((width, height + TILE, channels), F32)
    partner = pltpu.VMEM((width, s.slots, hidden), F32)

    def add(distance, own, other, before, narrow=False):
        return call(
            functools.partial(add_both, s, distance, narrow),
            [sums, shape(sums.shape, BF16) if narrow else sums],
            [tokens, tokens, padded, partner],
            2 * width * product,
            *shared,
            own,
            other,
            *before,
        )

    def in_turn(other, own, done):
        own = lax.optimization_barrier((own, done))[0]
        return lax.optimization_barrier((other, own))[0], own

    far = s.cols // 2
    def right_of(distance, block):
        out = shape((width, s.slots, hidden), BF16)
        body = functools.partial(own_right, s, distance)
        return call(body, out, [padded, partner], 0, *shared, block)

    def left_of(distance, block):
        return call(functools.partial(own_left, s, distance), sums, [], 0, *shared, block)

    other = shift(pair, crossed=True)
    own = shift(pair)
    right = right_of(0, pair)
    other, own = in_turn(other, own, right)
    total = ()
    for distance in range(1, far - 1):
        ahead = [shift(other), shift(own)]
        if distance == 1:
            left, swapped = left_of(0, pair), swap(lax.optimization_barrier((right, own))[0])
        elif distance == 2:
            mine = call(
                functools.partial(add_own, s),
                sums,
                [partner],
                width * product,
                left,
                right,
                swapped,
                lax.optimization_barrier((total[0], own))[0],
            )
            total = mine, total[1]
        total = add(distance, own, other, total)
        other, own = in_turn(*ahead, (total, left))
        if distance == 1:
            other, swapped = lax.optimization_barrier((other, swapped))
    last = shift(own)
    gating = call(
        functools.partial(gate, s),
        [sums, shape((1, hidden), F32), shape(out_weight.shape, BF16)],
        [],
        2 * height * width * channels * channels,
        *shared,
        pair,
        out_gate,
        output_gain.reshape(1, hidden),
        out_weight,
    )
    mine, theirs = add(far - 1, own, other, total, narrow=True)
    given = swap(theirs)
    last, mine, gating = lax.optimization_barrier((last, mine, gating))
    right = right_of(far, last)
    swapped = swap(right)
    left = left_of(far, last)
    update = call(
        functools.partial(finish, s),
        shape((width, height, channels), BF16),
        [partner, pltpu.VMEM(sums.shape, F32)],
        width * product,
        left,
        right,
        swapped,
        mine,
        given,
        *gating,
    )
    return jnp.transpose(update, (1, 0, 2))


def solution(mesh):
    return jax.shard_map(
        functools.partial(local, mesh),
        mesh=mesh,
        in_specs=(P(("parts", "row"), "col", None), P("parts")) + (P(),) * 8,
        out_specs=P(("parts", "row"), "col", None),
        check_vma=False,
    )
```

```python
import functools

import jax
import jax.numpy as jnp
from jax import lax
from jax.experimental import pallas as pl
from jax.experimental.pallas import tpu as pltpu
from jax.sharding import PartitionSpec as P

F32 = jnp.float32
BF16 = jnp.bfloat16
EPS = 1e-05
TILE = 16
CHUNK = 56
GROUP = 7


class Sizes:
    def __init__(self, mesh, height, width, channels, hidden):
        self.rows = mesh.shape["row"]
        self.cols = mesh.shape["col"]
        self.height, self.width = height, width
        self.channels, self.hidden = channels, hidden
        self.half = width // 2
        self.slots = -(-width // TILE) * TILE


def column_at(place, cols):
    return jnp.where(place < cols // 2, 2 * place, 2 * (cols - place) - 1)


def place_of(column, cols):
    return jnp.where(column % 2 == 0, column // 2, cols - 1 - column // 2)


def ring(cols):
    return [2 * at if at < cols // 2 else 2 * (cols - at) - 1 for at in range(cols)]


def normalise(values):
    average = jnp.mean(values, -1, keepdims=True)
    centered = values - average
    variance = jnp.mean(centered * centered, -1, keepdims=True)
    return centered * lax.rsqrt(variance + EPS)


def sigmoid(values):
    return 0.5 * jnp.tanh(0.5 * values) + 0.5


def dot(left, right):
    return jnp.dot(left, right, preferred_element_type=F32)


def gate(s, length, shared, pair, out_gate, last_gain, last_weight, gating, kept_gain, kept_weight):
    gain = Shared(s, length, shared).gain
    kept_gain[...] = last_gain[...]
    kept_weight[...] = last_weight[...]
    for start in range(0, s.width, s.half):
        normed = [
            normalise(pair[start + step].astype(F32)) * gain for step in range(s.half)
        ]
        value = sigmoid(dot(jnp.concatenate(normed, 0).astype(BF16), out_gate[...]))
        for step in range(s.half):
            gating[start + step] = value[step * s.height : (step + 1) * s.height]


def accumulate(s, left, partner, before, total):
    depth = left.shape[0]
    size = CHUNK if s.height % CHUNK == 0 else s.height
    group = GROUP if s.width % GROUP == 0 else 1

    def chunk(index, carry):
        at = pl.ds(pl.multiple_of(index * size, 8), size)
        for first in range(0, s.width, group):
            members = range(first, first + group)
            if before is None:
                sums = tuple(jnp.zeros((size, s.hidden), F32) for _ in members)
            else:
                sums = tuple(before[j, at] for j in members)

            def step(k, sums):
                value = left[k, at]
                return tuple(
                    so_far + value * partner[k, j : j + 1] for so_far, j in zip(sums, members)
                )

            sums = lax.fori_loop(0, depth, step, sums, unroll=s.half)
            for so_far, j in zip(sums, members):
                total[j, at] = so_far
        return carry

    lax.fori_loop(0, s.height // size, chunk, 0)


def owner_of(s, col):
    return col // (s.height // s.width)


def choose(first, one, other, target):
    @pl.when(first)
    def _():
        target[...] = one[...].astype(F32)

    @pl.when(jnp.logical_not(first))
    def _():
        target[...] = other[...].astype(F32)


def offset_in(s, col):
    return (col % (s.height // s.width)) * s.width


def column_from(s, distance):
    row, col = lax.axis_index("row"), lax.axis_index("col")
    step = distance * (1 - 2 * row)
    return column_at((place_of(col, s.cols) + step + s.cols) % s.cols, s.cols)


class Shared:
    def __init__(self, s, length, ref):
        h = s.hidden
        self.left = ref[: s.channels, : 2 * h].astype(BF16)
        self.right = ref[: s.channels, 2 * h :].astype(BF16)
        self.gain = ref[s.channels : s.channels + 1, : s.channels]
        self.limit = length[0]


def join(s, gain, left_gate, left_value, right_gate, right_value, shared):
    h = s.hidden
    for at, part in enumerate((left_gate, left_value, right_gate, right_value)):
        shared[: s.channels, at * h : (at + 1) * h] = part[...].astype(F32)
    shared[s.channels : s.channels + 1, : s.channels] = gain[...]


def gated(s, rows, gain, weight, masks):
    h, size = s.hidden, rows[0].shape[0]
    rows = [normalise(row) * gain for row in rows]
    out = dot(jnp.concatenate(rows, 0).astype(BF16), weight)
    value = sigmoid(out[:, :h]) * out[:, h:]
    return [value[at * size : (at + 1) * size] * mask for at, mask in enumerate(masks)]


def masks_of(tokens, first, count, limit):
    below = lax.broadcasted_iota(jnp.int32, (count, 1), 0) + first < limit
    return [(below & (token < limit)).astype(F32) for token in tokens]


def project_right(s, rows_of, base, depth, token, shared, partner):
    first = lax.axis_index("col") * s.width
    for start in range(0, depth, s.half):
        steps = range(start, start + s.half)
        masks = masks_of([token + step for step in steps], first, s.slots, shared.limit)
        rows = [rows_of(base + step) for step in steps]
        for step, part in zip(steps, gated(s, rows, shared.gain, shared.right, masks)):
            partner[step] = part


def project_left(s, block, row, base, depth, token, shared, left):
    first = row * s.height
    for start in range(0, depth, s.half):
        steps = range(start, start + s.half)
        masks = masks_of([token + step for step in steps], first, s.height, shared.limit)
        rows = [block[base + step].astype(F32) for step in steps]
        for step, part in zip(steps, gated(s, rows, shared.gain, shared.left, masks)):
            left[step] = part


def add_both(s, distance, narrow, length, shared, own, other, *refs):
    before, (mine, theirs, left, right, picked, partner) = refs[:-6], refs[-6:]
    row, col = lax.axis_index("row"), lax.axis_index("col")
    shared = Shared(s, length, shared)
    depth = left.shape[0]
    base = row * s.half if distance == 0 else 0
    token = column_from(s, distance) * s.width + base
    choose(row == owner_of(s, col), own, other, picked.at[:, : s.height])

    def rows_of(at):
        return picked[at, pl.ds(offset_in(s, col), s.slots), :]

    project_right(s, rows_of, base, depth, token, shared, partner)
    project_left(s, own, row, base, depth, token, shared, left)
    project_left(s, other, 1 - row, base, depth, token, shared, right)
    old_mine, old_theirs = before if before else (None, None)
    accumulate(s, left, partner, old_mine, mine)
    if not narrow:
        accumulate(s, right, partner, old_theirs, theirs)
    else:
        accumulate(s, right, partner, old_theirs, picked)
        theirs[...] = picked[:, : s.height].astype(BF16)


def last_right(s, length, shared, own, right, picked, partner):
    shared = Shared(s, length, shared)
    picked[:, : s.height] = own[...].astype(F32)
    offset = offset_in(s, lax.axis_index("col"))
    token = column_from(s, s.cols // 2) * s.width

    def rows_of(at):
        return picked[at, pl.ds(offset, s.slots), :]

    project_right(s, rows_of, 0, s.width, token, shared, partner)
    right[...] = partner[...].astype(BF16)


def last_left(s, length, shared, own, left):
    shared = Shared(s, length, shared)
    token = column_from(s, s.cols // 2) * s.width
    project_left(s, own, lax.axis_index("row"), 0, s.width, token, shared, left)


def finish(s, left, right, other, mine, given, gating, last_gain, last_weight, *refs):
    update, partner, total = refs
    choose(lax.axis_index("row") == owner_of(s, lax.axis_index("col")), right, other, partner)
    accumulate(s, left, partner, mine, total)
    for start in range(0, s.width, s.half):
        settled = [
            normalise(total[start + step] + given[start + step].astype(F32)) * last_gain[...]
            for step in range(s.half)
        ]
        value = dot(jnp.concatenate(settled, 0).astype(BF16), last_weight[...])
        for step in range(s.half):
            part = gating[start + step] * value[step * s.height : (step + 1) * s.height]
            update[start + step] = part.astype(BF16)


def call(body, out_shape, scratch, flops, *operands, grant=24):
    def space(operand):
        return pl.BlockSpec(memory_space=pltpu.SMEM if operand.dtype == jnp.int32 else pltpu.VMEM)

    sent = sum(o.size * o.dtype.itemsize for o in operands)
    return pl.pallas_call(
        body,
        out_shape=out_shape,
        in_specs=[space(o) for o in operands],
        out_specs=jax.tree.map(lambda _: pl.BlockSpec(memory_space=pltpu.VMEM), out_shape),
        scratch_shapes=scratch,
        compiler_params=pltpu.CompilerParams(vmem_limit_bytes=grant * 1024 * 1024),
        cost_estimate=pl.CostEstimate(flops=flops, bytes_accessed=sent, transcendentals=0),
        name=body.func.__name__,
    )(*operands)


def local(
    mesh,
    pair_state,
    valid_length,
    input_gain,
    left_gate,
    left_value,
    right_gate,
    right_value,
    out_gate,
    output_gain,
    out_weight,
):
    height, width, channels = pair_state.shape
    hidden = left_gate.shape[1]
    s = Sizes(mesh, height, width, channels, hidden)
    shape = jax.ShapeDtypeStruct
    pair = jnp.transpose(pair_state, (1, 0, 2))
    gain = input_gain.reshape(1, channels)
    shared = call(
        functools.partial(join, s),
        shape((channels + 8, 4 * hidden), F32),
        [],
        0,
        gain,
        left_gate,
        left_value,
        right_gate,
        right_value,
        grant=56,
    )
    shared = (valid_length, shared)
    order = ring(s.cols)

    def shift(block, crossed=False, by=1):
        pairs = []
        for row in range(s.rows):
            target = s.rows - 1 - row if crossed else row
            for at in range(s.cols):
                to = (at + by * (2 * target - 1)) % s.cols
                pairs.append((row * s.cols + order[at], target * s.cols + order[to]))
        return lax.ppermute(block, ("row", "col"), pairs)

    def swap(block):
        return lax.ppermute(block, "row", [(at, (at + 1) % s.rows) for at in range(s.rows)])

    sums = shape((width, height, hidden), F32)
    product = 16 * height * width * hidden
    tokens = pltpu.VMEM((width, height, hidden), F32)
    halved = pltpu.VMEM((s.half, height, hidden), F32)
    padded = pltpu.VMEM((width, height + TILE, channels), F32)
    partner = pltpu.VMEM((width, s.slots, hidden), F32)
    few = pltpu.VMEM((s.half, s.slots, hidden), F32)

    def add(distance, own, other, before, narrow=False):
        left, right = (halved, few) if distance == 0 else (tokens, partner)
        return call(
            functools.partial(add_both, s, distance, narrow),
            [sums, shape(sums.shape, BF16) if narrow else sums],
            [left, left, padded, right],
            2 * left.shape[0] * product,
            *shared,
            own,
            other,
            *before,
        )

    def in_turn(other, own, done):
        own = lax.optimization_barrier((own, done))[0]
        return lax.optimization_barrier((other, own))[0], own

    far = s.cols // 2
    other = shift(pair, crossed=True)
    own = shift(pair)
    total = add(0, pair, swap(pair), ())
    other, own = in_turn(other, own, total)
    for distance in range(1, far - 1):
        ahead = [shift(other), shift(own)]
        total = add(distance, own, other, total)
        if distance == 1:
            gating = call(
                functools.partial(gate, s),
                [sums, shape((1, hidden), F32), shape(out_weight.shape, BF16)],
                [],
                2 * height * width * channels * channels,
                *shared,
                pair,
                out_gate,
                output_gain.reshape(1, hidden),
                out_weight,
            )
        other, own = in_turn(*ahead, (total, gating))
    last = shift(own)
    mine, theirs = add(far - 1, own, other, total, narrow=True)
    given = swap(theirs)
    last, mine, gating = lax.optimization_barrier((last, mine, gating))
    right = call(
        functools.partial(last_right, s),
        shape((width, s.slots, hidden), BF16),
        [padded, partner],
        0,
        *shared,
        last,
    )
    swapped = swap(right)
    left = call(functools.partial(last_left, s), sums, [], 0, *shared, last)
    update = call(
        functools.partial(finish, s),
        shape((width, height, channels), BF16),
        [partner, pltpu.VMEM(sums.shape, F32)],
        width * product,
        left,
        right,
        swapped,
        mine,
        given,
        *gating,
    )
    return jnp.transpose(update, (1, 0, 2))


def solution(mesh):
    return jax.shard_map(
        functools.partial(local, mesh),
        mesh=mesh,
        in_specs=(P(("parts", "row"), "col", None), P("parts")) + (P(),) * 8,
        out_specs=P(("parts", "row"), "col", None),
        check_vma=False,
    )
```

```python
import functools

import jax
import jax.numpy as jnp
from jax import lax
from jax.experimental import pallas as pl
from jax.experimental.pallas import tpu as pltpu
from jax.sharding import PartitionSpec as P

F32 = jnp.float32
BF16 = jnp.bfloat16
EPS = 1e-05
TILE = 16
CHUNK = 56
GROUP = 7


class Sizes:
    def __init__(self, mesh, height, width, channels, hidden):
        self.rows = mesh.shape["row"]
        self.cols = mesh.shape["col"]
        self.height, self.width = height, width
        self.channels, self.hidden = channels, hidden
        self.half = width // 2
        self.slots = -(-width // TILE) * TILE


def column_at(place, cols):
    return jnp.where(place < cols // 2, 2 * place, 2 * (cols - place) - 1)


def place_of(column, cols):
    return jnp.where(column % 2 == 0, column // 2, cols - 1 - column // 2)


def ring(cols):
    return [2 * at if at < cols // 2 else 2 * (cols - at) - 1 for at in range(cols)]


def normalise(values):
    average = jnp.mean(values, -1, keepdims=True)
    centered = values - average
    variance = jnp.mean(centered * centered, -1, keepdims=True)
    return centered * lax.rsqrt(variance + EPS)


def sigmoid(values):
    return 0.5 * jnp.tanh(0.5 * values) + 0.5


def dot(left, right):
    return jnp.dot(left, right, preferred_element_type=F32)


def gate(s, length, shared, pair, out_gate, last_gain, last_weight, gating, kept_gain, kept_weight):
    gain = Shared(s, length, shared).gain
    kept_gain[...] = last_gain[...]
    kept_weight[...] = last_weight[...]
    for start in range(0, s.width, s.half):
        normed = [
            normalise(pair[start + step].astype(F32)) * gain for step in range(s.half)
        ]
        value = sigmoid(dot(jnp.concatenate(normed, 0).astype(BF16), out_gate[...]))
        for step in range(s.half):
            gating[start + step] = value[step * s.height : (step + 1) * s.height]


def accumulate(s, left, partner, before, total):
    depth = left.shape[0]
    size = CHUNK if s.height % CHUNK == 0 else s.height
    group = GROUP if s.width % GROUP == 0 else 1

    def chunk(index, carry):
        at = pl.ds(pl.multiple_of(index * size, 8), size)
        for first in range(0, s.width, group):
            members = range(first, first + group)
            if before is None:
                sums = tuple(jnp.zeros((size, s.hidden), F32) for _ in members)
            else:
                sums = tuple(before[j, at] for j in members)

            def step(k, sums):
                value = left[k, at]
                return tuple(
                    so_far + value * partner[k, j : j + 1] for so_far, j in zip(sums, members)
                )

            sums = lax.fori_loop(0, depth, step, sums, unroll=s.half)
            for so_far, j in zip(sums, members):
                total[j, at] = so_far
        return carry

    lax.fori_loop(0, s.height // size, chunk, 0)


def owner_of(s, col):
    return col // (s.height // s.width)


def choose(first, one, other, target):
    @pl.when(first)
    def _():
        target[...] = one[...].astype(F32)

    @pl.when(jnp.logical_not(first))
    def _():
        target[...] = other[...].astype(F32)


def offset_in(s, col):
    return (col % (s.height // s.width)) * s.width


def column_from(s, distance):
    row, col = lax.axis_index("row"), lax.axis_index("col")
    step = distance * (2 * row - 1)
    return column_at((place_of(col, s.cols) + step + s.cols) % s.cols, s.cols)


class Shared:
    def __init__(self, s, length, ref):
        h = s.hidden
        self.left = ref[: s.channels, : 2 * h].astype(BF16)
        self.right = ref[: s.channels, 2 * h :].astype(BF16)
        self.gain = ref[s.channels : s.channels + 1, : s.channels]
        self.limit = length[0]


def join(s, gain, left_gate, left_value, right_gate, right_value, shared):
    h = s.hidden
    for at, part in enumerate((left_gate, left_value, right_gate, right_value)):
        shared[: s.channels, at * h : (at + 1) * h] = part[...].astype(F32)
    shared[s.channels : s.channels + 1, : s.channels] = gain[...]


def gated(s, rows, gain, weight, masks):
    h, size = s.hidden, rows[0].shape[0]
    rows = [normalise(row) * gain for row in rows]
    out = dot(jnp.concatenate(rows, 0).astype(BF16), weight)
    value = sigmoid(out[:, :h]) * out[:, h:]
    return [value[at * size : (at + 1) * size] * mask for at, mask in enumerate(masks)]


def masks_of(tokens, first, count, limit):
    below = lax.broadcasted_iota(jnp.int32, (count, 1), 0) + first < limit
    return [(below & (token < limit)).astype(F32) for token in tokens]


def project_right(s, rows_of, base, depth, token, shared, partner):
    first = lax.axis_index("col") * s.width
    for start in range(0, depth, s.half):
        steps = range(start, start + s.half)
        masks = masks_of([token + step for step in steps], first, s.slots, shared.limit)
        rows = [rows_of(base + step) for step in steps]
        for step, part in zip(steps, gated(s, rows, shared.gain, shared.right, masks)):
            partner[step] = part


def project_left(s, block, row, base, depth, token, shared, left):
    first = row * s.height
    for start in range(0, depth, s.half):
        steps = range(start, start + s.half)
        masks = masks_of([token + step for step in steps], first, s.height, shared.limit)
        rows = [block[base + step].astype(F32) for step in steps]
        for step, part in zip(steps, gated(s, rows, shared.gain, shared.left, masks)):
            left[step] = part


def add_both(s, distance, narrow, length, shared, own, other, *refs):
    before, (mine, theirs, left, right, picked, partner) = refs[:-6], refs[-6:]
    row, col = lax.axis_index("row"), lax.axis_index("col")
    shared = Shared(s, length, shared)
    depth = left.shape[0]
    base = row * s.half if distance == 0 else 0
    token = column_from(s, distance) * s.width + base
    choose(row == owner_of(s, col), own, other, picked.at[:, : s.height])

    def rows_of(at):
        return picked[at, pl.ds(offset_in(s, col), s.slots), :]

    project_right(s, rows_of, base, depth, token, shared, partner)
    project_left(s, own, row, base, depth, token, shared, left)
    project_left(s, other, 1 - row, base, depth, token, shared, right)
    old_mine, old_theirs = before if before else (None, None)
    accumulate(s, left, partner, old_mine, mine)
    if not narrow:
        accumulate(s, right, partner, old_theirs, theirs)
    else:
        accumulate(s, right, partner, old_theirs, picked)
        theirs[...] = picked[:, : s.height].astype(BF16)


def last_right(s, length, shared, own, right, picked, partner):
    shared = Shared(s, length, shared)
    offset = offset_in(s, lax.axis_index("col"))
    for at in range(0, s.height, s.width):

        @pl.when(offset == at)
        def _(at=at):
            picked[:, : s.width] = own[:, at : at + s.width].astype(F32)

    token = column_from(s, s.cols // 2) * s.width

    def rows_of(at):
        return picked[at, : s.slots, :]

    project_right(s, rows_of, 0, s.width, token, shared, partner)
    right[...] = partner[...].astype(BF16)


def last_left(s, length, shared, own, mine, given, left, total):
    total[...] = mine[...] + given[...].astype(F32)
    shared = Shared(s, length, shared)
    token = column_from(s, s.cols // 2) * s.width
    project_left(s, own, lax.axis_index("row"), 0, s.width, token, shared, left)


def finish(s, left, right, other, mine, gating, last_gain, last_weight, *refs):
    update, partner, total, held, sent = refs
    copies = []
    choose(lax.axis_index("row") == owner_of(s, lax.axis_index("col")), right, other, partner)
    accumulate(s, left, partner, mine, total)
    for start in range(0, s.width, s.half):
        settled = [
            normalise(total[start + step]) * last_gain[...]
            for step in range(s.half)
        ]
        value = dot(jnp.concatenate(settled, 0).astype(BF16), last_weight[...])
        for step in range(s.half):
            part = gating[start + step] * value[step * s.height : (step + 1) * s.height]
            held[start + step] = part.astype(BF16)
        part = pl.ds(start, s.half)
        copies.append(pltpu.make_async_copy(held.at[part], update.at[part], sent.at[len(copies)]))
        copies[-1].start()
    for copy in copies:
        copy.wait()


def call(body, out_shape, scratch, flops, *operands, grant=24, out_memory=pltpu.VMEM):
    def space(operand):
        return pl.BlockSpec(memory_space=pltpu.SMEM if operand.dtype == jnp.int32 else pltpu.VMEM)

    sent = sum(o.size * o.dtype.itemsize for o in operands)
    return pl.pallas_call(
        body,
        out_shape=out_shape,
        in_specs=[space(o) for o in operands],
        out_specs=jax.tree.map(lambda _: pl.BlockSpec(memory_space=out_memory), out_shape),
        scratch_shapes=scratch,
        compiler_params=pltpu.CompilerParams(vmem_limit_bytes=grant * 1024 * 1024),
        cost_estimate=pl.CostEstimate(flops=flops, bytes_accessed=sent, transcendentals=0),
        name=body.func.__name__,
    )(*operands)


def local(
    mesh,
    pair_state,
    valid_length,
    input_gain,
    left_gate,
    left_value,
    right_gate,
    right_value,
    out_gate,
    output_gain,
    out_weight,
):
    height, width, channels = pair_state.shape
    hidden = left_gate.shape[1]
    s = Sizes(mesh, height, width, channels, hidden)
    shape = jax.ShapeDtypeStruct
    pair = jnp.transpose(pair_state, (1, 0, 2))
    gain = input_gain.reshape(1, channels)
    shared = call(
        functools.partial(join, s),
        shape((channels + 8, 4 * hidden), F32),
        [],
        0,
        gain,
        left_gate,
        left_value,
        right_gate,
        right_value,
        grant=56,
    )
    shared = (valid_length, shared)
    order = ring(s.cols)

    def shift(block, crossed=False, by=1):
        pairs = []
        for row in range(s.rows):
            target = s.rows - 1 - row if crossed else row
            for at in range(s.cols):
                to = (at + by * (1 - 2 * target)) % s.cols
                pairs.append((row * s.cols + order[at], target * s.cols + order[to]))
        return lax.ppermute(block, ("row", "col"), pairs)

    def swap(block):
        return lax.ppermute(block, "row", [(at, (at + 1) % s.rows) for at in range(s.rows)])

    sums = shape((width, height, hidden), F32)
    product = 16 * height * width * hidden
    tokens = pltpu.VMEM((width, height, hidden), F32)
    halved = pltpu.VMEM((s.half, height, hidden), F32)
    padded = pltpu.VMEM((width, height + TILE, channels), F32)
    partner = pltpu.VMEM((width, s.slots, hidden), F32)
    few = pltpu.VMEM((s.half, s.slots, hidden), F32)

    def add(distance, own, other, before, narrow=False):
        left, right = (halved, few) if distance == 0 else (tokens, partner)
        return call(
            functools.partial(add_both, s, distance, narrow),
            [sums, shape(sums.shape, BF16) if narrow else sums],
            [left, left, padded, right],
            2 * left.shape[0] * product,
            *shared,
            own,
            other,
            *before,
        )

    def in_turn(other, own, done):
        own = lax.optimization_barrier((own, done))[0]
        return lax.optimization_barrier((other, own))[0], own

    far = s.cols // 2
    other = shift(pair, crossed=True)
    own = shift(pair)
    total = add(0, pair, swap(pair), ())
    other, own = in_turn(other, own, total)
    for distance in range(1, far - 1):
        ahead = [shift(other), shift(own)]
        total = add(distance, own, other, total)
        if distance == 1:
            gating = call(
                functools.partial(gate, s),
                [sums, shape((1, hidden), F32), shape(out_weight.shape, BF16)],
                [],
                2 * height * width * channels * channels,
                *shared,
                pair,
                out_gate,
                output_gain.reshape(1, hidden),
                out_weight,
            )
        other, own = in_turn(*ahead, (total, gating))
    last = shift(own)
    mine, theirs = add(far - 1, own, other, total, narrow=True)
    given = swap(theirs)
    last, mine, gating = lax.optimization_barrier((last, mine, gating))
    right = call(
        functools.partial(last_right, s),
        shape((width, s.slots, hidden), BF16),
        [padded, partner],
        0,
        *shared,
        last,
    )
    swapped = swap(right)
    left, mine = call(
        functools.partial(last_left, s), [sums, sums], [], 0, *shared, last, mine, given
    )
    update = call(
        functools.partial(finish, s),
        shape((width, height, channels), BF16),
        [
            partner,
            pltpu.VMEM(sums.shape, F32),
            pltpu.VMEM(sums.shape, BF16),
            pltpu.SemaphoreType.DMA((2,)),
        ],
        width * product,
        left,
        right,
        swapped,
        mine,
        *gating,
        out_memory=pl.ANY,
    )
    return jnp.transpose(update, (1, 0, 2))


def solution(mesh):
    return jax.shard_map(
        functools.partial(local, mesh),
        mesh=mesh,
        in_specs=(P(("parts", "row"), "col", None), P("parts")) + (P(),) * 8,
        out_specs=P(("parts", "row"), "col", None),
        check_vma=False,
    )
```

```python
import functools

import jax
import jax.numpy as jnp
from jax import lax
from jax.experimental import pallas as pl
from jax.experimental.pallas import tpu as pltpu
from jax.sharding import PartitionSpec as P

F32 = jnp.float32
BF16 = jnp.bfloat16
EPS = 1e-05
TILE = 16
CHUNK = 56
GROUP = 7


class Sizes:
    def __init__(self, mesh, height, width, channels, hidden):
        self.rows = mesh.shape["row"]
        self.cols = mesh.shape["col"]
        self.height, self.width = height, width
        self.channels, self.hidden = channels, hidden
        self.half = width // 2
        self.slots = -(-width // TILE) * TILE


def column_at(place, cols):
    return jnp.where(place < cols // 2, 2 * place, 2 * (cols - place) - 1)


def place_of(column, cols):
    return jnp.where(column % 2 == 0, column // 2, cols - 1 - column // 2)


def ring(cols):
    return [2 * at if at < cols // 2 else 2 * (cols - at) - 1 for at in range(cols)]


def normalise(values):
    average = jnp.mean(values, -1, keepdims=True)
    centered = values - average
    variance = jnp.mean(centered * centered, -1, keepdims=True)
    return centered * lax.rsqrt(variance + EPS)


def sigmoid(values):
    return 0.5 * jnp.tanh(0.5 * values) + 0.5


def dot(left, right):
    return jnp.dot(left, right, preferred_element_type=F32)


def gate(s, gain, pair, out_gate, last_gain, last_weight, gating, kept_gain, kept_weight):
    kept_gain[...] = last_gain[...]
    kept_weight[...] = last_weight[...]
    for start in range(0, s.width, s.half):
        normed = [
            normalise(pair[start + step].astype(F32)) * gain[...] for step in range(s.half)
        ]
        value = sigmoid(dot(jnp.concatenate(normed, 0).astype(BF16), out_gate[...]))
        for step in range(s.half):
            gating[start + step] = value[step * s.height : (step + 1) * s.height]


def accumulate(s, left, partner, before, total):
    depth = left.shape[0]
    size = CHUNK if s.height % CHUNK == 0 else s.height
    group = GROUP if s.width % GROUP == 0 else 1

    def chunk(index, carry):
        at = pl.ds(pl.multiple_of(index * size, 8), size)
        for first in range(0, s.width, group):
            members = range(first, first + group)
            if before is None:
                sums = tuple(jnp.zeros((size, s.hidden), F32) for _ in members)
            else:
                sums = tuple(before[j, at] for j in members)

            def step(k, sums):
                value = left[k, at]
                return tuple(
                    so_far + value * partner[k, j : j + 1] for so_far, j in zip(sums, members)
                )

            sums = lax.fori_loop(0, depth, step, sums, unroll=s.half)
            for so_far, j in zip(sums, members):
                total[j, at] = so_far
        return carry

    lax.fori_loop(0, s.height // size, chunk, 0)


def owner_of(s, col):
    return col // (s.height // s.width)


def choose(first, one, other, target):
    @pl.when(first)
    def _():
        target[...] = one[...].astype(F32)

    @pl.when(jnp.logical_not(first))
    def _():
        target[...] = other[...].astype(F32)


def offset_in(s, col):
    return (col % (s.height // s.width)) * s.width


def column_from(s, distance):
    row, col = lax.axis_index("row"), lax.axis_index("col")
    step = distance * (2 * row - 1)
    return column_at((place_of(col, s.cols) + step + s.cols) % s.cols, s.cols)


class Shared:
    def __init__(self, s, length, ref):
        h = s.hidden
        self.left = ref[: s.channels, : 2 * h].astype(BF16)
        self.right = ref[: s.channels, 2 * h :].astype(BF16)
        self.gain = ref[s.channels : s.channels + 1, : s.channels]
        self.limit = length[0]


def join(s, gain, left_gate, left_value, right_gate, right_value, shared):
    h = s.hidden
    for at, part in enumerate((left_gate, left_value, right_gate, right_value)):
        shared[: s.channels, at * h : (at + 1) * h] = part[...].astype(F32)
    shared[s.channels : s.channels + 1, : s.channels] = gain[...]


def gain_of(s, length, shared, gain):
    gain[...] = Shared(s, length, shared).gain


def gated(s, rows, gain, weight, masks):
    h, size = s.hidden, rows[0].shape[0]
    rows = [normalise(row) * gain for row in rows]
    out = dot(jnp.concatenate(rows, 0).astype(BF16), weight)
    value = sigmoid(out[:, :h]) * out[:, h:]
    return [value[at * size : (at + 1) * size] * mask for at, mask in enumerate(masks)]


def masks_of(tokens, first, count, limit):
    below = lax.broadcasted_iota(jnp.int32, (count, 1), 0) + first < limit
    return [(below & (token < limit)).astype(F32) for token in tokens]


def project_right(s, rows_of, base, depth, token, shared, partner):
    first = lax.axis_index("col") * s.width
    for start in range(0, depth, s.half):
        steps = range(start, start + s.half)
        masks = masks_of([token + step for step in steps], first, s.slots, shared.limit)
        rows = [rows_of(base + step) for step in steps]
        for step, part in zip(steps, gated(s, rows, shared.gain, shared.right, masks)):
            partner[step] = part


def project_left(s, block, row, base, depth, token, shared, left):
    first = row * s.height
    for start in range(0, depth, s.half):
        steps = range(start, start + s.half)
        masks = masks_of([token + step for step in steps], first, s.height, shared.limit)
        rows = [block[base + step].astype(F32) for step in steps]
        for step, part in zip(steps, gated(s, rows, shared.gain, shared.left, masks)):
            left[step] = part


def add_both(s, distance, narrow, length, shared, own, other, *refs):
    before, (mine, theirs, left, right, picked, partner) = refs[:-6], refs[-6:]
    row, col = lax.axis_index("row"), lax.axis_index("col")
    shared = Shared(s, length, shared)
    depth = left.shape[0]
    base = row * s.half if distance == 0 else 0
    token = column_from(s, distance) * s.width + base
    choose(row == owner_of(s, col), own, other, picked.at[:, : s.height])

    def rows_of(at):
        return picked[at, pl.ds(offset_in(s, col), s.slots), :]

    project_right(s, rows_of, base, depth, token, shared, partner)
    project_left(s, own, row, base, depth, token, shared, left)
    project_left(s, other, 1 - row, base, depth, token, shared, right)
    old_mine, old_theirs = before if before else (None, None)
    accumulate(s, left, partner, old_mine, mine)
    if not narrow:
        accumulate(s, right, partner, old_theirs, theirs)
    else:
        accumulate(s, right, partner, old_theirs, picked)
        theirs[...] = picked[:, : s.height].astype(BF16)


def last_right(s, length, shared, own, right, picked, partner):
    shared = Shared(s, length, shared)
    picked[:, : s.height] = own[...].astype(F32)
    offset = offset_in(s, lax.axis_index("col"))
    token = column_from(s, s.cols // 2) * s.width

    def rows_of(at):
        return picked[at, pl.ds(offset, s.slots), :]

    project_right(s, rows_of, 0, s.width, token, shared, partner)
    right[...] = partner[...].astype(BF16)


def last_left(s, length, shared, own, left):
    shared = Shared(s, length, shared)
    token = column_from(s, s.cols // 2) * s.width
    project_left(s, own, lax.axis_index("row"), 0, s.width, token, shared, left)


def finish(s, left, right, other, mine, given, gating, last_gain, last_weight, *refs):
    update, partner, total = refs
    choose(lax.axis_index("row") == owner_of(s, lax.axis_index("col")), right, other, partner)
    accumulate(s, left, partner, mine, total)
    for start in range(0, s.width, s.half):
        settled = [
            normalise(total[start + step] + given[start + step].astype(F32)) * last_gain[...]
            for step in range(s.half)
        ]
        value = dot(jnp.concatenate(settled, 0).astype(BF16), last_weight[...])
        for step in range(s.half):
            part = gating[start + step] * value[step * s.height : (step + 1) * s.height]
            update[start + step] = part.astype(BF16)


def call(body, out_shape, scratch, flops, *operands, grant=24):
    def space(operand):
        return pl.BlockSpec(memory_space=pltpu.SMEM if operand.dtype == jnp.int32 else pltpu.VMEM)

    sent = sum(o.size * o.dtype.itemsize for o in operands)
    return pl.pallas_call(
        body,
        out_shape=out_shape,
        in_specs=[space(o) for o in operands],
        out_specs=jax.tree.map(lambda _: pl.BlockSpec(memory_space=pltpu.VMEM), out_shape),
        scratch_shapes=scratch,
        compiler_params=pltpu.CompilerParams(vmem_limit_bytes=grant * 1024 * 1024),
        cost_estimate=pl.CostEstimate(flops=flops, bytes_accessed=sent, transcendentals=0),
        name=body.func.__name__,
    )(*operands)


def local(
    mesh,
    pair_state,
    valid_length,
    input_gain,
    left_gate,
    left_value,
    right_gate,
    right_value,
    out_gate,
    output_gain,
    out_weight,
):
    height, width, channels = pair_state.shape
    hidden = left_gate.shape[1]
    s = Sizes(mesh, height, width, channels, hidden)
    shape = jax.ShapeDtypeStruct
    pair = jnp.transpose(pair_state, (1, 0, 2))
    gain = input_gain.reshape(1, channels)
    shared = call(
        functools.partial(join, s),
        shape((channels + 8, 4 * hidden), F32),
        [],
        0,
        gain,
        left_gate,
        left_value,
        right_gate,
        right_value,
        grant=56,
    )
    shared = (valid_length, shared)
    order = ring(s.cols)

    def shift(block, crossed=False, by=1):
        pairs = []
        for row in range(s.rows):
            target = s.rows - 1 - row if crossed else row
            for at in range(s.cols):
                to = (at + by * (1 - 2 * target)) % s.cols
                pairs.append((row * s.cols + order[at], target * s.cols + order[to]))
        return lax.ppermute(block, ("row", "col"), pairs)

    def swap(block):
        return lax.ppermute(block, "row", [(at, (at + 1) % s.rows) for at in range(s.rows)])

    sums = shape((width, height, hidden), F32)
    product = 16 * height * width * hidden
    tokens = pltpu.VMEM((width, height, hidden), F32)
    halved = pltpu.VMEM((s.half, height, hidden), F32)
    padded = pltpu.VMEM((width, height + TILE, channels), F32)
    partner = pltpu.VMEM((width, s.slots, hidden), F32)
    few = pltpu.VMEM((s.half, s.slots, hidden), F32)

    def add(distance, own, other, before, narrow=False):
        left, right = (halved, few) if distance == 0 else (tokens, partner)
        return call(
            functools.partial(add_both, s, distance, narrow),
            [sums, shape(sums.shape, BF16) if narrow else sums],
            [left, left, padded, right],
            2 * left.shape[0] * product,
            *shared,
            own,
            other,
            *before,
        )

    def in_turn(other, own, done):
        own = lax.optimization_barrier((own, done))[0]
        return lax.optimization_barrier((other, own))[0], own

    far = s.cols // 2
    other = shift(pair, crossed=True)
    own = shift(pair)
    given = swap(lax.optimization_barrier((pair, shared[1]))[0])
    kept = call(functools.partial(gain_of, s), shape(gain.shape, F32), [], 0, *shared)
    own, kept = lax.optimization_barrier((own, kept))
    other = lax.optimization_barrier((other, own))[0]
    for distance in range(1, far - 1):
        ahead = [shift(other), shift(own)]
        after = lax.optimization_barrier((pair, own))[0]
        if distance == 1:
            total, gating = add(0, after, given, ()), ()
        elif distance == 2:
            gating = call(
                functools.partial(gate, s),
                [sums, shape((1, hidden), F32), shape(out_weight.shape, BF16)],
                [],
                2 * height * width * channels * channels,
                kept,
                after,
                out_gate,
                output_gain.reshape(1, hidden),
                out_weight,
            )
        total = add(distance, own, other, total)
        other, own = in_turn(*ahead, (total, gating))
    last = shift(own)
    mine, theirs = add(far - 1, own, other, total, narrow=True)
    given = swap(theirs)
    last, mine, gating = lax.optimization_barrier((last, mine, gating))
    right = call(
        functools.partial(last_right, s),
        shape((width, s.slots, hidden), BF16),
        [padded, partner],
        0,
        *shared,
        last,
    )
    swapped = swap(right)
    left = call(functools.partial(last_left, s), sums, [], 0, *shared, last)
    update = call(
        functools.partial(finish, s),
        shape((width, height, channels), BF16),
        [partner, pltpu.VMEM(sums.shape, F32)],
        width * product,
        left,
        right,
        swapped,
        mine,
        given,
        *gating,
    )
    return jnp.transpose(update, (1, 0, 2))


def solution(mesh):
    return jax.shard_map(
        functools.partial(local, mesh),
        mesh=mesh,
        in_specs=(P(("parts", "row"), "col", None), P("parts")) + (P(),) * 8,
        out_specs=P(("parts", "row"), "col", None),
        check_vma=False,
    )
```
